32 devices in a mesh: pages: 4 (over y, x), blk: 8 (over z, core).
Axes of the slice: x: 2, y: 2, z: 4, core: 2. Of those that a mesh axis runs over, the one named last changes fastest.
Arguments:
- new_hidden: bfloat16 [32, 6144], P('pages', 'blk'), may hold values from -6 to 6
- attn_gain: float32 [6144], replicated, may hold values from 0.1 to 1.9
- mlp_gain: float32 [6144], replicated, may hold values from 0.1 to 1.9
- qkv_weight: bfloat16 [6144, 18432], P(None, 'blk'), may hold values from -0.078125 to 0.078125
- dense_weight: bfloat16 [6144, 6144], P('blk'), may hold values from -0.078125 to 0.078125
- in_weight: bfloat16 [6144, 24576], P(None, ('pages', 'blk')), may hold values from -0.078125 to 0.078125
- out_weight: bfloat16 [24576, 6144], P(('pages', 'blk')), may hold values from -0.078125 to 0.078125
- page_store: bfloat16 [384, 16, 12288], P(('pages', 'blk')), may hold values from -420 to 420
- held_states: bfloat16 [32, 8, 6144], P(('pages', 'blk')), may hold values from -6 to 6
- fold_weights: float32 [8, 16], replicated, may hold values from 0.02 to 0.14
- page_table: int32 [32, 12], replicated, may hold values from 0 to 383, as said below
- lengths: int32 [32], P('pages'), may hold values from 81 to 192, as said below
- keep_slots: int32 [32, 5], P('pages'), may hold values from 0 to 11, as said below
- fold_index: int32 [32, 12], P('pages'), may hold values from 0 to 7
- recompute_list: int32 [32, 8], P('pages'), may hold values from 0 to 79, as said below
Outputs:
- update: bfloat16 [32, 6144], P('pages', 'blk')
- folded: bfloat16 [32, 12, 12288], P('pages', None, 'blk')
The draws below stay inside these ranges and needn't reach their ends.
Inputs may be any that keep to these rules, and one draw needn't show every extreme that they name: `page_table`: every page id appears exactly once; the device of index s along pages+blk holds pages s*12 to s*12 + 11, and exactly 3 of them belong to requests of each group of 8 consecutive requests. `lengths`: one request in every draw holds 192 tokens. `keep_slots`: A request's kept slots are distinct, ascending, and all below lengths // 16. `recompute_list`: A request's entries are distinct and ascending.
All inputs are finite; a program needn't handle non-finite values.
Results may differ from the reference program's by a relative error of at most 0.024.
Values may be sent and summed in bfloat16 or wider, within the bound.
No kernel may reach another device: no remote copies, remote signals or barrier semaphores. Data moves between devices by JAX's collectives and lax.ppermute only.
A program may use at most 192 MiB of HBM per device.

```python
import math
import jax
import jax.numpy as jnp
from jax import lax

D = 6144
H = 64
HD = 96
FF = 24576
ROT = 24
PAGE = 16
PPR = 12
KP = 5
NREC = 8
NF = 8
RG = 8
R = 32
PD = 12
PGD = 3
NPAGES = 384


def draw_page_store(key, part):
    first_key = jax.random.fold_in(jax.random.fold_in(key, 5), 0)
    shape = (NPAGES, PAGE, 2 * D)
    values = jnp.clip(jax.random.normal(first_key, shape, jnp.float32), -6.0, 6.0)
    return values.astype(jnp.bfloat16)


def draw_page_table(key, part):
    first_key, second_key = jax.random.split(jax.random.fold_in(key, 11))
    owners = NPAGES // PD
    groups = R // RG
    local_slots = jnp.tile(jnp.arange(PD, dtype=jnp.int32)[None, :], (owners, 1))
    local_slots = jax.random.permutation(first_key, local_slots, axis=1, independent=True)
    page_ids = jnp.arange(owners, dtype=jnp.int32)[:, None] * PD + local_slots
    page_ids = page_ids.reshape(owners, groups, PGD).transpose(1, 0, 2).reshape(groups, owners * PGD)
    page_ids = jax.random.permutation(second_key, page_ids, axis=1, independent=True)
    return page_ids.reshape(R, PPR).astype(jnp.int32)


def length_helper(key):
    first_key, second_key, third_key = jax.random.split(jax.random.fold_in(key, 31), 3)
    counts = jax.random.randint(first_key, (R,), KP * PAGE + 1, PPR * PAGE + 1)
    longest = jax.random.randint(second_key, (), 0, R)
    shortest = (longest + 1 + jax.random.randint(third_key, (), 0, R - 1)) % R
    row_ids = jnp.arange(R)
    counts = jnp.where(row_ids == longest, PPR * PAGE, counts)
    counts = jnp.where(row_ids == shortest, KP * PAGE + 1, counts)
    return counts.astype(jnp.int32)


def draw_lengths(key, part):
    return length_helper(key)


def draw_keep_slots(key, part):
    counts = length_helper(key)
    full_pages = counts // PAGE
    slot_ids = jnp.arange(PPR, dtype=jnp.int32)
    scores = jax.random.randint(jax.random.fold_in(key, 41), (R, PPR), 0, 1 << 20) * PPR + slot_ids[None, :]
    scores = jnp.where(slot_ids[None, :] < full_pages[:, None], scores, (1 << 20) * PPR + slot_ids[None, :])
    chosen = jnp.argsort(scores, axis=1)[:, :KP]
    return jnp.sort(chosen, axis=1).astype(jnp.int32)


def draw_recompute_list(key, part):
    kept_count = KP * PAGE
    scores = jax.random.randint(jax.random.fold_in(key, 53), (R, kept_count), 0, 1 << 20) * kept_count + jnp.arange(kept_count, dtype=jnp.int32)[None, :]
    chosen = jnp.argsort(scores, axis=1)[:, :NREC]
    return jnp.sort(chosen, axis=1).astype(jnp.int32)


def with_ends(result, key, smallest, largest):
    dims = result.shape
    spot = [jax.random.randint(jax.random.fold_in(key, axis), (), 0, dims[axis]) for axis in range(len(dims))]
    result = result.at[tuple(spot)].set(smallest)
    longest = dims.index(max(dims))
    spot[longest] = (spot[longest] + 1) % dims[longest]
    return result.at[tuple(spot)].set(largest)


def strengthened(array, stream_key, source, target, blocks, factor):
    def block_of(axis_at):
        return (jnp.arange(array.shape[axis_at]) // (array.shape[axis_at] // blocks)).reshape((-1,) + (1,) * (array.ndim - 1 - axis_at))

    first = jax.random.permutation(stream_key, blocks)[block_of(target)]
    other_side = (block_of(target) + blocks // 2) % blocks
    return jnp.where((block_of(source) == first) | (block_of(source) == other_side), factor * array, array)


def block_scale(stream_key, dims, shards, smallest, top_value):
    def one(axis_at, shards_of):
        steps = jax.random.uniform(jax.random.fold_in(jax.random.fold_in(stream_key, 6), axis_at), (shards_of,), jnp.float32, smallest / len(shards), top_value / len(shards))
        return jnp.repeat(jnp.exp(steps), dims[axis_at] // shards_of).reshape((-1,) + (1,) * (len(dims) - axis_at - 1))

    loudness = one(*shards[0])
    for cut in shards[1:]:
        loudness = loudness * one(*cut)
    return loudness


def normal_values(stream_key, extent, deviation, most, pieces=(), held_as=jnp.bfloat16):
    result = deviation * jax.random.normal(stream_key, extent, jnp.float32)
    if pieces:
        result = result * block_scale(stream_key, extent, pieces, -0.22, 0.18)
    return jnp.clip(result, -most, most).astype(held_as)


def gaussian_with(key, extent, scale, most, cuts, heavy, kind=jnp.bfloat16):
    values = scale * jax.random.normal(key, extent, jnp.float32)
    if cuts:
        values = values * block_scale(key, extent, cuts, -0.22, 0.18)
    return jnp.clip(strengthened(values, jax.random.fold_in(key, 3), *heavy), -most, most).astype(kind)


def setup_inputs(seed: int = 0) -> dict:
    key_list = jax.random.split(jax.random.key(seed), 16)
    return {
        "new_hidden": normal_values(key_list[0], (R, D), 1.0, 6.0, ((0, 4), (1, 8))),
        "attn_gain": jnp.clip(1.0 + 0.18 * jax.random.normal(key_list[1], (D,), jnp.float32), 0.1, 1.9),
        "mlp_gain": jnp.clip(1.0 + 0.18 * jax.random.normal(key_list[2], (D,), jnp.float32), 0.1, 1.9),
        "qkv_weight": normal_values(key_list[3], (D, 3 * D), D ** -0.5, 0.078125, ((1, 8),)),
        "dense_weight": normal_values(key_list[4], (D, D), D ** -0.5, 0.078125, ((0, 8),)),
        "in_weight": normal_values(key_list[5], (D, FF), D ** -0.5, 0.078125, ((1, 32),)),
        "out_weight": gaussian_with(key_list[6], (FF, D), FF ** -0.5, 0.078125, ((0, 32),), (0, 1, 32, 2.75)),
        "page_store": draw_page_store(jax.random.fold_in(key_list[15], 71), 0),
        "held_states": normal_values(key_list[8], (R, NREC, D), 1.0, 6.0, ((0, 32),)),
        "fold_weights": jnp.clip(jax.random.uniform(key_list[9], (NF, PAGE), jnp.float32, 0.02, 0.14), 0.02, 0.14),
        "page_table": draw_page_table(jax.random.fold_in(key_list[15], 71), 0),
        "lengths": draw_lengths(jax.random.fold_in(key_list[15], 71), 0),
        "keep_slots": draw_keep_slots(jax.random.fold_in(key_list[15], 71), 0),
        "fold_index": with_ends(jax.random.randint(key_list[13], (R, PPR), 0, NF), jax.random.fold_in(key_list[13], 1), 0, NF - 1).astype(jnp.int32),
        "recompute_list": draw_recompute_list(jax.random.fold_in(key_list[15], 71), 0),
    }


EPSILON = 1e-05
ROT_BASE = 10000.0

def layer_norm(values, scale_gain):
    values = values.astype(jnp.float32)
    centered = values - lax.optimization_barrier(jnp.mean(values, axis=-1, keepdims=True))
    spread = lax.optimization_barrier(jnp.mean(centered * centered, axis=-1, keepdims=True))
    return centered * lax.rsqrt(spread + EPSILON) * scale_gain

def rotate(values, positions):
    half_rot = ROT // 2
    frequency = ROT_BASE ** (-2.0 * jnp.arange(half_rot, dtype=jnp.float32) / ROT)
    angles = positions.astype(jnp.float32)[..., None] * frequency
    cos_part = jnp.cos(angles)
    sin_part = jnp.sin(angles)
    lower_part = values[..., :half_rot]
    upper_part = values[..., half_rot:ROT]
    return jnp.concatenate([lower_part * cos_part - upper_part * sin_part, upper_part * cos_part + lower_part * sin_part, values[..., ROT:]], axis=-1)

def reference(new_hidden, attn_gain, mlp_gain, qkv_weight, dense_weight, in_weight, out_weight, page_store, held_states, fold_weights, page_table, lengths, keep_slots, fold_index, recompute_list):
    scale = 1.0 / math.sqrt(HD)
    normed_attn = layer_norm(new_hidden, attn_gain).astype(jnp.bfloat16)
    normed_mlp = layer_norm(new_hidden, mlp_gain).astype(jnp.bfloat16)
    projected = jnp.dot(normed_attn, qkv_weight, preferred_element_type=jnp.float32).reshape(R, H, 3, HD)
    new_pos = lengths[:, None]
    query = rotate(projected[:, :, 0], new_pos).astype(jnp.bfloat16)
    new_key = rotate(projected[:, :, 1], new_pos).astype(jnp.bfloat16)
    new_value = projected[:, :, 2].astype(jnp.bfloat16)
    key_weight = qkv_weight.reshape(D, H, 3, HD)[:, :, 1, :].reshape(D, D)
    normed_held = layer_norm(held_states.reshape(R * NREC, D), attn_gain).astype(jnp.bfloat16)
    fresh = jnp.dot(normed_held, key_weight, preferred_element_type=jnp.float32).reshape(R, NREC, H, HD)
    rec_slot = jnp.take_along_axis(keep_slots, recompute_list // PAGE, axis=1)
    rec_pos = rec_slot * PAGE + recompute_list % PAGE
    fresh = rotate(fresh, rec_pos[:, :, None]).astype(jnp.bfloat16)
    slot_ids = jnp.arange(PPR, dtype=jnp.int32)
    token_ids = jnp.arange(PAGE, dtype=jnp.int32)
    kept_ids = jnp.arange(KP * PAGE, dtype=jnp.int32)

    def one_request(request_items):
        table_row, length, keep_row, fold_row, rec_row, query_row, key_row, value_row, fresh_row = request_items
        page_rows = page_store[table_row]
        split_rows = page_rows.reshape(PPR, PAGE, H, 2, HD)
        kept = split_rows[keep_row].reshape(KP * PAGE, H, 2, HD)
        hits = (rec_row[:, None] == kept_ids[None, :]).astype(jnp.float32)
        touched = lax.optimization_barrier(jnp.sum(hits, axis=0)) > 0.5
        placed = jnp.einsum('nk,nhd->khd', hits, fresh_row.astype(jnp.float32))
        keys = jnp.where(touched[:, None, None], placed, kept[:, :, 0].astype(jnp.float32))
        values = kept[:, :, 1].astype(jnp.float32)
        is_kept = jnp.any(keep_row[:, None] == slot_ids[None, :], axis=0)
        dropped = jnp.logical_and(jnp.logical_not(is_kept), slot_ids * PAGE < length)
        live = slot_ids[:, None] * PAGE + token_ids[None, :] < length
        weight_rows = jnp.where(jnp.logical_and(live, dropped[:, None]), fold_weights[fold_row], 0.0)
        folded_row = jnp.einsum('jt,jtc->jc', weight_rows, page_rows.astype(jnp.float32), precision=lax.Precision.HIGHEST).astype(jnp.bfloat16)
        fold_pairs = folded_row.reshape(PPR, H, 2, HD).astype(jnp.float32)
        query_f = query_row.astype(jnp.float32)
        kept_scores = jnp.einsum('hd,khd->hk', query_f, keys) * scale
        fold_scores = jnp.einsum('hd,jhd->hj', query_f, fold_pairs[:, :, 0]) * scale
        fold_scores = jnp.where(dropped[None, :], fold_scores, -1e+30)
        own_score = lax.optimization_barrier(jnp.sum(query_f * key_row.astype(jnp.float32), axis=-1)) * scale
        top = jnp.maximum(jnp.maximum(lax.optimization_barrier(jnp.max(kept_scores, axis=-1)), lax.optimization_barrier(jnp.max(fold_scores, axis=-1))), own_score)
        kept_exp = jnp.exp(kept_scores - top[:, None])
        fold_exp = jnp.exp(fold_scores - top[:, None])
        own_exp = jnp.exp(own_score - top)
        total = lax.optimization_barrier(jnp.sum(kept_exp, axis=-1)) + lax.optimization_barrier(jnp.sum(fold_exp, axis=-1)) + own_exp
        kept_prob = (kept_exp / total[:, None]).astype(jnp.bfloat16).astype(jnp.float32)
        fold_prob = (fold_exp / total[:, None]).astype(jnp.bfloat16).astype(jnp.float32)
        own_prob = (own_exp / total).astype(jnp.bfloat16).astype(jnp.float32)
        mixed = jnp.einsum('hk,khd->hd', kept_prob, values) + jnp.einsum('hj,jhd->hd', fold_prob, fold_pairs[:, :, 1]) + own_prob[:, None] * value_row.astype(jnp.float32)
        return (mixed.reshape(D).astype(jnp.bfloat16), folded_row)
    attended, folded = lax.map(one_request, (page_table, lengths, keep_slots, fold_index, recompute_list, query, new_key, new_value, fresh))
    attn_part = jnp.dot(attended, dense_weight, preferred_element_type=jnp.float32)
    activated = jax.nn.gelu(jnp.dot(normed_mlp, in_weight, preferred_element_type=jnp.float32), approximate=False).astype(jnp.bfloat16)
    mlp_part = jnp.dot(activated, out_weight, preferred_element_type=jnp.float32)
    return ((attn_part + mlp_part).astype(jnp.bfloat16), folded)
```

```python
import functools
import math

import jax
import jax.numpy as jnp
import numpy as np
from jax import lax
from jax.experimental import pallas as pl
from jax.experimental.pallas import tpu as pltpu
from jax.sharding import PartitionSpec as P

D = 6144
H = 64
HD = 96
ROT = 24
PAGE = 16
PPR = 12
KP = 5
NREC = 8
NF = 8
FF = 24576

EPSILON = 1e-05
ROT_BASE = 10000.0
NEVER = -1e30
F32 = jnp.float32
BF16 = jnp.bfloat16
SCALE = 1.0 / math.sqrt(HD)
MIB = 1024 * 1024
STEP_HEADS = 32
QUAD = 4
OCTET = 8


def iota(shape, axis):
    return lax.broadcasted_iota(jnp.int32, shape, axis)


def dot(left, right):
    return jnp.dot(left, right, preferred_element_type=F32)


def dot_nt(left, right):
    return lax.dot_general(left, right, (((1,), (1,)), ((), ())), preferred_element_type=F32)


def dot_tn(left, right):
    return lax.dot_general(left, right, (((0,), (0,)), ((), ())), preferred_element_type=F32)


def parts_of(values, count):
    parts = []
    for _ in range(count):
        part = values.astype(BF16)
        parts.append(part)
        values = values - part.astype(F32)
    return parts


def split_dot(values, selector, count):
    total = None
    for part in parts_of(values, count):
        term = dot(part, selector)
        total = term if total is None else total + term
    return total


def wire_split(width):
    return (width // 128 + 1) // 2 * 128 if width % 128 == 0 else (width + 1) // 2


def to_wire(ref, index, rows):
    width = rows.shape[1]
    first = wire_split(width)
    ref[(*index, slice(None), slice(0, width))] = rows[:2].astype(BF16)
    rest = rows[2:3, first:]
    if width < 2 * first:
        rest = jnp.concatenate([rest, jnp.zeros((1, 2 * first - width), F32)], axis=1)
    tail = jnp.concatenate([rows[2:3, :first], rest], axis=0)
    ref[(*index, slice(None), slice(width, width + first))] = tail.astype(BF16)


def from_wire(ref, index, width, start, stop):
    first = wire_split(width)
    pair = ref[(*index, slice(None), slice(start, stop))].astype(F32)
    third = []
    if start < first:
        third.append(ref[(*index, slice(0, 1), slice(width + start, width + min(stop, first)))].astype(F32))
    if stop > first:
        begin = max(start, first) - first
        third.append(ref[(*index, slice(1, 2), slice(width + begin, width + stop - first))].astype(F32))
    third = third[0] if len(third) == 1 else jnp.concatenate(third, axis=1)
    return jnp.concatenate([pair, third, jnp.zeros_like(third)], axis=0)


def prep_kernel(dims, table_smem, table_ref, length_ref, keep_ref, choice_ref, list_ref, frequency_ref, *refs):
    n_pages, pages_dev, slots, period_heads = dims
    cos_ref, low_ref, high_ref, sel_ref, sel_all_ref, back_ref, pick_ref, number_ref = refs
    group = keep_ref.shape[0]
    n_rows = sel_ref.shape[0]
    mine = lax.axis_index("pages")

    ids = table_ref[:, :group]
    for g in range(1, n_pages):
        ids = jnp.where(mine == g, table_ref[:, g * group : (g + 1) * group], ids)
    holder = jnp.floor((ids.astype(F32) + 0.5) * (1.0 / pages_dev)).astype(jnp.int32)

    def one_request(r, rank):
        for j in range(PPR):
            other = table_smem[j, mine * group + r]
            earlier = (holder == lax.div(other, jnp.int32(pages_dev))) & (ids > other)
            rank = rank + jnp.where(earlier, 1, 0)
        return rank

    row = holder * slots + lax.fori_loop(0, group, one_request, jnp.zeros_like(ids))
    at = iota((n_rows, group), 0)
    hit = None
    for j in range(PPR):
        one = at == row[j : j + 1, :]
        hit = one if hit is None else hit | one
    hit = jnp.where(hit, 1.0, 0.0)
    same = jnp.where(iota((group, group), 0) == iota((group, group), 1), 1.0, 0.0)
    sel_ref[...] = hit.astype(BF16)
    sel_all_ref[:n_rows, :] = hit
    sel_all_ref[n_rows:, :] = same
    turned = row.astype(F32).T
    at = iota((group, n_rows), 1).astype(F32)
    back = jnp.zeros((group, n_rows), F32)
    for j in range(PPR):
        one = jnp.where(at == turned[:, j : j + 1], 1.0, 0.0)
        pick_ref[j * group : (j + 1) * group, :] = one.astype(BF16)
        back = back + one
    back_ref[:, :n_rows] = back.astype(BF16)
    back_ref[:, n_rows:] = same.astype(BF16)

    length = jnp.sum(same * length_ref[...].astype(F32), axis=1, keepdims=True)
    renewed = list_ref[...]
    slot = jnp.zeros_like(renewed)
    for k in range(KP):
        slot = jnp.where(jnp.right_shift(renewed, 4) == k, keep_ref[:, k : k + 1], slot)
    place = (slot * PAGE + jnp.bitwise_and(renewed, PAGE - 1)).astype(F32)
    place = jnp.broadcast_to(place[:, None, :], (group, NREC, NREC)).reshape(group * NREC, NREC)
    shape = (group * NREC, NREC)
    place = jnp.where(jnp.bitwise_and(iota(shape, 0), NREC - 1) == iota(shape, 1), place, 0.0)
    place = jnp.concatenate([length, jnp.sum(place, axis=1, keepdims=True)], axis=0)
    angle = place * frequency_ref[...]
    cosine, sine = jnp.cos(angle), jnp.sin(angle)
    lane = iota(angle.shape, 1)
    low = jnp.where(lane < ROT // 2, -sine, 0.0)
    high = jnp.where((lane >= ROT // 2) & (lane < ROT), sine, 0.0)
    one, none = jnp.ones_like(angle), jnp.zeros_like(angle)
    cos_ref[...] = jnp.concatenate([cosine, cosine, one] * period_heads, axis=1)
    low_ref[...] = jnp.concatenate([low, low, none] * period_heads, axis=1)
    high_ref[...] = jnp.concatenate([high, high, none] * period_heads, axis=1)
    numbers = [length.astype(jnp.int32), keep_ref[...], choice_ref[...], renewed]
    number_ref[...] = jnp.concatenate(numbers, axis=1)


def pack_kernel(held_ref, new_ref, out_ref):
    held_rows = held_ref.shape[0]
    group, chunk = new_ref.shape
    held = held_ref[...].astype(F32)
    rows = [held[:, c * chunk : (c + 1) * chunk] for c in range(D // chunk)] + [new_ref[...].astype(F32)]
    rows = jnp.concatenate(rows, axis=0).astype(BF16)
    for i in range(out_ref.shape[0]):
        out_ref[i] = rows


def project_kernel(dims, *refs):
    group, n_blk, held_rows, heads, slots = dims
    pack_refs, refs = refs[:2], refs[2:]
    gain_ref, weight_hbm, cos_ref, low_ref, high_ref, sel_ref, *refs = refs
    send_ref, own_ref, leaf_ref, weight_buf, rows_ref, acc_ref, sems = refs
    chunk = D // n_blk
    width = 3 * heads * HD
    head_lanes = heads * HD
    extra = 2 * heads * NREC
    period = cos_ref.shape[1]
    period_heads = period // (3 * HD)
    core = jnp.bitwise_and(lax.axis_index("blk"), 1)

    def weight_copy(part, step):
        return pltpu.make_async_copy(
            weight_hbm.at[pl.ds(step * chunk, chunk), pl.ds(part * period, period)],
            weight_buf.at[part, step],
            sems.at[part, step],
        )

    for part in range(width // period):
        for step in range(n_blk):
            weight_copy(part, step).start()

    pieces, places = [], []
    for other in range(2):
        for z in range(n_blk // 2):
            b = 2 * z + jnp.bitwise_xor(core, other)
            values = pack_refs[other][z].astype(F32)
            pieces.append(values[n_blk * held_rows :])
            places.append(b)
            values = values[: n_blk * held_rows].reshape(n_blk, held_rows, chunk)
            mean = jnp.sum(jnp.sum(values, axis=0), axis=1, keepdims=True) / D
            values = values - mean[None]
            spread = jnp.sum(jnp.sum(values * values, axis=0), axis=1, keepdims=True) / D
            values = values * lax.rsqrt(spread + EPSILON)[None]
            first = pl.multiple_of(group + b * held_rows, 8)
            for c in range(n_blk):
                rows_ref[c, pl.ds(first, held_rows), :] = values[c] * gain_ref[:, c * chunk : (c + 1) * chunk]
    leaf_ref[...] = jnp.concatenate(pieces, axis=0).astype(BF16)
    mean = sum(jnp.sum(piece, axis=1, keepdims=True) for piece in pieces) / D
    pieces = [piece - mean for piece in pieces]
    spread = sum(jnp.sum(piece * piece, axis=1, keepdims=True) for piece in pieces) / D
    spread = lax.rsqrt(spread + EPSILON)
    for i, (b, piece) in enumerate(zip(places, pieces)):
        z = i % (n_blk // 2)
        gain = gain_ref[:, 2 * z * chunk : 2 * (z + 1) * chunk]
        gain = jnp.where(b == 2 * z, gain[:, :chunk], gain[:, chunk:])
        rows_ref[b, 0:group, :] = piece * spread * gain

    rows = acc_ref.shape[0]
    wide = heads * NREC
    score = jnp.zeros((rows, wide), F32)
    head_at = jnp.right_shift(iota((rows, wide), 1), 3)
    queries, values = [], []
    for j in range(width // period):
        acc_ref[...] = jnp.zeros_like(acc_ref)

        def one_chunk(step, carry, j=j):
            weight_copy(j, step).wait()
            acc_ref[...] += dot(rows_ref[step].astype(BF16), weight_buf[j, step])
            return carry

        lax.fori_loop(0, n_blk, one_chunk, 0)
        block = acc_ref[...]
        up = jnp.concatenate([block[:, ROT // 2 :], block[:, : ROT // 2]], axis=1)
        down = jnp.concatenate([block[:, -ROT // 2 :], block[:, : -ROT // 2]], axis=1)
        turned = block * cos_ref[...] + up * low_ref[...] + down * high_ref[...]
        turned = turned.astype(BF16).astype(F32)
        for h in range(period_heads):
            first = h * 3 * HD
            query = turned[:group, first : first + HD]
            key = turned[:, first + HD : first + 2 * HD]
            queries.append(query)
            values.append(turned[:group, first + 2 * HD : first + 3 * HD])
            own_product = key[:group] * query
            held_product = key[group:].reshape(group, -1, HD) * query[:, None, :]
            product = jnp.concatenate([own_product, held_product.reshape(rows - group, HD)], axis=0)
            score = jnp.where(
                head_at == j * period_heads + h, jnp.sum(product, axis=1, keepdims=True), score
            )
    score = score * SCALE
    sel = sel_ref[...]
    asked = dot(sel, jnp.concatenate(queries, axis=1).astype(BF16))
    own_ref[:, :head_lanes] = jnp.concatenate(values, axis=1).astype(BF16)

    held_score = score[group:]
    held_count = held_score.shape[0]
    row_id = jnp.bitwise_and(iota((held_count, wide), 0), NREC - 1)
    lane_id = jnp.bitwise_and(iota((held_count, wide), 1), NREC - 1)
    held_score = jnp.where(row_id == lane_id, held_score, 0.0)
    per_request = held_count // group
    spread_ids = jnp.right_shift(iota((group, held_count), 1), per_request.bit_length() - 1)
    spread_rows = jnp.where(spread_ids == iota((group, held_count), 0), 1.0, 0.0).astype(BF16)
    sel_rows = dot(sel, spread_rows).astype(BF16)
    both = jnp.concatenate(parts_of(held_score, 2), axis=1)
    given = dot(sel_rows, both)
    both = jnp.concatenate([asked, given], axis=1)
    for d in range(send_ref.shape[0]):
        to_wire(send_ref, (d,), both[d * slots : (d + 1) * slots])

    own_score = score[:group]
    lane = iota((group, extra), 1)
    own = jnp.zeros((group, extra), F32)
    for i, part in enumerate(parts_of(own_score, 3)):
        part = part.astype(F32)
        for h in range(heads):
            own = jnp.where(lane == i * heads + h, part[:, h * NREC : h * NREC + 1], own)
    own_ref[:, head_lanes : head_lanes + extra] = own.astype(BF16)


def fold_kernel(weight_ref, page_ref, fold_ref):
    parts = jnp.concatenate(parts_of(weight_ref[...], 3), axis=0)
    rows = weight_ref.shape[0]
    sums = dot(parts, page_ref[...])
    folded = sums[:rows] + sums[rows : 2 * rows] + sums[2 * rows :]
    fold_ref[...] = folded.astype(BF16)


def place_kernel(dims, pick_ref, got_ref, out_ref, rows_ref):
    slots, width, first_lane = dims
    for d in range(got_ref.shape[0]):
        rows_ref[d * slots : (d + 1) * slots, :] = from_wire(got_ref, (d,), width, first_lane, width)
    found = dot(pick_ref[...], rows_ref[...].astype(BF16)).astype(BF16)
    group = out_ref.shape[1]
    for j in range(out_ref.shape[0]):
        out_ref[j] = found[j * group : (j + 1) * group]


def attend_kernel(dims, ask_ref, valid_ref, place_ref, page_ref, fold_ref, *refs):
    send_ref = refs[-1]
    n_pages, slots, dests, heads = dims
    rows = n_pages * slots
    head_lanes = heads * HD
    extra = 2 * heads * NREC
    tokens = page_ref.shape[0]
    asks = [
        jnp.concatenate(
            [from_wire(ask_ref, (g, b), head_lanes + extra, 0, head_lanes + extra) for g in range(n_pages)],
            axis=0,
        )
        for b in range(dests)
    ]
    query = jnp.concatenate([a[:, :head_lanes] for a in asks], axis=1)
    given = jnp.concatenate([a[:, head_lanes : head_lanes + extra] for a in asks], axis=1)
    valid = valid_ref[...] > 0.5
    place = place_ref[...]
    touched = jnp.sum(place[:, :NREC].astype(F32), axis=1, keepdims=True) > 0.5
    lanes = OCTET * rows
    shift = rows.bit_length() - 1
    lane_head = jnp.right_shift(iota((HD, lanes), 1), shift)
    blank = jnp.zeros((HD, lanes), F32)
    lane = iota((lanes, lanes), 1)
    lane_in = jnp.bitwise_and(lane, extra - 1)
    lane_dest = jnp.right_shift(lane, extra.bit_length() - 1) * heads
    given_head = jnp.right_shift(jnp.bitwise_and(lane_in, heads * NREC - 1), 3) + lane_dest
    row_head = jnp.right_shift(iota((lanes, lanes), 0), shift)
    own_lane = jnp.bitwise_and(iota((rows, lanes), 1), rows - 1) == iota((rows, lanes), 0)
    goals = []
    for i in range(3):
        hit = (lane_in >= i * heads) & (lane_in < (i + 1) * heads)
        hit = hit & (row_head == lane_dest + lane_in - i * heads)
        goals.append(jnp.where(hit, 1.0, 0.0).astype(BF16))
    gathered, extras = [], []
    for o in range(STEP_HEADS // OCTET):
        heads_here = range(o * OCTET, (o + 1) * OCTET)
        asked = jnp.concatenate([query[:, h * HD : (h + 1) * HD] for h in heads_here], axis=0)
        asked = jnp.concatenate([asked, jnp.zeros((lanes, 128 - HD), F32)], axis=1).T[:HD]
        stacked = []
        for h in range(OCTET):
            stacked += [jnp.where(lane_head == h, asked, 0.0), blank]
        stacked = jnp.concatenate(stacked, axis=0).astype(BF16)
        told = jnp.concatenate([given[:, o * lanes : (o + 1) * lanes]] * OCTET, axis=0)
        told = jnp.where(given_head == row_head, told, 0.0).T.astype(BF16)
        some = slice(o * OCTET * 2 * HD, (o + 1) * OCTET * 2 * HD)
        page = jnp.concatenate([page_ref[:, some], fold_ref[:, some]], axis=0)
        scores = jnp.where(touched, dot(place, told), dot(page, stacked) * SCALE)
        scores = jnp.where(valid, scores, NEVER)
        top = jnp.max(scores, axis=0, keepdims=True)
        weights = jnp.where(valid, jnp.exp(scores - top), 0.0)
        total = jnp.sum(weights, axis=0, keepdims=True)
        safe = jnp.where(total > 0.0, total, 1.0)
        rest = jnp.zeros((256 - weights.shape[0], lanes), F32)
        weights = jnp.concatenate([weights * (1.0 / safe), rest], axis=0).T.astype(BF16)
        page = jnp.concatenate([page, jnp.zeros((rest.shape[0], page.shape[1]), BF16)], axis=0)
        for i in range(OCTET // QUAD):
            mixed = dot(
                weights[i * QUAD * rows : (i + 1) * QUAD * rows],
                page[:, i * QUAD * 2 * HD : (i + 1) * QUAD * 2 * HD],
            )
            for h in range(QUAD):
                gathered.append(mixed[h * rows : (h + 1) * rows, 2 * HD * h + HD : 2 * HD * (h + 1)])
        lse = jnp.where(own_lane, jnp.where(total > 0.0, top + jnp.log(safe), NEVER), 0.0)
        spread = jnp.zeros((rows, lanes), F32)
        for part, goal in zip(parts_of(lse, 3), goals):
            spread = spread + dot(part, goal)
        extras.append(spread)
    gathered = jnp.concatenate(gathered, axis=1)
    extras = jnp.concatenate(extras, axis=1)
    width = 2 * head_lanes
    folded = fold_ref[...].astype(F32)
    for b in range(dests):
        whole = jnp.concatenate(
            [
                gathered[:, b * head_lanes : (b + 1) * head_lanes],
                extras[:, b * extra : (b + 1) * extra],
                folded[:, b * width : (b + 1) * width],
            ],
            axis=1,
        )
        for g in range(n_pages):
            to_wire(send_ref, (g, b), whole[g * slots : (g + 1) * slots])


def merge_kernel(
    dims, got_ref, own_ref, sel_ref, back_ref, *refs
):
    group, n_dev, slots, heads, n_pages = dims
    share_refs, dense_hbm, refs = refs[:n_pages], refs[n_pages], refs[n_pages + 1 :]
    head_lanes = heads * HD
    extra = 2 * heads * NREC
    n_blk = n_dev // n_pages
    out_ref, dense_buf, rows_ref, sems = refs
    chunk = D // n_blk
    steps, _, cols = dense_buf.shape

    def dense_copy(step):
        return pltpu.make_async_copy(
            dense_hbm.at[:, pl.ds(step * cols, cols)], dense_buf.at[step], sems.at[step]
        )

    for step in range(steps):
        dense_copy(step).start()
    for d in range(n_dev):
        rows_ref[d * slots : (d + 1) * slots, :] = from_wire(
            got_ref, (d,), 3 * head_lanes + extra, 0, head_lanes + extra
        )
    rows_ref[n_dev * slots :, :] = own_ref[...].astype(F32)
    count = rows_ref.shape[0]
    parts = rows_ref[:, head_lanes : head_lanes + extra].astype(BF16)
    to, source = iota((extra, 128), 1), iota((extra, 128), 0)
    hit = None
    for i in range(3):
        one = (to < heads) & (source == to + i * heads)
        hit = one if hit is None else hit | one
    lse = dot(parts, jnp.where(hit, 1.0, 0.0).astype(BF16))
    tops = jnp.zeros((count, 128), F32)
    for r in range(group):
        mine = sel_ref[:, r : r + 1] > 0.5
        top = jnp.max(jnp.where(mine, lse, -3e38), axis=0, keepdims=True)
        tops = jnp.where(mine, top, tops)
    weights = jnp.exp(jnp.minimum(lse - tops, 0.0))
    back = back_ref[...]
    totals = jnp.zeros((group, 128), F32)
    for part in parts_of(weights, 3):
        totals = totals + dot(back, part)
    inverse = 1.0 / totals
    lanes, heads_of = iota((128, head_lanes), 1), iota((128, head_lanes), 0)
    over = lanes - heads_of * HD
    spread = jnp.where((over >= 0) & (over < HD), 1.0, 0.0).astype(BF16)
    weighted = split_dot(weights, spread, 2) * rows_ref[:, :head_lanes]
    mixed = jnp.zeros((group, head_lanes), F32)
    for part in parts_of(weighted, 2):
        mixed = mixed + dot(back, part)
    attended = (mixed * split_dot(inverse, spread, 3)).astype(BF16)
    for step in range(steps):
        dense_copy(step).wait()
        some = slice(step * cols, (step + 1) * cols)
        result = dot(attended, dense_buf[step])
        for share_ref in share_refs:
            result = result + share_ref[:, some].astype(F32)
        for i in range(cols // chunk):
            out_ref[step * (cols // chunk) + i] = result[:, i * chunk : (i + 1) * chunk].astype(BF16)


def mlp_kernel(dims, *refs):
    group, n_pages, n_blk = dims
    leaf_refs, refs = refs[:n_pages], refs[n_pages:]
    gain_ref, in_hbm, out_hbm, _, *refs = refs
    part_refs, (in_buf, out_buf, rows_ref, sems_in, sems_out) = refs[:n_pages], refs[n_pages:]
    chunk = D // n_blk
    n_steps, cols = out_buf.shape[0], out_buf.shape[2]
    core = jnp.bitwise_and(lax.axis_index("blk"), 1)

    def in_copy(step):
        return pltpu.make_async_copy(
            in_hbm.at[pl.ds(step * chunk, chunk), :], in_buf.at[step], sems_in.at[step]
        )

    def out_copy(step):
        return pltpu.make_async_copy(
            out_hbm.at[:, pl.ds(step * cols, cols)], out_buf.at[step], sems_out.at[step]
        )

    for step in range(n_blk):
        in_copy(step).start()
    for step in range(n_steps):
        out_copy(step).start()
    for g in range(n_pages):
        leaf = leaf_refs[g][...].astype(F32)
        pieces = [leaf[i * group : (i + 1) * group] for i in range(n_blk)]
        mean = sum(jnp.sum(piece, axis=1, keepdims=True) for piece in pieces) / D
        pieces = [piece - mean for piece in pieces]
        spread = sum(jnp.sum(piece * piece, axis=1, keepdims=True) for piece in pieces) / D
        spread = lax.rsqrt(spread + EPSILON)
        for i in range(n_blk):
            c = 2 * (i % (n_blk // 2)) + jnp.bitwise_xor(core, i // (n_blk // 2))
            z = i % (n_blk // 2)
            gain = gain_ref[:, 2 * z * chunk : 2 * (z + 1) * chunk]
            gain = jnp.where(c == 2 * z, gain[:, :chunk], gain[:, chunk:])
            rows_ref[c, g * group : (g + 1) * group, :] = pieces[i] * spread * gain
    hidden = jnp.zeros((n_pages * group, in_buf.shape[2]), F32)
    for step in range(n_blk):
        in_copy(step).wait()
        hidden = hidden + dot(rows_ref[step].astype(BF16), in_buf[step])
    active = (0.5 * hidden * (1.0 + lax.erf(hidden * math.sqrt(0.5)))).astype(BF16)
    for step in range(n_steps):
        out_copy(step).wait()
        result = dot(active, out_buf[step]).astype(BF16)
        for g in range(n_pages):
            part_refs[g][:, step * cols : (step + 1) * cols] = result[g * group : (g + 1) * group]


VMEM = pl.BlockSpec(memory_space=pltpu.VMEM)
HBM = pl.BlockSpec(memory_space=pltpu.HBM)
ANY = pl.BlockSpec(memory_space=pl.ANY)


def shape_of(shape, kind=BF16):
    return jax.ShapeDtypeStruct(shape, kind)


def params_of(mib):
    return pltpu.CompilerParams(vmem_limit_bytes=mib * MIB)


def cost_of(flops, nbytes):
    return pl.CostEstimate(flops=int(flops), bytes_accessed=int(nbytes), transcendentals=0)


def on_device(
    new_hidden,
    attn_gain,
    mlp_gain,
    qkv_weight,
    dense_weight,
    in_weight,
    out_weight,
    page_store,
    held_states,
    fold_weights,
    page_table,
    lengths,
    keep_slots,
    fold_index,
    recompute_list,
):
    n_pages = lax.axis_size("pages")
    n_blk = lax.axis_size("blk")
    n_dev = n_pages * n_blk
    mine = lax.axis_index("pages")
    device = lax.axis_index(("pages", "blk"))
    group = lengths.shape[0]
    pages_dev = page_store.shape[0]
    slots = -(-(pages_dev // n_pages) // 4) * 4
    ranks = n_pages * slots
    heads = H // n_blk
    head_lanes = heads * HD
    extra = 2 * heads * NREC
    lanes = head_lanes + extra
    chunk = D // n_blk
    held_rows = held_states.shape[0] * NREC
    kept_count = KP * PAGE

    def swapped(array, axis, size, by):
        return lax.ppermute(array, axis, [(i, i ^ by) for i in range(size)])

    def swapped(array, axis, size, by):
        return lax.ppermute(array, axis, [(i, i ^ by) for i in range(size)])

    def fixed(array):
        return pltpu.with_memory_space_constraint(array, pltpu.HBM)

    half = n_blk // 2
    pack = pl.pallas_call(
        pack_kernel,
        in_specs=[VMEM, VMEM],
        out_specs=VMEM,
        out_shape=shape_of((half, n_blk * held_rows + group, chunk)),
        compiler_params=params_of(16),
        name="pack",
    )(fixed(held_states.reshape(held_rows, D)), fixed(new_hidden))
    pack = lax.all_to_all(
        pack,
        "blk",
        0,
        0,
        axis_index_groups=[list(range(core, n_blk, 2)) for core in range(2)],
        tiled=True,
    )
    packs = [pack, swapped(pack, "blk", n_blk, 1)]

    n_rows = n_dev * slots
    rows = group * (1 + NREC)
    period = 12 * HD if (3 * head_lanes) % (12 * HD) == 0 else 3 * head_lanes
    lane = np.arange(HD)
    frequency = np.where(lane < ROT, ROT_BASE ** (-2.0 * (lane % (ROT // 2)) / ROT), 0.0).astype(np.float32)
    cosine, low, high, sel, sel_all, back, pick, numbers = pl.pallas_call(
        functools.partial(prep_kernel, (n_pages, pages_dev, slots, period // (3 * HD))),
        in_specs=[pl.BlockSpec(memory_space=pltpu.SMEM)] + [VMEM] * 6,
        out_specs=[VMEM] * 8,
        out_shape=[
            *[shape_of((rows, period), F32)] * 3,
            shape_of((n_rows, group)),
            shape_of((n_rows + group, group), F32),
            shape_of((group, n_rows + group)),
            shape_of((PPR * group, n_rows)),
            shape_of((group, 1 + KP + PPR + NREC), jnp.int32),
        ],
        compiler_params=params_of(16),
        cost_estimate=cost_of(0, 0),
        name="prep",
    )(
        page_table.T,
        fixed(page_table.T),
        fixed(lengths[None]),
        fixed(keep_slots),
        fixed(fold_index),
        fixed(recompute_list),
        fixed(jnp.asarray(frequency[None])),
    )

    numbers = jnp.concatenate(
        [numbers] + [swapped(numbers, "pages", n_pages, i) for i in range(1, n_pages)], axis=0
    )

    tokens = pages_dev * PAGE
    pages = page_store.reshape(tokens, 2 * D)
    steps = H // STEP_HEADS
    step_lanes = STEP_HEADS * 2 * HD
    dests = STEP_HEADS // heads
    fold_width = 2 * head_lanes

    wire = lanes + wire_split(lanes)
    send, own, leaf = pl.pallas_call(
        functools.partial(project_kernel, (group, n_blk, held_rows, heads, slots)),
        in_specs=[VMEM] * 3 + [HBM] + [VMEM] * 4,
        out_specs=[VMEM] * 3,
        out_shape=[
            shape_of((n_dev, 2, wire)),
            shape_of((group, lanes)),
            shape_of((n_blk * group, chunk)),
        ],
        scratch_shapes=[
            pltpu.VMEM((3 * head_lanes // period, n_blk, chunk, period), BF16),
            pltpu.VMEM((n_blk, rows, chunk), F32),
            pltpu.VMEM((rows, period), F32),
            pltpu.SemaphoreType.DMA((3 * head_lanes // period, n_blk)),
        ],
        compiler_params=params_of(50),
        cost_estimate=cost_of(2 * rows * D * 3 * head_lanes, 6 * D * head_lanes),
        name="project",
    )(
        *packs,
        fixed(attn_gain[None]),
        fixed(qkv_weight),
        cosine,
        low,
        high,
        sel,
    )
    send, numbers, late_table = lax.optimization_barrier((send, numbers, page_table))
    asked = lax.all_to_all(send, ("pages", "blk"), 0, 0, tiled=True)

    token = jnp.arange(tokens, dtype=jnp.int32)
    local, inside = token // PAGE, token % PAGE
    found = late_table[:, :, None] == (device * pages_dev + local)[None, None, :]
    request_hit = jnp.any(found, axis=1)
    slot_hit = jnp.any(found, axis=0)
    slot_ids = jnp.arange(PPR, dtype=jnp.int32)
    slot = jnp.sum(jnp.where(slot_hit, slot_ids[:, None], 0), axis=0)
    request = jnp.sum(jnp.where(request_hit, jnp.arange(n_pages * group, dtype=jnp.int32)[:, None], 0), axis=0)
    owner = request // group
    request_hit = (
        jnp.arange(n_pages * group, dtype=jnp.int32)[:, None]
        == (jnp.bitwise_xor(owner, mine) * group + request % group)[None]
    )
    facts = jnp.dot(numbers.astype(BF16).T, request_hit.astype(BF16), preferred_element_type=F32).astype(jnp.int32)
    length, keeps = facts[0], facts[1 : 1 + KP]
    choices, renewed = facts[1 + KP : 1 + KP + PPR], facts[1 + KP + PPR :]
    choice = jnp.sum(jnp.where(slot_hit, choices, 0), axis=0)
    kept_hit = keeps == slot[None]
    kept = jnp.any(kept_hit, axis=0)
    kept_place = jnp.sum(jnp.where(kept_hit, jnp.arange(KP, dtype=jnp.int32)[:, None] * PAGE, 0), axis=0)
    dropped = jnp.logical_and(jnp.logical_not(kept), slot * PAGE < length)
    live = slot * PAGE + inside < length
    fold_row = jnp.sum(
        jnp.where(
            choice[None] == jnp.arange(NF, dtype=jnp.int32)[:, None],
            jnp.tile(fold_weights, (1, pages_dev)),
            0.0,
        ),
        axis=0,
    )
    earlier = (owner[:, None] == owner[None]) & (local[:, None] < local[None]) & (inside == 0)[:, None]
    rank_in = jnp.sum(earlier.astype(jnp.int32), axis=0)
    rank = owner * slots + rank_in
    ids = jnp.arange(ranks, dtype=jnp.int32)
    rank_hit = ids[:, None] == rank[None]
    fold_rows = jnp.where(rank_hit & (dropped & live)[None], fold_row[None], 0.0)
    fold_drop = jnp.any(rank_hit & dropped[None], axis=1)
    octet_lane = jnp.arange(OCTET * ranks, dtype=jnp.int32) % ranks
    valid = jnp.concatenate(
        [
            ((rank[:, None] == octet_lane[None]) & kept[:, None]).astype(F32),
            ((ids[:, None] == octet_lane[None]) & fold_drop[:, None]).astype(F32),
        ],
        axis=0,
    )
    renew = ((renewed == (kept_place + inside)[None]) & kept[None]).astype(BF16)
    renew = jnp.pad(jnp.tile(renew.T, (1, 2 * OCTET)), ((0, ranks), (0, 0)))

    leaf, fold_rows = lax.optimization_barrier((leaf, fold_rows))
    leaves = [leaf] + [swapped(leaf, "pages", n_pages, i) for i in range(1, n_pages)]

    folded_rows = pl.pallas_call(
        fold_kernel,
        grid=(steps,),
        in_specs=[
            pl.BlockSpec((ranks, tokens), lambda i: (0, 0)),
            pl.BlockSpec((tokens, step_lanes), lambda i: (0, i)),
        ],
        out_specs=pl.BlockSpec((ranks, step_lanes), lambda i: (0, i)),
        out_shape=shape_of((ranks, 2 * D)),
        compiler_params=params_of(16),
        cost_estimate=cost_of(0, 0),
        name="fold",
    )(fold_rows, fixed(pages))

    all_lanes = lanes + fold_width
    all_wire = all_lanes + wire_split(all_lanes)
    partial = pl.pallas_call(
        functools.partial(attend_kernel, (n_pages, slots, dests, heads)),
        grid=(steps,),
        in_specs=[
            pl.BlockSpec((n_pages, dests, 2, wire), lambda i: (0, i, 0, 0)),
            pl.BlockSpec((tokens + ranks, OCTET * ranks), lambda i: (0, 0)),
            pl.BlockSpec((tokens + ranks, 2 * OCTET * NREC), lambda i: (0, 0)),
            pl.BlockSpec((tokens, step_lanes), lambda i: (0, i)),
            pl.BlockSpec((ranks, step_lanes), lambda i: (0, i)),
            *[ANY] * (n_pages - 1),
        ],
        out_specs=pl.BlockSpec((n_pages, dests, 2, all_wire), lambda i: (0, i, 0, 0)),
        out_shape=shape_of((n_pages, n_blk, 2, all_wire)),
        compiler_params=params_of(16),
        cost_estimate=cost_of(2 * 128 * tokens * 2 * D, tokens * 4 * D),
        name="attend",
    )(asked.reshape(n_pages, n_blk, 2, wire), valid, renew, fixed(pages), folded_rows, *leaves[1:])
    got = lax.all_to_all(partial.reshape(n_dev, 2, all_wire), ("pages", "blk"), 0, 0, tiled=True)

    hidden = in_weight.shape[1]
    mlp_parts = pl.pallas_call(
        functools.partial(mlp_kernel, (group, n_pages, n_blk)),
        in_specs=[VMEM] * (n_pages + 1) + [HBM, HBM, ANY],
        out_specs=[VMEM] * n_pages,
        out_shape=[shape_of((group, D))] * n_pages,
        scratch_shapes=[
            pltpu.VMEM((n_blk, chunk, hidden), BF16),
            pltpu.VMEM((8, hidden, D // 8), BF16),
            pltpu.VMEM((n_blk, n_pages * group, chunk), F32),
            pltpu.SemaphoreType.DMA((n_blk,)),
            pltpu.SemaphoreType.DMA((8,)),
        ],
        compiler_params=params_of(24),
        cost_estimate=cost_of(4 * n_pages * group * D * hidden, 4 * D * hidden),
        name="mlp",
    )(*leaves, fixed(mlp_gain[None]), fixed(in_weight), fixed(out_weight), partial)
    mlp_share = [mlp_parts[0]] + [swapped(mlp_parts[i], "pages", n_pages, i) for i in range(1, n_pages)]

    out_part = pl.pallas_call(
        functools.partial(merge_kernel, (group, n_dev, slots, heads, n_pages)),
        in_specs=[VMEM] * (n_pages + 4) + [HBM],
        out_specs=VMEM,
        out_shape=shape_of((n_blk, group, chunk)),
        scratch_shapes=[
            pltpu.VMEM((8, head_lanes, D // 8), BF16),
            pltpu.VMEM((n_rows + group, lanes), F32),
            pltpu.SemaphoreType.DMA((8,)),
        ],
        compiler_params=params_of(24),
        cost_estimate=cost_of(2 * group * D * head_lanes, 2 * D * head_lanes),
        name="merge",
    )(
        got,
        own,
        sel_all,
        back,
        *mlp_share,
        fixed(dense_weight),
    )
    out_got = lax.all_to_all(out_part, "blk", 0, 0, tiled=True)
    summed = jnp.sum(out_got.astype(F32), axis=0).astype(BF16)

    folded = pl.pallas_call(
        functools.partial(place_kernel, (slots, all_lanes, lanes)),
        in_specs=[VMEM, VMEM],
        out_specs=VMEM,
        out_shape=shape_of((PPR, group, fold_width)),
        scratch_shapes=[pltpu.VMEM((n_rows, fold_width), F32)],
        compiler_params=params_of(16),
        cost_estimate=cost_of(0, 4 * n_rows * fold_width),
        name="place",
    )(pick, got)
    folded = jnp.transpose(folded, (1, 0, 2))
    return (summed, folded)


def solution(mesh):
    in_specs = (
        P("pages", "blk"),
        P(),
        P(),
        P(None, "blk"),
        P("blk", None),
        P(None, ("pages", "blk")),
        P(("pages", "blk"), None),
        P(("pages", "blk"), None, None),
        P(("pages", "blk"), None, None),
        P(),
        P(),
        P("pages"),
        P("pages", None),
        P("pages", None),
        P("pages", None),
    )
    out_specs = (P("pages", "blk"), P("pages", None, "blk"))
    return jax.shard_map(
        on_device, mesh=mesh, in_specs=in_specs, out_specs=out_specs, check_vma=False
    )
```

```python
import functools
import math

import jax
import jax.numpy as jnp
import numpy as np
from jax import lax
from jax.experimental import pallas as pl
from jax.experimental.pallas import tpu as pltpu
from jax.sharding import PartitionSpec as P

D = 6144
H = 64
HD = 96
ROT = 24
PAGE = 16
PPR = 12
KP = 5
NREC = 8
NF = 8
FF = 24576

EPSILON = 1e-05
ROT_BASE = 10000.0
NEVER = -1e30
F32 = jnp.float32
BF16 = jnp.bfloat16
SCALE = 1.0 / math.sqrt(HD)
MIB = 1024 * 1024
STEP_HEADS = 32
QUAD = 4
OCTET = 8


def iota(shape, axis):
    return lax.broadcasted_iota(jnp.int32, shape, axis)


def dot(left, right):
    return jnp.dot(left, right, preferred_element_type=F32)


def dot_nt(left, right):
    return lax.dot_general(left, right, (((1,), (1,)), ((), ())), preferred_element_type=F32)


def dot_tn(left, right):
    return lax.dot_general(left, right, (((0,), (0,)), ((), ())), preferred_element_type=F32)


def parts_of(values, count):
    parts = []
    for _ in range(count):
        part = values.astype(BF16)
        parts.append(part)
        values = values - part.astype(F32)
    return parts


def split_dot(values, selector, count):
    total = None
    for part in parts_of(values, count):
        term = dot(part, selector)
        total = term if total is None else total + term
    return total


def wire_split(width):
    return (width // 128 + 1) // 2 * 128 if width % 128 == 0 else (width + 1) // 2


def to_wire(ref, index, rows):
    width = rows.shape[1]
    first = wire_split(width)
    ref[(*index, slice(None), slice(0, width))] = rows[:2].astype(BF16)
    rest = rows[2:3, first:]
    if width < 2 * first:
        rest = jnp.concatenate([rest, jnp.zeros((1, 2 * first - width), F32)], axis=1)
    tail = jnp.concatenate([rows[2:3, :first], rest], axis=0)
    ref[(*index, slice(None), slice(width, width + first))] = tail.astype(BF16)


def from_wire(ref, index, width, start, stop):
    first = wire_split(width)
    pair = ref[(*index, slice(None), slice(start, stop))].astype(F32)
    third = []
    if start < first:
        third.append(ref[(*index, slice(0, 1), slice(width + start, width + min(stop, first)))].astype(F32))
    if stop > first:
        begin = max(start, first) - first
        third.append(ref[(*index, slice(1, 2), slice(width + begin, width + stop - first))].astype(F32))
    third = third[0] if len(third) == 1 else jnp.concatenate(third, axis=1)
    return jnp.concatenate([pair, third, jnp.zeros_like(third)], axis=0)


def prep_kernel(dims, table_smem, table_ref, length_ref, keep_ref, choice_ref, list_ref, frequency_ref, *refs):
    n_pages, pages_dev, slots, period_heads = dims
    cos_ref, low_ref, high_ref, sel_ref, sel_all_ref, back_ref, pick_ref, number_ref = refs
    group = keep_ref.shape[0]
    n_rows = sel_ref.shape[0]
    mine = lax.axis_index("pages")

    ids = table_ref[:, :group]
    for g in range(1, n_pages):
        ids = jnp.where(mine == g, table_ref[:, g * group : (g + 1) * group], ids)
    holder = jnp.floor((ids.astype(F32) + 0.5) * (1.0 / pages_dev)).astype(jnp.int32)

    def one_request(r, rank):
        for j in range(PPR):
            other = table_smem[j, mine * group + r]
            earlier = (holder == lax.div(other, jnp.int32(pages_dev))) & (ids > other)
            rank = rank + jnp.where(earlier, 1, 0)
        return rank

    row = holder * slots + lax.fori_loop(0, group, one_request, jnp.zeros_like(ids))
    at = iota((n_rows, group), 0)
    hit = None
    for j in range(PPR):
        one = at == row[j : j + 1, :]
        hit = one if hit is None else hit | one
    hit = jnp.where(hit, 1.0, 0.0)
    same = jnp.where(iota((group, group), 0) == iota((group, group), 1), 1.0, 0.0)
    sel_ref[...] = hit.astype(BF16)
    sel_all_ref[:n_rows, :] = hit
    sel_all_ref[n_rows:, :] = same
    turned = row.astype(F32).T
    at = iota((group, n_rows), 1).astype(F32)
    back = jnp.zeros((group, n_rows), F32)
    for j in range(PPR):
        one = jnp.where(at == turned[:, j : j + 1], 1.0, 0.0)
        pick_ref[j * group : (j + 1) * group, :] = one.astype(BF16)
        back = back + one
    back_ref[:, :n_rows] = back.astype(BF16)
    back_ref[:, n_rows:] = same.astype(BF16)

    length = jnp.sum(same * length_ref[...].astype(F32), axis=1, keepdims=True)
    renewed = list_ref[...]
    slot = jnp.zeros_like(renewed)
    for k in range(KP):
        slot = jnp.where(jnp.right_shift(renewed, 4) == k, keep_ref[:, k : k + 1], slot)
    place = (slot * PAGE + jnp.bitwise_and(renewed, PAGE - 1)).astype(F32)
    place = jnp.broadcast_to(place[:, None, :], (group, NREC, NREC)).reshape(group * NREC, NREC)
    shape = (group * NREC, NREC)
    place = jnp.where(jnp.bitwise_and(iota(shape, 0), NREC - 1) == iota(shape, 1), place, 0.0)
    place = jnp.concatenate([length, jnp.sum(place, axis=1, keepdims=True)], axis=0)
    angle = place * frequency_ref[...]
    cosine, sine = jnp.cos(angle), jnp.sin(angle)
    lane = iota(angle.shape, 1)
    low = jnp.where(lane < ROT // 2, -sine, 0.0)
    high = jnp.where((lane >= ROT // 2) & (lane < ROT), sine, 0.0)
    one, none = jnp.ones_like(angle), jnp.zeros_like(angle)
    cos_ref[...] = jnp.concatenate([cosine, cosine, one] * period_heads, axis=1)
    low_ref[...] = jnp.concatenate([low, low, none] * period_heads, axis=1)
    high_ref[...] = jnp.concatenate([high, high, none] * period_heads, axis=1)
    numbers = [length.astype(jnp.int32), keep_ref[...], choice_ref[...], renewed]
    number_ref[...] = jnp.concatenate(numbers, axis=1)


def facts_kernel(dims, *refs):
    n_pages, pages_dev, slots = dims
    number_refs, (table_ref, fold_ref, weight_ref, valid_ref, renew_ref) = refs[:n_pages], refs[n_pages:]
    group = number_refs[0].shape[0]
    requests = n_pages * group
    ranks = n_pages * slots
    mine = lax.axis_index("pages")
    device = lax.axis_index(("pages", "blk"))
    numbers = []
    for g in range(n_pages):
        got = number_refs[0][...]
        for i in range(1, n_pages):
            got = jnp.where(jnp.bitwise_xor(mine, g) == i, number_refs[i][...], got)
        numbers.append(got.astype(F32))
    numbers = jnp.concatenate(numbers, axis=0).astype(BF16)

    local = iota((ranks, requests), 0)
    hits = jnp.zeros((ranks, requests), F32)
    slot = jnp.zeros((ranks, 1), F32)
    for j in range(PPR):
        one = jnp.where(local == table_ref[j : j + 1, :] - device * pages_dev, 1.0, 0.0)
        hits = hits + one
        slot = slot + j * jnp.sum(one, axis=1, keepdims=True)
    hits = jnp.where(local < pages_dev, hits, 0.0)
    facts = dot(hits.astype(BF16), numbers)
    length, keeps = facts[:, :1], facts[:, 1 : 1 + KP]
    choices, renewed = facts[:, 1 + KP : 1 + KP + PPR], facts[:, 1 + KP + PPR : 1 + KP + PPR + NREC]
    place = iota((ranks, PPR), 1).astype(F32)
    choice = jnp.sum(jnp.where(place == slot, choices, 0.0), axis=1, keepdims=True)
    found = jnp.sum(hits, axis=1, keepdims=True) > 0.5
    kept_hit = jnp.where(keeps == slot, 1.0, 0.0)
    kept = (jnp.sum(kept_hit, axis=1, keepdims=True) > 0.5) & found
    kept_place = PAGE * jnp.sum(kept_hit * iota((ranks, KP), 1).astype(F32), axis=1, keepdims=True)
    dropped = jnp.logical_not(kept) & found & (slot * PAGE < length)

    owner = jnp.concatenate(
        [jnp.sum(hits[:, g * group : (g + 1) * group], axis=1, keepdims=True) for g in range(n_pages)], axis=1
    )
    below = jnp.where(iota((ranks, ranks), 0) > iota((ranks, ranks), 1), 1.0, 0.0).astype(BF16)
    before = dot(below, owner.astype(BF16))
    rank = jnp.sum(owner * (before + slots * iota((ranks, n_pages), 1).astype(F32)), axis=1, keepdims=True)
    rank = jnp.where(found, rank, -1.0)
    rank_hit = jnp.where(rank == iota((ranks, ranks), 1).astype(F32), 1.0, 0.0).astype(BF16)

    weights = jnp.zeros((ranks, PAGE), F32)
    for f in range(NF):
        weights = jnp.where(choice == f, fold_ref[f : f + 1, :], weights)
    live = slot * PAGE + iota((ranks, PAGE), 1).astype(F32) < length
    weights = jnp.where(live & dropped, weights, 0.0)
    weights = jnp.concatenate([weights] * pages_dev, axis=1)
    tokens = pages_dev * PAGE
    own = jnp.right_shift(iota((ranks, tokens), 1), 4) == iota((ranks, tokens), 0)
    weights = jnp.where(own, weights, 0.0)
    total = jnp.zeros((ranks, tokens), F32)
    for part in parts_of(weights, 3):
        total = total + dot_tn(rank_hit, part)
    weight_ref[...] = total

    lanes = valid_ref.shape[1]
    lane_rank = jnp.bitwise_and(iota((ranks, lanes), 1), ranks - 1).astype(F32)
    for_rank = jnp.where(lane_rank == rank, 1.0, 0.0)
    kept_for = jnp.where(kept, for_rank, 0.0)
    dropped_for = jnp.where(dropped, for_rank, 0.0)
    renewed = jnp.concatenate([renewed] * (renew_ref.shape[1] // NREC), axis=1)
    renewed = jnp.where(kept, renewed - kept_place, -1.0)
    inside = iota((PAGE, renew_ref.shape[1]), 0).astype(F32)
    for p in range(pages_dev):
        some = slice(p * PAGE, (p + 1) * PAGE)
        valid_ref[some, :] = jnp.broadcast_to(kept_for[p : p + 1, :], (PAGE, lanes))
        renew_ref[some, :] = jnp.where(inside == renewed[p : p + 1, :], 1.0, 0.0).astype(BF16)
    valid_ref[tokens:, :] = dot_tn(rank_hit, dropped_for.astype(BF16))
    renew_ref[tokens:, :] = jnp.zeros((ranks, renew_ref.shape[1]), BF16)


def pack_kernel(held_ref, new_ref, gain_ref, out_ref):
    group, chunk = new_ref.shape
    held = held_ref[...].astype(F32)
    held = held - jnp.sum(held, axis=1, keepdims=True) / D
    spread = jnp.sum(held * held, axis=1, keepdims=True) / D
    held = held * lax.rsqrt(spread + EPSILON) * gain_ref[...]
    rows = [held[:, c * chunk : (c + 1) * chunk] for c in range(D // chunk)] + [new_ref[...].astype(F32)]
    rows = jnp.concatenate(rows, axis=0).astype(BF16)
    for i in range(out_ref.shape[0]):
        out_ref[i] = rows


def project_kernel(dims, *refs):
    group, n_blk, held_rows, heads, slots = dims
    pack_refs, refs = refs[:2], refs[2:]
    gain_ref, mlp_gain_ref, weight_hbm, cos_ref, low_ref, high_ref, sel_ref, *refs = refs
    send_ref, own_ref, leaf_ref, weight_buf, rows_ref, acc_ref, sems = refs
    chunk = D // n_blk
    width = 3 * heads * HD
    head_lanes = heads * HD
    extra = 2 * heads * NREC
    period = cos_ref.shape[1]
    period_heads = period // (3 * HD)
    core = jnp.bitwise_and(lax.axis_index("blk"), 1)

    def weight_copy(part, step):
        return pltpu.make_async_copy(
            weight_hbm.at[pl.ds(step * chunk, chunk), pl.ds(part * period, period)],
            weight_buf.at[part, step],
            sems.at[part, step],
        )

    for part in range(width // period):
        for step in range(n_blk):
            weight_copy(part, step).start()

    pieces, places = [], []
    for other in range(2):
        for z in range(n_blk // 2):
            b = 2 * z + jnp.bitwise_xor(core, other)
            values = pack_refs[other][z].astype(F32)
            pieces.append(values[n_blk * held_rows :])
            places.append(b)
            first = pl.multiple_of(group + b * held_rows, 8)
            for c in range(n_blk):
                rows_ref[c, pl.ds(first, held_rows), :] = values[c * held_rows : (c + 1) * held_rows]
    mean = sum(jnp.sum(piece, axis=1, keepdims=True) for piece in pieces) / D
    pieces = [piece - mean for piece in pieces]
    spread = sum(jnp.sum(piece * piece, axis=1, keepdims=True) for piece in pieces) / D
    spread = lax.rsqrt(spread + EPSILON)
    leaves = []
    for i, (b, piece) in enumerate(zip(places, pieces)):
        z = i % (n_blk // 2)
        some = slice(2 * z * chunk, 2 * (z + 1) * chunk)
        gain, mlp_gain = (
            jnp.where(b == 2 * z, ref[:, some][:, :chunk], ref[:, some][:, chunk:])
            for ref in (gain_ref, mlp_gain_ref)
        )
        piece = piece * spread
        rows_ref[b, 0:group, :] = piece * gain
        leaves.append(piece * mlp_gain)
    leaf_ref[...] = jnp.concatenate(leaves, axis=0).astype(BF16)

    rows = acc_ref.shape[0]
    wide = heads * NREC
    score = jnp.zeros((rows, wide), F32)
    head_at = jnp.right_shift(iota((rows, wide), 1), 3)
    queries, values = [], []
    for j in range(width // period):
        acc_ref[...] = jnp.zeros_like(acc_ref)

        def one_chunk(step, carry, j=j):
            weight_copy(j, step).wait()
            acc_ref[...] += dot(rows_ref[step].astype(BF16), weight_buf[j, step])
            return carry

        lax.fori_loop(0, n_blk, one_chunk, 0)
        block = acc_ref[...]
        up = jnp.concatenate([block[:, ROT // 2 :], block[:, : ROT // 2]], axis=1)
        down = jnp.concatenate([block[:, -ROT // 2 :], block[:, : -ROT // 2]], axis=1)
        turned = block * cos_ref[...] + up * low_ref[...] + down * high_ref[...]
        turned = turned.astype(BF16).astype(F32)
        for h in range(period_heads):
            first = h * 3 * HD
            query = turned[:group, first : first + HD]
            key = turned[:, first + HD : first + 2 * HD]
            queries.append(query)
            values.append(turned[:group, first + 2 * HD : first + 3 * HD])
            own_product = key[:group] * query
            held_product = key[group:].reshape(group, -1, HD) * query[:, None, :]
            product = jnp.concatenate([own_product, held_product.reshape(rows - group, HD)], axis=0)
            score = jnp.where(
                head_at == j * period_heads + h, jnp.sum(product, axis=1, keepdims=True), score
            )
    score = score * SCALE
    sel = sel_ref[...]
    asked = dot(sel, jnp.concatenate(queries, axis=1).astype(BF16))
    own_ref[:, :head_lanes] = jnp.concatenate(values, axis=1).astype(BF16)

    held_score = score[group:]
    held_count = held_score.shape[0]
    row_id = jnp.bitwise_and(iota((held_count, wide), 0), NREC - 1)
    lane_id = jnp.bitwise_and(iota((held_count, wide), 1), NREC - 1)
    held_score = jnp.where(row_id == lane_id, held_score, 0.0)
    per_request = held_count // group
    spread_ids = jnp.right_shift(iota((group, held_count), 1), per_request.bit_length() - 1)
    spread_rows = jnp.where(spread_ids == iota((group, held_count), 0), 1.0, 0.0).astype(BF16)
    sel_rows = dot(sel, spread_rows).astype(BF16)
    both = jnp.concatenate(parts_of(held_score, 2), axis=1)
    given = dot(sel_rows, both)
    both = jnp.concatenate([asked, given], axis=1)
    for d in range(send_ref.shape[0]):
        to_wire(send_ref, (d,), both[d * slots : (d + 1) * slots])

    own_score = score[:group]
    lane = iota((group, extra), 1)
    own = jnp.zeros((group, extra), F32)
    for i, part in enumerate(parts_of(own_score, 3)):
        part = part.astype(F32)
        for h in range(heads):
            own = jnp.where(lane == i * heads + h, part[:, h * NREC : h * NREC + 1], own)
    own_ref[:, head_lanes : head_lanes + extra] = own.astype(BF16)


def fold_kernel(weight_ref, page_ref, fold_ref):
    parts = jnp.concatenate(parts_of(weight_ref[...], 3), axis=0)
    rows = weight_ref.shape[0]
    sums = dot(parts, page_ref[...])
    folded = sums[:rows] + sums[rows : 2 * rows] + sums[2 * rows :]
    fold_ref[...] = folded.astype(BF16)


def place_kernel(dims, pick_ref, got_ref, out_ref, rows_ref):
    slots, width, first_lane = dims
    for d in range(got_ref.shape[0]):
        rows_ref[d * slots : (d + 1) * slots, :] = from_wire(got_ref, (d,), width, first_lane, width)
    found = dot(pick_ref[...], rows_ref[...].astype(BF16)).astype(BF16)
    group = out_ref.shape[1]
    for j in range(out_ref.shape[0]):
        out_ref[j] = found[j * group : (j + 1) * group]


def attend_kernel(dims, ask_ref, valid_ref, place_ref, page_ref, fold_ref, *refs):
    send_ref = refs[-1]
    n_pages, slots, dests, heads = dims
    rows = n_pages * slots
    head_lanes = heads * HD
    extra = 2 * heads * NREC
    tokens = page_ref.shape[0]
    asks = [
        jnp.concatenate(
            [from_wire(ask_ref, (g, b), head_lanes + extra, 0, head_lanes + extra) for g in range(n_pages)],
            axis=0,
        )
        for b in range(dests)
    ]
    query = jnp.concatenate([a[:, :head_lanes] for a in asks], axis=1)
    given = jnp.concatenate([a[:, head_lanes : head_lanes + extra] for a in asks], axis=1)
    valid = valid_ref[...] > 0.5
    place = place_ref[...]
    touched = jnp.sum(place[:, :NREC].astype(F32), axis=1, keepdims=True) > 0.5
    lanes = OCTET * rows
    shift = rows.bit_length() - 1
    lane_head = jnp.right_shift(iota((HD, lanes), 1), shift)
    blank = jnp.zeros((HD, lanes), F32)
    lane = iota((lanes, lanes), 1)
    lane_in = jnp.bitwise_and(lane, extra - 1)
    lane_dest = jnp.right_shift(lane, extra.bit_length() - 1) * heads
    given_head = jnp.right_shift(jnp.bitwise_and(lane_in, heads * NREC - 1), 3) + lane_dest
    row_head = jnp.right_shift(iota((lanes, lanes), 0), shift)
    own_lane = jnp.bitwise_and(iota((rows, lanes), 1), rows - 1) == iota((rows, lanes), 0)
    goals = []
    for i in range(3):
        hit = (lane_in >= i * heads) & (lane_in < (i + 1) * heads)
        hit = hit & (row_head == lane_dest + lane_in - i * heads)
        goals.append(jnp.where(hit, 1.0, 0.0).astype(BF16))
    gathered, extras = [], []
    for o in range(STEP_HEADS // OCTET):
        heads_here = range(o * OCTET, (o + 1) * OCTET)
        asked = jnp.concatenate([query[:, h * HD : (h + 1) * HD] for h in heads_here], axis=0)
        asked = jnp.concatenate([asked, jnp.zeros((lanes, 128 - HD), F32)], axis=1).T[:HD]
        stacked = []
        for h in range(OCTET):
            stacked += [jnp.where(lane_head == h, asked, 0.0), blank]
        stacked = jnp.concatenate(stacked, axis=0).astype(BF16)
        told = jnp.concatenate([given[:, o * lanes : (o + 1) * lanes]] * OCTET, axis=0)
        told = jnp.where(given_head == row_head, told, 0.0).T.astype(BF16)
        some = slice(o * OCTET * 2 * HD, (o + 1) * OCTET * 2 * HD)
        page = jnp.concatenate([page_ref[:, some], fold_ref[:, some]], axis=0)
        scores = jnp.where(touched, dot(place, told), dot(page, stacked) * SCALE)
        scores = jnp.where(valid, scores, NEVER)
        top = jnp.max(scores, axis=0, keepdims=True)
        weights = jnp.where(valid, jnp.exp(scores - top), 0.0)
        total = jnp.sum(weights, axis=0, keepdims=True)
        safe = jnp.where(total > 0.0, total, 1.0)
        rest = jnp.zeros((256 - weights.shape[0], lanes), F32)
        weights = jnp.concatenate([weights * (1.0 / safe), rest], axis=0).T.astype(BF16)
        page = jnp.concatenate([page, jnp.zeros((rest.shape[0], page.shape[1]), BF16)], axis=0)
        for i in range(OCTET // QUAD):
            mixed = dot(
                weights[i * QUAD * rows : (i + 1) * QUAD * rows],
                page[:, i * QUAD * 2 * HD : (i + 1) * QUAD * 2 * HD],
            )
            for h in range(QUAD):
                gathered.append(mixed[h * rows : (h + 1) * rows, 2 * HD * h + HD : 2 * HD * (h + 1)])
        lse = jnp.where(own_lane, jnp.where(total > 0.0, top + jnp.log(safe), NEVER), 0.0)
        spread = jnp.zeros((rows, lanes), F32)
        for part, goal in zip(parts_of(lse, 3), goals):
            spread = spread + dot(part, goal)
        extras.append(spread)
    gathered = jnp.concatenate(gathered, axis=1)
    extras = jnp.concatenate(extras, axis=1)
    width = 2 * head_lanes
    folded = fold_ref[...].astype(F32)
    for b in range(dests):
        whole = jnp.concatenate(
            [
                gathered[:, b * head_lanes : (b + 1) * head_lanes],
                extras[:, b * extra : (b + 1) * extra],
                folded[:, b * width : (b + 1) * width],
            ],
            axis=1,
        )
        for g in range(n_pages):
            to_wire(send_ref, (g, b), whole[g * slots : (g + 1) * slots])


def merge_kernel(
    dims, got_ref, own_ref, sel_ref, back_ref, *refs
):
    group, n_dev, slots, heads, n_pages = dims
    share_refs, dense_hbm, refs = refs[:n_pages], refs[n_pages], refs[n_pages + 1 :]
    head_lanes = heads * HD
    extra = 2 * heads * NREC
    n_blk = n_dev // n_pages
    out_ref, dense_buf, rows_ref, sems = refs
    chunk = D // n_blk
    steps, _, cols = dense_buf.shape

    def dense_copy(step):
        return pltpu.make_async_copy(
            dense_hbm.at[:, pl.ds(step * cols, cols)], dense_buf.at[step], sems.at[step]
        )

    for step in range(steps):
        dense_copy(step).start()
    for d in range(n_dev):
        rows_ref[d * slots : (d + 1) * slots, :] = from_wire(
            got_ref, (d,), 3 * head_lanes + extra, 0, head_lanes + extra
        )
    rows_ref[n_dev * slots :, :] = own_ref[...].astype(F32)
    count = rows_ref.shape[0]
    parts = rows_ref[:, head_lanes : head_lanes + extra].astype(BF16)
    to, source = iota((extra, 128), 1), iota((extra, 128), 0)
    hit = None
    for i in range(3):
        one = (to < heads) & (source == to + i * heads)
        hit = one if hit is None else hit | one
    lse = dot(parts, jnp.where(hit, 1.0, 0.0).astype(BF16))
    tops = jnp.zeros((count, 128), F32)
    for r in range(group):
        mine = sel_ref[:, r : r + 1] > 0.5
        top = jnp.max(jnp.where(mine, lse, -3e38), axis=0, keepdims=True)
        tops = jnp.where(mine, top, tops)
    weights = jnp.exp(jnp.minimum(lse - tops, 0.0))
    back = back_ref[...]
    totals = jnp.zeros((group, 128), F32)
    for part in parts_of(weights, 3):
        totals = totals + dot(back, part)
    inverse = 1.0 / totals
    lanes, heads_of = iota((128, head_lanes), 1), iota((128, head_lanes), 0)
    over = lanes - heads_of * HD
    spread = jnp.where((over >= 0) & (over < HD), 1.0, 0.0).astype(BF16)
    weighted = split_dot(weights, spread, 2) * rows_ref[:, :head_lanes]
    mixed = jnp.zeros((group, head_lanes), F32)
    for part in parts_of(weighted, 2):
        mixed = mixed + dot(back, part)
    attended = (mixed * split_dot(inverse, spread, 3)).astype(BF16)
    for step in range(steps):
        dense_copy(step).wait()
        some = slice(step * cols, (step + 1) * cols)
        result = dot(attended, dense_buf[step])
        for share_ref in share_refs:
            result = result + share_ref[:, some].astype(F32)
        for i in range(cols // chunk):
            out_ref[step * (cols // chunk) + i] = result[:, i * chunk : (i + 1) * chunk].astype(BF16)


def mlp_kernel(dims, *refs):
    group, n_pages, n_blk = dims
    leaf_refs, refs = refs[:n_pages], refs[n_pages:]
    in_hbm, out_hbm, _, *refs = refs
    part_refs, (in_buf, out_buf, sems_in, sems_out) = refs[:n_pages], refs[n_pages:]
    chunk = D // n_blk
    n_steps, cols = out_buf.shape[0], out_buf.shape[2]
    core = jnp.bitwise_and(lax.axis_index("blk"), 1)

    def in_copy(step):
        return pltpu.make_async_copy(
            in_hbm.at[pl.ds(step * chunk, chunk), :], in_buf.at[step], sems_in.at[step]
        )

    def out_copy(step):
        return pltpu.make_async_copy(
            out_hbm.at[:, pl.ds(step * cols, cols)], out_buf.at[step], sems_out.at[step]
        )

    for step in range(n_blk):
        in_copy(step).start()
    for step in range(n_steps):
        out_copy(step).start()
    leaves = [ref[...].astype(F32) for ref in leaf_refs]
    half = n_blk // 2
    hidden = jnp.zeros((n_pages * group, in_buf.shape[2]), F32)
    for z in range(half):
        in_copy(2 * z).wait()
        in_copy(2 * z + 1).wait()
        for i, c in ((z, 2 * z + core), (half + z, 2 * z + 1 - core)):
            rows = [leaf[i * group : (i + 1) * group] for leaf in leaves]
            hidden = hidden + dot(jnp.concatenate(rows, axis=0).astype(BF16), in_buf[c])
    active = (0.5 * hidden * (1.0 + lax.erf(hidden * math.sqrt(0.5)))).astype(BF16)
    for step in range(n_steps):
        out_copy(step).wait()
        result = dot(active, out_buf[step]).astype(BF16)
        for g in range(n_pages):
            part_refs[g][:, step * cols : (step + 1) * cols] = result[g * group : (g + 1) * group]


VMEM = pl.BlockSpec(memory_space=pltpu.VMEM)
HBM = pl.BlockSpec(memory_space=pltpu.HBM)
ANY = pl.BlockSpec(memory_space=pl.ANY)


def shape_of(shape, kind=BF16):
    return jax.ShapeDtypeStruct(shape, kind)


def params_of(mib):
    return pltpu.CompilerParams(vmem_limit_bytes=mib * MIB)


def cost_of(flops, nbytes):
    return pl.CostEstimate(flops=int(flops), bytes_accessed=int(nbytes), transcendentals=0)


def on_device(
    new_hidden,
    attn_gain,
    mlp_gain,
    qkv_weight,
    dense_weight,
    in_weight,
    out_weight,
    page_store,
    held_states,
    fold_weights,
    page_table,
    lengths,
    keep_slots,
    fold_index,
    recompute_list,
):
    n_pages = lax.axis_size("pages")
    n_blk = lax.axis_size("blk")
    n_dev = n_pages * n_blk
    mine = lax.axis_index("pages")
    device = lax.axis_index(("pages", "blk"))
    group = lengths.shape[0]
    pages_dev = page_store.shape[0]
    slots = -(-(pages_dev // n_pages) // 4) * 4
    ranks = n_pages * slots
    heads = H // n_blk
    head_lanes = heads * HD
    extra = 2 * heads * NREC
    lanes = head_lanes + extra
    chunk = D // n_blk
    held_rows = held_states.shape[0] * NREC
    kept_count = KP * PAGE

    def swapped(array, axis, size, by):
        return lax.ppermute(array, axis, [(i, i ^ by) for i in range(size)])

    def swapped(array, axis, size, by):
        return lax.ppermute(array, axis, [(i, i ^ by) for i in range(size)])

    def fixed(array):
        return pltpu.with_memory_space_constraint(array, pltpu.HBM)

    half = n_blk // 2
    pack = pl.pallas_call(
        pack_kernel,
        in_specs=[VMEM] * 3,
        out_specs=VMEM,
        out_shape=shape_of((half, n_blk * held_rows + group, chunk)),
        compiler_params=params_of(16),
        name="pack",
    )(fixed(held_states.reshape(held_rows, D)), fixed(new_hidden), fixed(attn_gain[None]))
    pack = lax.all_to_all(
        pack,
        "blk",
        0,
        0,
        axis_index_groups=[list(range(core, n_blk, 2)) for core in range(2)],
        tiled=True,
    )
    packs = [pack, swapped(pack, "blk", n_blk, 1)]

    n_rows = n_dev * slots
    rows = group * (1 + NREC)
    period = 12 * HD if (3 * head_lanes) % (12 * HD) == 0 else 3 * head_lanes
    lane = np.arange(HD)
    frequency = np.where(lane < ROT, ROT_BASE ** (-2.0 * (lane % (ROT // 2)) / ROT), 0.0).astype(np.float32)
    cosine, low, high, sel, sel_all, back, pick, numbers = pl.pallas_call(
        functools.partial(prep_kernel, (n_pages, pages_dev, slots, period // (3 * HD))),
        in_specs=[pl.BlockSpec(memory_space=pltpu.SMEM)] + [VMEM] * 6,
        out_specs=[VMEM] * 8,
        out_shape=[
            *[shape_of((rows, period), F32)] * 3,
            shape_of((n_rows, group)),
            shape_of((n_rows + group, group), F32),
            shape_of((group, n_rows + group)),
            shape_of((PPR * group, n_rows)),
            shape_of((group, 1 + KP + PPR + NREC), jnp.int32),
        ],
        compiler_params=params_of(16),
        cost_estimate=cost_of(0, 0),
        name="prep",
    )(
        page_table.T,
        fixed(page_table.T),
        fixed(lengths[None]),
        fixed(keep_slots),
        fixed(fold_index),
        fixed(recompute_list),
        fixed(jnp.asarray(frequency[None])),
    )

    numbers = [numbers] + [swapped(numbers, "pages", n_pages, i) for i in range(1, n_pages)]

    tokens = pages_dev * PAGE
    pages = page_store.reshape(tokens, 2 * D)
    steps = H // STEP_HEADS
    step_lanes = STEP_HEADS * 2 * HD
    dests = STEP_HEADS // heads
    fold_width = 2 * head_lanes

    wire = lanes + wire_split(lanes)
    send, own, leaf = pl.pallas_call(
        functools.partial(project_kernel, (group, n_blk, held_rows, heads, slots)),
        in_specs=[VMEM] * 4 + [HBM] + [VMEM] * 4,
        out_specs=[VMEM] * 3,
        out_shape=[
            shape_of((n_dev, 2, wire)),
            shape_of((group, lanes)),
            shape_of((n_blk * group, chunk)),
        ],
        scratch_shapes=[
            pltpu.VMEM((3 * head_lanes // period, n_blk, chunk, period), BF16),
            pltpu.VMEM((n_blk, rows, chunk), F32),
            pltpu.VMEM((rows, period), F32),
            pltpu.SemaphoreType.DMA((3 * head_lanes // period, n_blk)),
        ],
        compiler_params=params_of(50),
        cost_estimate=cost_of(2 * rows * D * 3 * head_lanes, 6 * D * head_lanes),
        name="project",
    )(
        *packs,
        fixed(attn_gain[None]),
        fixed(mlp_gain[None]),
        fixed(qkv_weight),
        cosine,
        low,
        high,
        sel,
    )
    send, *numbers = lax.optimization_barrier((send, *numbers))
    asked = lax.all_to_all(send, ("pages", "blk"), 0, 0, tiled=True)
    fold_rows, valid, renew = pl.pallas_call(
        functools.partial(facts_kernel, (n_pages, pages_dev, slots)),
        in_specs=[VMEM] * (n_pages + 2),
        out_specs=[VMEM] * 3,
        out_shape=[
            shape_of((ranks, tokens), F32),
            shape_of((tokens + ranks, OCTET * ranks), F32),
            shape_of((tokens + ranks, 2 * OCTET * NREC)),
        ],
        compiler_params=params_of(16),
        cost_estimate=cost_of(0, 0),
        name="facts",
    )(*numbers, fixed(page_table.T), fixed(fold_weights))

    leaf, fold_rows = lax.optimization_barrier((leaf, fold_rows))
    leaves = [leaf] + [swapped(leaf, "pages", n_pages, i) for i in range(1, n_pages)]

    folded_rows = pl.pallas_call(
        fold_kernel,
        grid=(steps,),
        in_specs=[
            pl.BlockSpec((ranks, tokens), lambda i: (0, 0)),
            pl.BlockSpec((tokens, step_lanes), lambda i: (0, i)),
        ],
        out_specs=pl.BlockSpec((ranks, step_lanes), lambda i: (0, i)),
        out_shape=shape_of((ranks, 2 * D)),
        compiler_params=params_of(16),
        cost_estimate=cost_of(0, 0),
        name="fold",
    )(fold_rows, fixed(pages))

    all_lanes = lanes + fold_width
    all_wire = all_lanes + wire_split(all_lanes)
    partial = pl.pallas_call(
        functools.partial(attend_kernel, (n_pages, slots, dests, heads)),
        grid=(steps,),
        in_specs=[
            pl.BlockSpec((n_pages, dests, 2, wire), lambda i: (0, i, 0, 0)),
            pl.BlockSpec((tokens + ranks, OCTET * ranks), lambda i: (0, 0)),
            pl.BlockSpec((tokens + ranks, 2 * OCTET * NREC), lambda i: (0, 0)),
            pl.BlockSpec((tokens, step_lanes), lambda i: (0, i)),
            pl.BlockSpec((ranks, step_lanes), lambda i: (0, i)),
        ],
        out_specs=pl.BlockSpec((n_pages, dests, 2, all_wire), lambda i: (0, i, 0, 0)),
        out_shape=shape_of((n_pages, n_blk, 2, all_wire)),
        compiler_params=params_of(16),
        cost_estimate=cost_of(2 * 128 * tokens * 2 * D, tokens * 4 * D),
        name="attend",
    )(asked.reshape(n_pages, n_blk, 2, wire), valid, renew, fixed(pages), folded_rows)
    partial, *leaves = lax.optimization_barrier((partial, *leaves))
    got = lax.all_to_all(partial.reshape(n_dev, 2, all_wire), ("pages", "blk"), 0, 0, tiled=True)

    hidden = in_weight.shape[1]
    mlp_parts = pl.pallas_call(
        functools.partial(mlp_kernel, (group, n_pages, n_blk)),
        in_specs=[VMEM] * n_pages + [HBM, HBM, ANY],
        out_specs=[VMEM] * n_pages,
        out_shape=[shape_of((group, D))] * n_pages,
        scratch_shapes=[
            pltpu.VMEM((n_blk, chunk, hidden), BF16),
            pltpu.VMEM((8, hidden, D // 8), BF16),
            pltpu.SemaphoreType.DMA((n_blk,)),
            pltpu.SemaphoreType.DMA((8,)),
        ],
        compiler_params=params_of(24),
        cost_estimate=cost_of(4 * n_pages * group * D * hidden, 4 * D * hidden),
        name="mlp",
    )(*leaves, fixed(in_weight), fixed(out_weight), partial)
    mlp_share = [mlp_parts[0]] + [swapped(mlp_parts[i], "pages", n_pages, i) for i in range(1, n_pages)]

    out_part = pl.pallas_call(
        functools.partial(merge_kernel, (group, n_dev, slots, heads, n_pages)),
        in_specs=[VMEM] * (n_pages + 4) + [HBM],
        out_specs=VMEM,
        out_shape=shape_of((n_blk, group, chunk)),
        scratch_shapes=[
            pltpu.VMEM((8, head_lanes, D // 8), BF16),
            pltpu.VMEM((n_rows + group, lanes), F32),
            pltpu.SemaphoreType.DMA((8,)),
        ],
        compiler_params=params_of(24),
        cost_estimate=cost_of(2 * group * D * head_lanes, 2 * D * head_lanes),
        name="merge",
    )(
        got,
        own,
        sel_all,
        back,
        *mlp_share,
        fixed(dense_weight),
    )
    out_got = lax.all_to_all(out_part, "blk", 0, 0, tiled=True)
    summed = jnp.sum(out_got.astype(F32), axis=0).astype(BF16)

    folded = pl.pallas_call(
        functools.partial(place_kernel, (slots, all_lanes, lanes)),
        in_specs=[VMEM, VMEM],
        out_specs=VMEM,
        out_shape=shape_of((PPR, group, fold_width)),
        scratch_shapes=[pltpu.VMEM((n_rows, fold_width), F32)],
        compiler_params=params_of(16),
        cost_estimate=cost_of(0, 4 * n_rows * fold_width),
        name="place",
    )(pick, got)
    folded = jnp.transpose(folded, (1, 0, 2))
    return (summed, folded)


def solution(mesh):
    in_specs = (
        P("pages", "blk"),
        P(),
        P(),
        P(None, "blk"),
        P("blk", None),
        P(None, ("pages", "blk")),
        P(("pages", "blk"), None),
        P(("pages", "blk"), None, None),
        P(("pages", "blk"), None, None),
        P(),
        P(),
        P("pages"),
        P("pages", None),
        P("pages", None),
        P("pages", None),
    )
    out_specs = (P("pages", "blk"), P("pages", None, "blk"))
    return jax.shard_map(
        on_device, mesh=mesh, in_specs=in_specs, out_specs=out_specs, check_vma=False
    )
```

```python
import functools
import math

import jax
import jax.numpy as jnp
import numpy as np
from jax import lax
from jax.experimental import pallas as pl
from jax.experimental.pallas import tpu as pltpu
from jax.sharding import PartitionSpec as P

D = 6144
H = 64
HD = 96
ROT = 24
PAGE = 16
PPR = 12
KP = 5
NREC = 8
NF = 8
FF = 24576

EPSILON = 1e-05
ROT_BASE = 10000.0
NEVER = -1e30
F32 = jnp.float32
BF16 = jnp.bfloat16
SCALE = 1.0 / math.sqrt(HD)
MIB = 1024 * 1024
STEP_HEADS = 32
QUAD = 4
OCTET = 8


def iota(shape, axis):
    return lax.broadcasted_iota(jnp.int32, shape, axis)


def dot(left, right):
    return jnp.dot(left, right, preferred_element_type=F32)


def dot_nt(left, right):
    return lax.dot_general(left, right, (((1,), (1,)), ((), ())), preferred_element_type=F32)


def dot_tn(left, right):
    return lax.dot_general(left, right, (((0,), (0,)), ((), ())), preferred_element_type=F32)


def parts_of(values, count):
    parts = []
    for _ in range(count):
        part = values.astype(BF16)
        parts.append(part)
        values = values - part.astype(F32)
    return parts


def split_dot(values, selector, count):
    total = None
    for part in parts_of(values, count):
        term = dot(part, selector)
        total = term if total is None else total + term
    return total


def wire_split(width):
    return (width // 128 + 1) // 2 * 128 if width % 128 == 0 else (width + 1) // 2


def to_wire(ref, index, rows):
    width = rows.shape[1]
    first = wire_split(width)
    ref[(*index, slice(None), slice(0, width))] = rows[:2].astype(BF16)
    rest = rows[2:3, first:]
    if width < 2 * first:
        rest = jnp.concatenate([rest, jnp.zeros((1, 2 * first - width), F32)], axis=1)
    tail = jnp.concatenate([rows[2:3, :first], rest], axis=0)
    ref[(*index, slice(None), slice(width, width + first))] = tail.astype(BF16)


def from_wire(ref, index, width, start, stop):
    first = wire_split(width)
    pair = ref[(*index, slice(None), slice(start, stop))].astype(F32)
    third = []
    if start < first:
        third.append(ref[(*index, slice(0, 1), slice(width + start, width + min(stop, first)))].astype(F32))
    if stop > first:
        begin = max(start, first) - first
        third.append(ref[(*index, slice(1, 2), slice(width + begin, width + stop - first))].astype(F32))
    third = third[0] if len(third) == 1 else jnp.concatenate(third, axis=1)
    return jnp.concatenate([pair, third, jnp.zeros_like(third)], axis=0)


def prep_kernel(dims, table_smem, table_ref, length_ref, keep_ref, choice_ref, list_ref, frequency_ref, *refs):
    n_pages, pages_dev, slots, period_heads = dims
    attn_gain_ref, mlp_gain_ref, *refs = refs
    gain_ref, cos_ref, low_ref, high_ref, sel_ref, sel_all_ref, back_ref, pick_ref, number_ref = refs
    gain_ref[0:1, :] = attn_gain_ref[...]
    gain_ref[1:2, :] = mlp_gain_ref[...]
    group = keep_ref.shape[0]
    n_rows = sel_ref.shape[0]
    mine = lax.axis_index("pages")

    ids = table_ref[:, :group]
    for g in range(1, n_pages):
        ids = jnp.where(mine == g, table_ref[:, g * group : (g + 1) * group], ids)
    holder = jnp.floor((ids.astype(F32) + 0.5) * (1.0 / pages_dev)).astype(jnp.int32)

    def one_request(r, rank):
        for j in range(PPR):
            other = table_smem[j, mine * group + r]
            earlier = (holder == lax.div(other, jnp.int32(pages_dev))) & (ids > other)
            rank = rank + jnp.where(earlier, 1, 0)
        return rank

    row = holder * slots + lax.fori_loop(0, group, one_request, jnp.zeros_like(ids))
    at = iota((n_rows, group), 0)
    hit = None
    for j in range(PPR):
        one = at == row[j : j + 1, :]
        hit = one if hit is None else hit | one
    hit = jnp.where(hit, 1.0, 0.0)
    same = jnp.where(iota((group, group), 0) == iota((group, group), 1), 1.0, 0.0)
    sel_ref[...] = hit.astype(BF16)
    sel_all_ref[:n_rows, :] = hit
    sel_all_ref[n_rows:, :] = same
    turned = row.astype(F32).T
    at = iota((group, n_rows), 1).astype(F32)
    back = jnp.zeros((group, n_rows), F32)
    for j in range(PPR):
        one = jnp.where(at == turned[:, j : j + 1], 1.0, 0.0)
        pick_ref[j * group : (j + 1) * group, :] = one.astype(BF16)
        back = back + one
    back_ref[:, :n_rows] = back.astype(BF16)
    back_ref[:, n_rows:] = same.astype(BF16)

    length = jnp.sum(same * length_ref[...].astype(F32), axis=1, keepdims=True)
    renewed = list_ref[...]
    slot = jnp.zeros_like(renewed)
    for k in range(KP):
        slot = jnp.where(jnp.right_shift(renewed, 4) == k, keep_ref[:, k : k + 1], slot)
    place = (slot * PAGE + jnp.bitwise_and(renewed, PAGE - 1)).astype(F32)
    place = jnp.broadcast_to(place[:, None, :], (group, NREC, NREC)).reshape(group * NREC, NREC)
    shape = (group * NREC, NREC)
    place = jnp.where(jnp.bitwise_and(iota(shape, 0), NREC - 1) == iota(shape, 1), place, 0.0)
    place = jnp.concatenate([length, jnp.sum(place, axis=1, keepdims=True)], axis=0)
    angle = place * frequency_ref[...]
    cosine, sine = jnp.cos(angle), jnp.sin(angle)
    lane = iota(angle.shape, 1)
    low = jnp.where(lane < ROT // 2, -sine, 0.0)
    high = jnp.where((lane >= ROT // 2) & (lane < ROT), sine, 0.0)
    one, none = jnp.ones_like(angle), jnp.zeros_like(angle)
    cos_ref[...] = jnp.concatenate([cosine, cosine, one] * period_heads, axis=1)
    low_ref[...] = jnp.concatenate([low, low, none] * period_heads, axis=1)
    high_ref[...] = jnp.concatenate([high, high, none] * period_heads, axis=1)
    numbers = [length.astype(jnp.int32), keep_ref[...], choice_ref[...], renewed]
    number_ref[...] = jnp.concatenate(numbers, axis=1)


def facts_kernel(dims, *refs):
    n_pages, pages_dev, slots = dims
    number_refs, (table_ref, fold_ref, weight_ref, valid_ref, renew_ref) = refs[:n_pages], refs[n_pages:]
    group = number_refs[0].shape[0]
    requests = n_pages * group
    ranks = n_pages * slots
    mine = lax.axis_index("pages")
    device = lax.axis_index(("pages", "blk"))
    numbers = []
    for g in range(n_pages):
        got = number_refs[0][...]
        for i in range(1, n_pages):
            got = jnp.where(jnp.bitwise_xor(mine, g) == i, number_refs[i][...], got)
        numbers.append(got.astype(F32))
    numbers = jnp.concatenate(numbers, axis=0).astype(BF16)

    local = iota((ranks, requests), 0)
    hits = jnp.zeros((ranks, requests), F32)
    slot = jnp.zeros((ranks, 1), F32)
    for j in range(PPR):
        one = jnp.where(local == table_ref[j : j + 1, :] - device * pages_dev, 1.0, 0.0)
        hits = hits + one
        slot = slot + j * jnp.sum(one, axis=1, keepdims=True)
    hits = jnp.where(local < pages_dev, hits, 0.0)
    facts = dot(hits.astype(BF16), numbers)
    length, keeps = facts[:, :1], facts[:, 1 : 1 + KP]
    choices, renewed = facts[:, 1 + KP : 1 + KP + PPR], facts[:, 1 + KP + PPR : 1 + KP + PPR + NREC]
    place = iota((ranks, PPR), 1).astype(F32)
    choice = jnp.sum(jnp.where(place == slot, choices, 0.0), axis=1, keepdims=True)
    found = jnp.sum(hits, axis=1, keepdims=True) > 0.5
    kept_hit = jnp.where(keeps == slot, 1.0, 0.0)
    kept = (jnp.sum(kept_hit, axis=1, keepdims=True) > 0.5) & found
    kept_place = PAGE * jnp.sum(kept_hit * iota((ranks, KP), 1).astype(F32), axis=1, keepdims=True)
    dropped = jnp.logical_not(kept) & found & (slot * PAGE < length)

    owner = jnp.concatenate(
        [jnp.sum(hits[:, g * group : (g + 1) * group], axis=1, keepdims=True) for g in range(n_pages)], axis=1
    )
    below = jnp.where(iota((ranks, ranks), 0) > iota((ranks, ranks), 1), 1.0, 0.0).astype(BF16)
    before = dot(below, owner.astype(BF16))
    rank = jnp.sum(owner * (before + slots * iota((ranks, n_pages), 1).astype(F32)), axis=1, keepdims=True)
    rank = jnp.where(found, rank, -1.0)
    rank_hit = jnp.where(rank == iota((ranks, ranks), 1).astype(F32), 1.0, 0.0).astype(BF16)

    weights = jnp.zeros((ranks, PAGE), F32)
    for f in range(NF):
        weights = jnp.where(choice == f, fold_ref[f : f + 1, :], weights)
    live = slot * PAGE + iota((ranks, PAGE), 1).astype(F32) < length
    weights = jnp.where(live & dropped, weights, 0.0)
    weights = jnp.concatenate([weights] * pages_dev, axis=1)
    tokens = pages_dev * PAGE
    own = jnp.right_shift(iota((ranks, tokens), 1), 4) == iota((ranks, tokens), 0)
    weights = jnp.where(own, weights, 0.0)
    total = jnp.zeros((ranks, tokens), F32)
    for part in parts_of(weights, 3):
        total = total + dot_tn(rank_hit, part)
    weight_ref[...] = total

    lanes = valid_ref.shape[1]
    lane_rank = jnp.bitwise_and(iota((ranks, lanes), 1), ranks - 1).astype(F32)
    for_rank = jnp.where(lane_rank == rank, 1.0, 0.0)
    kept_for = jnp.where(kept, for_rank, 0.0)
    dropped_for = jnp.where(dropped, for_rank, 0.0)
    renewed = jnp.concatenate([renewed] * (renew_ref.shape[1] // NREC), axis=1)
    renewed = jnp.where(kept, renewed - kept_place, -1.0)
    inside = iota((PAGE, renew_ref.shape[1]), 0).astype(F32)
    for p in range(pages_dev):
        some = slice(p * PAGE, (p + 1) * PAGE)
        valid_ref[some, :] = jnp.broadcast_to(kept_for[p : p + 1, :], (PAGE, lanes))
        renew_ref[some, :] = jnp.where(inside == renewed[p : p + 1, :], 1.0, 0.0).astype(BF16)
    valid_ref[tokens:, :] = dot_tn(rank_hit, dropped_for.astype(BF16))
    renew_ref[tokens:, :] = jnp.zeros((ranks, renew_ref.shape[1]), BF16)


def pack_kernel(held_ref, new_ref, gain_ref, out_ref):
    group, chunk = new_ref.shape
    held = held_ref[...].astype(F32)
    held = held - jnp.sum(held, axis=1, keepdims=True) / D
    spread = jnp.sum(held * held, axis=1, keepdims=True) / D
    held = held * lax.rsqrt(spread + EPSILON) * gain_ref[...]
    rows = [held[:, c * chunk : (c + 1) * chunk] for c in range(D // chunk)] + [new_ref[...].astype(F32)]
    rows = jnp.concatenate(rows, axis=0).astype(BF16)
    for i in range(out_ref.shape[0]):
        out_ref[i] = rows


def load_kernel(weight_hbm, _, buf_ref, loaded_ref, sems):
    rows, lanes = buf_ref.shape
    count = sems.shape[0]
    rows = rows // count

    def copy(step):
        some = pl.ds(step * rows, rows)
        return pltpu.make_async_copy(weight_hbm.at[some, pl.ds(0, lanes)], buf_ref.at[some, :], sems.at[step])

    for step in range(count):
        copy(step).start()
    loaded_ref[...] = jnp.zeros_like(loaded_ref)
    for step in range(count):
        copy(step).wait()


def project_kernel(dims, *refs):
    group, n_blk, held_rows, heads, slots = dims
    pack_refs, refs = refs[:2], refs[2:]
    gain_ref, weight_ref, weight_hbm, cos_ref, low_ref, high_ref, sel_ref, *refs = refs
    _, send_ref, own_ref, leaf_ref, weight_buf, rows_ref, acc_ref, sems = refs
    chunk = D // n_blk
    width = 3 * heads * HD
    head_lanes = heads * HD
    extra = 2 * heads * NREC
    period = cos_ref.shape[1]
    period_heads = period // (3 * HD)
    core = jnp.bitwise_and(lax.axis_index("blk"), 1)

    def weight_copy(part, step):
        return pltpu.make_async_copy(
            weight_hbm.at[pl.ds(step * chunk, chunk), pl.ds(part * period, period)],
            weight_buf.at[part - 1, step],
            sems.at[part - 1, step],
        )

    for part in range(1, width // period):
        for step in range(n_blk):
            weight_copy(part, step).start()

    pieces, places = [], []
    for other in range(2):
        for z in range(n_blk // 2):
            b = 2 * z + jnp.bitwise_xor(core, other)
            values = pack_refs[other][z].astype(F32)
            pieces.append(values[n_blk * held_rows :])
            places.append(b)
            first = pl.multiple_of(group + b * held_rows, 8)
            for c in range(n_blk):
                rows_ref[c, pl.ds(first, held_rows), :] = values[c * held_rows : (c + 1) * held_rows]
    mean = sum(jnp.sum(piece, axis=1, keepdims=True) for piece in pieces) / D
    pieces = [piece - mean for piece in pieces]
    spread = sum(jnp.sum(piece * piece, axis=1, keepdims=True) for piece in pieces) / D
    spread = lax.rsqrt(spread + EPSILON)
    leaves = []
    for i, (b, piece) in enumerate(zip(places, pieces)):
        z = i % (n_blk // 2)
        some = slice(2 * z * chunk, 2 * (z + 1) * chunk)
        gain = gain_ref[:, some]
        gain = jnp.where(b == 2 * z, gain[:, :chunk], gain[:, chunk:])
        piece = piece * spread
        rows_ref[b, 0:group, :] = piece * gain[0:1]
        leaves.append(piece * gain[1:2])
    leaf_ref[...] = jnp.concatenate(leaves, axis=0).astype(BF16)

    rows = acc_ref.shape[0]
    wide = heads * NREC
    score = jnp.zeros((rows, wide), F32)
    head_at = jnp.right_shift(iota((rows, wide), 1), 3)
    queries, values = [], []
    for j in range(width // period):
        acc_ref[...] = jnp.zeros_like(acc_ref)

        def one_chunk(step, carry, j=j):
            if j == 0:
                weight = weight_ref[pl.ds(pl.multiple_of(step * chunk, 16), chunk), :]
            else:
                weight_copy(j, step).wait()
                weight = weight_buf[j - 1, step]
            acc_ref[...] += dot(rows_ref[step].astype(BF16), weight)
            return carry

        lax.fori_loop(0, n_blk, one_chunk, 0)
        block = acc_ref[...]
        up = jnp.concatenate([block[:, ROT // 2 :], block[:, : ROT // 2]], axis=1)
        down = jnp.concatenate([block[:, -ROT // 2 :], block[:, : -ROT // 2]], axis=1)
        turned = block * cos_ref[...] + up * low_ref[...] + down * high_ref[...]
        turned = turned.astype(BF16).astype(F32)
        for h in range(period_heads):
            first = h * 3 * HD
            query = turned[:group, first : first + HD]
            key = turned[:, first + HD : first + 2 * HD]
            queries.append(query)
            values.append(turned[:group, first + 2 * HD : first + 3 * HD])
            own_product = key[:group] * query
            held_product = key[group:].reshape(group, -1, HD) * query[:, None, :]
            product = jnp.concatenate([own_product, held_product.reshape(rows - group, HD)], axis=0)
            score = jnp.where(
                head_at == j * period_heads + h, jnp.sum(product, axis=1, keepdims=True), score
            )
    score = score * SCALE
    sel = sel_ref[...]
    asked = dot(sel, jnp.concatenate(queries, axis=1).astype(BF16))
    own_ref[:, :head_lanes] = jnp.concatenate(values, axis=1).astype(BF16)

    held_score = score[group:]
    held_count = held_score.shape[0]
    row_id = jnp.bitwise_and(iota((held_count, wide), 0), NREC - 1)
    lane_id = jnp.bitwise_and(iota((held_count, wide), 1), NREC - 1)
    held_score = jnp.where(row_id == lane_id, held_score, 0.0)
    per_request = held_count // group
    spread_ids = jnp.right_shift(iota((group, held_count), 1), per_request.bit_length() - 1)
    spread_rows = jnp.where(spread_ids == iota((group, held_count), 0), 1.0, 0.0).astype(BF16)
    sel_rows = dot(sel, spread_rows).astype(BF16)
    both = jnp.concatenate(parts_of(held_score, 2), axis=1)
    given = dot(sel_rows, both)
    both = jnp.concatenate([asked, given], axis=1)
    for d in range(send_ref.shape[0]):
        to_wire(send_ref, (d,), both[d * slots : (d + 1) * slots])

    own_score = score[:group]
    lane = iota((group, extra), 1)
    own = jnp.zeros((group, extra), F32)
    for i, part in enumerate(parts_of(own_score, 3)):
        part = part.astype(F32)
        for h in range(heads):
            own = jnp.where(lane == i * heads + h, part[:, h * NREC : h * NREC + 1], own)
    own_ref[:, head_lanes : head_lanes + extra] = own.astype(BF16)


def fold_kernel(weight_ref, page_ref, fold_ref):
    parts = jnp.concatenate(parts_of(weight_ref[...], 3), axis=0)
    rows = weight_ref.shape[0]
    sums = dot(parts, page_ref[...])
    folded = sums[:rows] + sums[rows : 2 * rows] + sums[2 * rows :]
    fold_ref[...] = folded.astype(BF16)


def place_kernel(dims, pick_ref, got_ref, out_ref, rows_ref):
    slots, width, first_lane = dims
    for d in range(got_ref.shape[0]):
        rows_ref[d * slots : (d + 1) * slots, :] = from_wire(got_ref, (d,), width, first_lane, width)
    found = dot(pick_ref[...], rows_ref[...].astype(BF16)).astype(BF16)
    group = out_ref.shape[1]
    for j in range(out_ref.shape[0]):
        out_ref[j] = found[j * group : (j + 1) * group]


def attend_kernel(dims, ask_ref, valid_ref, place_ref, page_ref, fold_ref, *refs):
    send_ref = refs[-1]
    n_pages, slots, dests, heads = dims
    rows = n_pages * slots
    head_lanes = heads * HD
    extra = 2 * heads * NREC
    tokens = page_ref.shape[0]
    asks = [
        jnp.concatenate(
            [from_wire(ask_ref, (g, b), head_lanes + extra, 0, head_lanes + extra) for g in range(n_pages)],
            axis=0,
        )
        for b in range(dests)
    ]
    query = jnp.concatenate([a[:, :head_lanes] for a in asks], axis=1)
    given = jnp.concatenate([a[:, head_lanes : head_lanes + extra] for a in asks], axis=1)
    valid = valid_ref[...] > 0.5
    place = place_ref[...]
    touched = jnp.sum(place[:, :NREC].astype(F32), axis=1, keepdims=True) > 0.5
    lanes = OCTET * rows
    shift = rows.bit_length() - 1
    lane_head = jnp.right_shift(iota((HD, lanes), 1), shift)
    blank = jnp.zeros((HD, lanes), F32)
    lane = iota((lanes, lanes), 1)
    lane_in = jnp.bitwise_and(lane, extra - 1)
    lane_dest = jnp.right_shift(lane, extra.bit_length() - 1) * heads
    given_head = jnp.right_shift(jnp.bitwise_and(lane_in, heads * NREC - 1), 3) + lane_dest
    row_head = jnp.right_shift(iota((lanes, lanes), 0), shift)
    own_lane = jnp.bitwise_and(iota((rows, lanes), 1), rows - 1) == iota((rows, lanes), 0)
    goals = []
    for i in range(3):
        hit = (lane_in >= i * heads) & (lane_in < (i + 1) * heads)
        hit = hit & (row_head == lane_dest + lane_in - i * heads)
        goals.append(jnp.where(hit, 1.0, 0.0).astype(BF16))
    gathered, extras = [], []
    for o in range(STEP_HEADS // OCTET):
        heads_here = range(o * OCTET, (o + 1) * OCTET)
        asked = jnp.concatenate([query[:, h * HD : (h + 1) * HD] for h in heads_here], axis=0)
        asked = jnp.concatenate([asked, jnp.zeros((lanes, 128 - HD), F32)], axis=1).T[:HD]
        stacked = []
        for h in range(OCTET):
            stacked += [jnp.where(lane_head == h, asked, 0.0), blank]
        stacked = jnp.concatenate(stacked, axis=0).astype(BF16)
        told = jnp.concatenate([given[:, o * lanes : (o + 1) * lanes]] * OCTET, axis=0)
        told = jnp.where(given_head == row_head, told, 0.0).T.astype(BF16)
        some = slice(o * OCTET * 2 * HD, (o + 1) * OCTET * 2 * HD)
        page = jnp.concatenate([page_ref[:, some], fold_ref[:, some]], axis=0)
        scores = jnp.where(touched, dot(place, told), dot(page, stacked) * SCALE)
        scores = jnp.where(valid, scores, NEVER)
        top = jnp.max(scores, axis=0, keepdims=True)
        weights = jnp.where(valid, jnp.exp(scores - top), 0.0)
        total = jnp.sum(weights, axis=0, keepdims=True)
        safe = jnp.where(total > 0.0, total, 1.0)
        rest = jnp.zeros((256 - weights.shape[0], lanes), F32)
        weights = jnp.concatenate([weights * (1.0 / safe), rest], axis=0).T.astype(BF16)
        page = jnp.concatenate([page, jnp.zeros((rest.shape[0], page.shape[1]), BF16)], axis=0)
        for i in range(OCTET // QUAD):
            mixed = dot(
                weights[i * QUAD * rows : (i + 1) * QUAD * rows],
                page[:, i * QUAD * 2 * HD : (i + 1) * QUAD * 2 * HD],
            )
            for h in range(QUAD):
                gathered.append(mixed[h * rows : (h + 1) * rows, 2 * HD * h + HD : 2 * HD * (h + 1)])
        lse = jnp.where(own_lane, jnp.where(total > 0.0, top + jnp.log(safe), NEVER), 0.0)
        spread = jnp.zeros((rows, lanes), F32)
        for part, goal in zip(parts_of(lse, 3), goals):
            spread = spread + dot(part, goal)
        extras.append(spread)
    gathered = jnp.concatenate(gathered, axis=1)
    extras = jnp.concatenate(extras, axis=1)
    width = 2 * head_lanes
    folded = fold_ref[...].astype(F32)
    for b in range(dests):
        whole = jnp.concatenate(
            [
                gathered[:, b * head_lanes : (b + 1) * head_lanes],
                extras[:, b * extra : (b + 1) * extra],
                folded[:, b * width : (b + 1) * width],
            ],
            axis=1,
        )
        for g in range(n_pages):
            to_wire(send_ref, (g, b), whole[g * slots : (g + 1) * slots])


def merge_kernel(
    dims, got_ref, own_ref, sel_ref, back_ref, *refs
):
    group, n_dev, slots, heads, n_pages = dims
    share_refs, dense_hbm, refs = refs[:n_pages], refs[n_pages], refs[n_pages + 1 :]
    head_lanes = heads * HD
    extra = 2 * heads * NREC
    n_blk = n_dev // n_pages
    out_ref, dense_buf, rows_ref, sems = refs
    chunk = D // n_blk
    steps, _, cols = dense_buf.shape

    def dense_copy(step):
        return pltpu.make_async_copy(
            dense_hbm.at[:, pl.ds(step * cols, cols)], dense_buf.at[step], sems.at[step]
        )

    for step in range(steps):
        dense_copy(step).start()
    for d in range(n_dev):
        rows_ref[d * slots : (d + 1) * slots, :] = from_wire(
            got_ref, (d,), 3 * head_lanes + extra, 0, head_lanes + extra
        )
    rows_ref[n_dev * slots :, :] = own_ref[...].astype(F32)
    count = rows_ref.shape[0]
    parts = rows_ref[:, head_lanes : head_lanes + extra].astype(BF16)
    to, source = iota((extra, 128), 1), iota((extra, 128), 0)
    hit = None
    for i in range(3):
        one = (to < heads) & (source == to + i * heads)
        hit = one if hit is None else hit | one
    lse = dot(parts, jnp.where(hit, 1.0, 0.0).astype(BF16))
    tops = jnp.zeros((count, 128), F32)
    for r in range(group):
        mine = sel_ref[:, r : r + 1] > 0.5
        top = jnp.max(jnp.where(mine, lse, -3e38), axis=0, keepdims=True)
        tops = jnp.where(mine, top, tops)
    weights = jnp.exp(jnp.minimum(lse - tops, 0.0))
    back = back_ref[...]
    totals = jnp.zeros((group, 128), F32)
    for part in parts_of(weights, 3):
        totals = totals + dot(back, part)
    inverse = 1.0 / totals
    lanes, heads_of = iota((128, head_lanes), 1), iota((128, head_lanes), 0)
    over = lanes - heads_of * HD
    spread = jnp.where((over >= 0) & (over < HD), 1.0, 0.0).astype(BF16)
    weighted = split_dot(weights, spread, 2) * rows_ref[:, :head_lanes]
    mixed = jnp.zeros((group, head_lanes), F32)
    for part in parts_of(weighted, 2):
        mixed = mixed + dot(back, part)
    attended = (mixed * split_dot(inverse, spread, 3)).astype(BF16)
    for step in range(steps):
        dense_copy(step).wait()
        some = slice(step * cols, (step + 1) * cols)
        result = dot(attended, dense_buf[step])
        for share_ref in share_refs:
            result = result + share_ref[:, some].astype(F32)
        for i in range(cols // chunk):
            out_ref[step * (cols // chunk) + i] = result[:, i * chunk : (i + 1) * chunk].astype(BF16)


def mlp_kernel(dims, *refs):
    group, n_pages, n_blk = dims
    leaf_refs, refs = refs[:n_pages], refs[n_pages:]
    in_hbm, out_hbm, _, *refs = refs
    part_refs, (in_buf, out_buf, sems_in, sems_out) = refs[:n_pages], refs[n_pages:]
    chunk = D // n_blk
    n_steps, cols = out_buf.shape[0], out_buf.shape[2]
    core = jnp.bitwise_and(lax.axis_index("blk"), 1)

    def in_copy(step):
        return pltpu.make_async_copy(
            in_hbm.at[pl.ds(step * chunk, chunk), :], in_buf.at[step], sems_in.at[step]
        )

    def out_copy(step):
        return pltpu.make_async_copy(
            out_hbm.at[:, pl.ds(step * cols, cols)], out_buf.at[step], sems_out.at[step]
        )

    copies = [in_copy(step) for step in range(n_blk)] + [out_copy(step) for step in range(n_steps)]
    flight = 4
    for copy in copies[:flight]:
        copy.start()

    def arrived(step):
        copies[step].wait()
        if step + flight < len(copies):
            copies[step + flight].start()

    leaves = [ref[...].astype(F32) for ref in leaf_refs]
    half = n_blk // 2
    hidden = jnp.zeros((n_pages * group, in_buf.shape[2]), F32)
    for z in range(half):
        arrived(2 * z)
        arrived(2 * z + 1)
        for i, c in ((z, 2 * z + core), (half + z, 2 * z + 1 - core)):
            rows = [leaf[i * group : (i + 1) * group] for leaf in leaves]
            hidden = hidden + dot(jnp.concatenate(rows, axis=0).astype(BF16), in_buf[c])
    active = (0.5 * hidden * (1.0 + lax.erf(hidden * math.sqrt(0.5)))).astype(BF16)
    for step in range(n_steps):
        arrived(n_blk + step)
        result = dot(active, out_buf[step]).astype(BF16)
        for g in range(n_pages):
            part_refs[g][:, step * cols : (step + 1) * cols] = result[g * group : (g + 1) * group]


VMEM = pl.BlockSpec(memory_space=pltpu.VMEM)
HBM = pl.BlockSpec(memory_space=pltpu.HBM)
ANY = pl.BlockSpec(memory_space=pl.ANY)


def shape_of(shape, kind=BF16):
    return jax.ShapeDtypeStruct(shape, kind)


def params_of(mib):
    return pltpu.CompilerParams(vmem_limit_bytes=mib * MIB)


def cost_of(flops, nbytes):
    return pl.CostEstimate(flops=int(flops), bytes_accessed=int(nbytes), transcendentals=0)


def on_device(
    new_hidden,
    attn_gain,
    mlp_gain,
    qkv_weight,
    dense_weight,
    in_weight,
    out_weight,
    page_store,
    held_states,
    fold_weights,
    page_table,
    lengths,
    keep_slots,
    fold_index,
    recompute_list,
):
    n_pages = lax.axis_size("pages")
    n_blk = lax.axis_size("blk")
    n_dev = n_pages * n_blk
    mine = lax.axis_index("pages")
    device = lax.axis_index(("pages", "blk"))
    group = lengths.shape[0]
    pages_dev = page_store.shape[0]
    slots = -(-(pages_dev // n_pages) // 4) * 4
    ranks = n_pages * slots
    heads = H // n_blk
    head_lanes = heads * HD
    extra = 2 * heads * NREC
    lanes = head_lanes + extra
    chunk = D // n_blk
    held_rows = held_states.shape[0] * NREC
    kept_count = KP * PAGE

    def swapped(array, axis, size, by):
        return lax.ppermute(array, axis, [(i, i ^ by) for i in range(size)])

    def swapped(array, axis, size, by):
        return lax.ppermute(array, axis, [(i, i ^ by) for i in range(size)])

    def fixed(array):
        return pltpu.with_memory_space_constraint(array, pltpu.HBM)

    half = n_blk // 2
    pack = pl.pallas_call(
        pack_kernel,
        in_specs=[VMEM] * 3,
        out_specs=VMEM,
        out_shape=shape_of((half, n_blk * held_rows + group, chunk)),
        compiler_params=params_of(16),
        name="pack",
    )(fixed(held_states.reshape(held_rows, D)), fixed(new_hidden), fixed(attn_gain[None]))
    pack = lax.all_to_all(
        pack,
        "blk",
        0,
        0,
        axis_index_groups=[list(range(core, n_blk, 2)) for core in range(2)],
        tiled=True,
    )

    n_rows = n_dev * slots
    rows = group * (1 + NREC)
    period = 12 * HD if (3 * head_lanes) % (12 * HD) == 0 else 3 * head_lanes
    lane = np.arange(HD)
    frequency = np.where(lane < ROT, ROT_BASE ** (-2.0 * (lane % (ROT // 2)) / ROT), 0.0).astype(np.float32)
    gains, cosine, low, high, sel, sel_all, back, pick, numbers = pl.pallas_call(
        functools.partial(prep_kernel, (n_pages, pages_dev, slots, period // (3 * HD))),
        in_specs=[pl.BlockSpec(memory_space=pltpu.SMEM)] + [VMEM] * 8,
        out_specs=[VMEM] * 9,
        out_shape=[
            shape_of((2, D), F32),
            *[shape_of((rows, period), F32)] * 3,
            shape_of((n_rows, group)),
            shape_of((n_rows + group, group), F32),
            shape_of((group, n_rows + group)),
            shape_of((PPR * group, n_rows)),
            shape_of((group, 1 + KP + PPR + NREC), jnp.int32),
        ],
        compiler_params=params_of(16),
        cost_estimate=cost_of(0, 0),
        name="prep",
    )(
        page_table.T,
        fixed(page_table.T),
        fixed(lengths[None]),
        fixed(keep_slots),
        fixed(fold_index),
        fixed(recompute_list),
        fixed(jnp.asarray(frequency[None])),
        fixed(attn_gain[None]),
        fixed(mlp_gain[None]),
    )

    numbers = [numbers] + [swapped(numbers, "pages", n_pages, i) for i in range(1, n_pages)]

    tokens = pages_dev * PAGE
    pages = page_store.reshape(tokens, 2 * D)
    steps = H // STEP_HEADS
    step_lanes = STEP_HEADS * 2 * HD
    dests = STEP_HEADS // heads
    fold_width = 2 * head_lanes

    later = max(3 * head_lanes // period - 1, 1)
    first_part, loaded = pl.pallas_call(
        load_kernel,
        in_specs=[HBM, ANY],
        out_specs=[VMEM, VMEM],
        out_shape=[pltpu.VMEM((D, period), BF16), shape_of((8, 128), F32)],
        scratch_shapes=[pltpu.SemaphoreType.DMA((8,))],
        compiler_params=params_of(4),
        cost_estimate=cost_of(0, 0),
        name="load_qkv",
    )(fixed(qkv_weight), numbers[0])
    pack, cosine, loaded = lax.optimization_barrier((pack, cosine, loaded))
    packs = [pack, swapped(pack, "blk", n_blk, 1)]

    wire = lanes + wire_split(lanes)
    send, own, leaf = pl.pallas_call(
        functools.partial(project_kernel, (group, n_blk, held_rows, heads, slots)),
        in_specs=[VMEM] * 4 + [HBM] + [VMEM] * 4 + [ANY],
        out_specs=[VMEM] * 3,
        out_shape=[
            shape_of((n_dev, 2, wire)),
            shape_of((group, lanes)),
            shape_of((n_blk * group, chunk)),
        ],
        scratch_shapes=[
            pltpu.VMEM((later, n_blk, chunk, period), BF16),
            pltpu.VMEM((n_blk, rows, chunk), F32),
            pltpu.VMEM((rows, period), F32),
            pltpu.SemaphoreType.DMA((later, n_blk)),
        ],
        compiler_params=params_of(32),
        cost_estimate=cost_of(2 * rows * D * 3 * head_lanes, 6 * D * head_lanes),
        name="project",
    )(
        *packs,
        gains,
        pltpu.with_memory_space_constraint(first_part, pltpu.VMEM),
        fixed(qkv_weight),
        cosine,
        low,
        high,
        sel,
        loaded,
    )
    send, *numbers = lax.optimization_barrier((send, *numbers))
    asked = lax.all_to_all(send, ("pages", "blk"), 0, 0, tiled=True)
    fold_rows, valid, renew = pl.pallas_call(
        functools.partial(facts_kernel, (n_pages, pages_dev, slots)),
        in_specs=[VMEM] * (n_pages + 2),
        out_specs=[VMEM] * 3,
        out_shape=[
            shape_of((ranks, tokens), F32),
            shape_of((tokens + ranks, OCTET * ranks), F32),
            shape_of((tokens + ranks, 2 * OCTET * NREC)),
        ],
        compiler_params=params_of(16),
        cost_estimate=cost_of(0, 0),
        name="facts",
    )(*numbers, fixed(page_table.T), fixed(fold_weights))

    leaf, fold_rows = lax.optimization_barrier((leaf, fold_rows))
    leaves = [leaf] + [swapped(leaf, "pages", n_pages, i) for i in range(1, n_pages)]

    folded_rows = pl.pallas_call(
        fold_kernel,
        grid=(steps,),
        in_specs=[
            pl.BlockSpec((ranks, tokens), lambda i: (0, 0)),
            pl.BlockSpec((tokens, step_lanes), lambda i: (0, i)),
        ],
        out_specs=pl.BlockSpec((ranks, step_lanes), lambda i: (0, i)),
        out_shape=shape_of((ranks, 2 * D)),
        compiler_params=params_of(16),
        cost_estimate=cost_of(0, 0),
        name="fold",
    )(fold_rows, fixed(pages))

    all_lanes = lanes + fold_width
    all_wire = all_lanes + wire_split(all_lanes)
    partial = pl.pallas_call(
        functools.partial(attend_kernel, (n_pages, slots, dests, heads)),
        grid=(steps,),
        in_specs=[
            pl.BlockSpec((n_pages, dests, 2, wire), lambda i: (0, i, 0, 0)),
            pl.BlockSpec((tokens + ranks, OCTET * ranks), lambda i: (0, 0)),
            pl.BlockSpec((tokens + ranks, 2 * OCTET * NREC), lambda i: (0, 0)),
            pl.BlockSpec((tokens, step_lanes), lambda i: (0, i)),
            pl.BlockSpec((ranks, step_lanes), lambda i: (0, i)),
        ],
        out_specs=pl.BlockSpec((n_pages, dests, 2, all_wire), lambda i: (0, i, 0, 0)),
        out_shape=shape_of((n_pages, n_blk, 2, all_wire)),
        compiler_params=params_of(16),
        cost_estimate=cost_of(2 * 128 * tokens * 2 * D, tokens * 4 * D),
        name="attend",
    )(asked.reshape(n_pages, n_blk, 2, wire), valid, renew, fixed(pages), folded_rows)
    partial, *leaves = lax.optimization_barrier((partial, *leaves))
    got = lax.all_to_all(partial.reshape(n_dev, 2, all_wire), ("pages", "blk"), 0, 0, tiled=True)

    hidden = in_weight.shape[1]
    mlp_parts = pl.pallas_call(
        functools.partial(mlp_kernel, (group, n_pages, n_blk)),
        in_specs=[VMEM] * n_pages + [HBM, HBM, ANY],
        out_specs=[VMEM] * n_pages,
        out_shape=[shape_of((group, D))] * n_pages,
        scratch_shapes=[
            pltpu.VMEM((n_blk, chunk, hidden), BF16),
            pltpu.VMEM((8, hidden, D // 8), BF16),
            pltpu.SemaphoreType.DMA((n_blk,)),
            pltpu.SemaphoreType.DMA((8,)),
        ],
        compiler_params=params_of(24),
        cost_estimate=cost_of(4 * n_pages * group * D * hidden, 4 * D * hidden),
        name="mlp",
    )(*leaves, fixed(in_weight), fixed(out_weight), partial)
    mlp_share = [mlp_parts[0]] + [swapped(mlp_parts[i], "pages", n_pages, i) for i in range(1, n_pages)]

    out_part = pl.pallas_call(
        functools.partial(merge_kernel, (group, n_dev, slots, heads, n_pages)),
        in_specs=[VMEM] * (n_pages + 4) + [HBM],
        out_specs=VMEM,
        out_shape=shape_of((n_blk, group, chunk)),
        scratch_shapes=[
            pltpu.VMEM((8, head_lanes, D // 8), BF16),
            pltpu.VMEM((n_rows + group, lanes), F32),
            pltpu.SemaphoreType.DMA((8,)),
        ],
        compiler_params=params_of(24),
        cost_estimate=cost_of(2 * group * D * head_lanes, 2 * D * head_lanes),
        name="merge",
    )(
        got,
        own,
        sel_all,
        back,
        *mlp_share,
        fixed(dense_weight),
    )
    out_got = lax.all_to_all(out_part, "blk", 0, 0, tiled=True)
    summed = jnp.sum(out_got.astype(F32), axis=0).astype(BF16)

    folded = pl.pallas_call(
        functools.partial(place_kernel, (slots, all_lanes, lanes)),
        in_specs=[VMEM, VMEM],
        out_specs=VMEM,
        out_shape=shape_of((PPR, group, fold_width)),
        scratch_shapes=[pltpu.VMEM((n_rows, fold_width), F32)],
        compiler_params=params_of(16),
        cost_estimate=cost_of(0, 4 * n_rows * fold_width),
        name="place",
    )(pick, got)
    folded = jnp.transpose(folded, (1, 0, 2))
    return (summed, folded)


def solution(mesh):
    in_specs = (
        P("pages", "blk"),
        P(),
        P(),
        P(None, "blk"),
        P("blk", None),
        P(None, ("pages", "blk")),
        P(("pages", "blk"), None),
        P(("pages", "blk"), None, None),
        P(("pages", "blk"), None, None),
        P(),
        P(),
        P("pages"),
        P("pages", None),
        P("pages", None),
        P("pages", None),
    )
    out_specs = (P("pages", "blk"), P("pages", None, "blk"))
    return jax.shard_map(
        on_device, mesh=mesh, in_specs=in_specs, out_specs=out_specs, check_vma=False
    )
```

```python
import functools
import math

import jax
import jax.numpy as jnp
import numpy as np
from jax import lax
from jax.experimental import pallas as pl
from jax.experimental.pallas import tpu as pltpu
from jax.sharding import PartitionSpec as P

D = 6144
H = 64
HD = 96
ROT = 24
PAGE = 16
PPR = 12
KP = 5
NREC = 8
NF = 8
FF = 24576

EPSILON = 1e-05
ROT_BASE = 10000.0
NEVER = -1e30
F32 = jnp.float32
BF16 = jnp.bfloat16
SCALE = 1.0 / math.sqrt(HD)
MIB = 1024 * 1024
STEP_HEADS = 32
QUAD = 4
OCTET = 8


def iota(shape, axis):
    return lax.broadcasted_iota(jnp.int32, shape, axis)


def dot(left, right):
    return jnp.dot(left, right, preferred_element_type=F32)


def dot_nt(left, right):
    return lax.dot_general(left, right, (((1,), (1,)), ((), ())), preferred_element_type=F32)


def dot_tn(left, right):
    return lax.dot_general(left, right, (((0,), (0,)), ((), ())), preferred_element_type=F32)


def parts_of(values, count):
    parts = []
    for _ in range(count):
        part = values.astype(BF16)
        parts.append(part)
        values = values - part.astype(F32)
    return parts


def split_dot(values, selector, count):
    total = None
    for part in parts_of(values, count):
        term = dot(part, selector)
        total = term if total is None else total + term
    return total


def wire_split(width):
    return (width // 128 + 1) // 2 * 128 if width % 128 == 0 else (width + 1) // 2


def wire_tail(thirds, width):
    first = wire_split(width)
    count = thirds.shape[0]
    at, of = iota((2 * count, count), 0), iota((2 * count, count), 1)
    upper = jnp.where(at == 2 * of, 1.0, 0.0).astype(BF16)
    lower = jnp.where(at == 2 * of + 1, 1.0, 0.0).astype(BF16)
    rest = thirds[:, first:]
    if width < 2 * first:
        rest = jnp.concatenate([rest, jnp.zeros((count, 2 * first - width), BF16)], axis=1)
    return (dot(upper, thirds[:, :first]) + dot(lower, rest)).astype(BF16)


def third_row(ref, index, width, start, stop):
    first = wire_split(width)
    third = []
    if start < first:
        third.append(ref[(*index, slice(0, 1), slice(width + start, width + min(stop, first)))].astype(F32))
    if stop > first:
        begin = max(start, first) - first
        third.append(ref[(*index, slice(1, 2), slice(width + begin, width + stop - first))].astype(F32))
    return third[0] if len(third) == 1 else jnp.concatenate(third, axis=1)


def prep_kernel(dims, table_smem, table_ref, length_ref, keep_ref, choice_ref, list_ref, frequency_ref, *refs):
    n_pages, pages_dev, period_heads = dims
    attn_gain_ref, mlp_gain_ref, *refs = refs
    gain_ref, cos_ref, low_ref, high_ref, sel_ref, sel_all_ref, back_ref, pick_ref, number_ref = refs
    gain_ref[0:1, :] = attn_gain_ref[...]
    gain_ref[1:2, :] = mlp_gain_ref[...]
    group = keep_ref.shape[0]
    n_rows = sel_ref.shape[0]
    mine = lax.axis_index("pages")

    ids = table_ref[:, :group]
    for g in range(1, n_pages):
        ids = jnp.where(mine == g, table_ref[:, g * group : (g + 1) * group], ids)
    holder = jnp.floor((ids.astype(F32) + 0.5) * (1.0 / pages_dev)).astype(jnp.int32)

    def one_request(r, rank):
        for j in range(PPR):
            other = table_smem[j, mine * group + r]
            earlier = (holder == lax.div(other, jnp.int32(pages_dev))) & (ids > other)
            rank = rank + jnp.where(earlier, 1, 0)
        return rank

    rank = lax.fori_loop(0, group, one_request, jnp.zeros_like(ids))
    row = jnp.where(rank < 2, 2 * holder + rank, n_rows // 3 * 2 + holder)
    at = iota((n_rows, group), 0)
    hit = None
    for j in range(PPR):
        one = at == row[j : j + 1, :]
        hit = one if hit is None else hit | one
    hit = jnp.where(hit, 1.0, 0.0)
    same = jnp.where(iota((group, group), 0) == iota((group, group), 1), 1.0, 0.0)
    sel_ref[...] = hit.astype(BF16)
    sel_all_ref[:n_rows, :] = hit
    sel_all_ref[n_rows:, :] = same
    turned = row.astype(F32).T
    at = iota((group, n_rows), 1).astype(F32)
    back = jnp.zeros((group, n_rows), F32)
    for j in range(PPR):
        one = jnp.where(at == turned[:, j : j + 1], 1.0, 0.0)
        pick_ref[j * group : (j + 1) * group, :] = one.astype(BF16)
        back = back + one
    back_ref[:, :n_rows] = back.astype(BF16)
    back_ref[:, n_rows:] = same.astype(BF16)

    length = jnp.sum(same * length_ref[...].astype(F32), axis=1, keepdims=True)
    renewed = list_ref[...]
    slot = jnp.zeros_like(renewed)
    for k in range(KP):
        slot = jnp.where(jnp.right_shift(renewed, 4) == k, keep_ref[:, k : k + 1], slot)
    place = (slot * PAGE + jnp.bitwise_and(renewed, PAGE - 1)).astype(F32)
    place = jnp.broadcast_to(place[:, None, :], (group, NREC, NREC)).reshape(group * NREC, NREC)
    shape = (group * NREC, NREC)
    place = jnp.where(jnp.bitwise_and(iota(shape, 0), NREC - 1) == iota(shape, 1), place, 0.0)
    place = jnp.concatenate([length, jnp.sum(place, axis=1, keepdims=True)], axis=0)
    angle = place * frequency_ref[...]
    cosine, sine = jnp.cos(angle), jnp.sin(angle)
    lane = iota(angle.shape, 1)
    low = jnp.where(lane < ROT // 2, -sine, 0.0)
    high = jnp.where((lane >= ROT // 2) & (lane < ROT), sine, 0.0)
    one, none = jnp.ones_like(angle), jnp.zeros_like(angle)
    cos_ref[...] = jnp.concatenate([cosine, cosine, one] * period_heads, axis=1)
    low_ref[...] = jnp.concatenate([low, low, none] * period_heads, axis=1)
    high_ref[...] = jnp.concatenate([high, high, none] * period_heads, axis=1)
    numbers = [length.astype(jnp.int32), keep_ref[...], choice_ref[...], renewed]
    number_ref[...] = jnp.concatenate(numbers, axis=1)


def facts_kernel(dims, *refs):
    n_pages, pages_dev, slots = dims
    number_refs, (table_ref, fold_ref, weight_ref, valid_ref, renew_ref) = refs[:n_pages], refs[n_pages:]
    group = number_refs[0].shape[0]
    requests = n_pages * group
    ranks = n_pages * slots
    mine = lax.axis_index("pages")
    device = lax.axis_index(("pages", "blk"))
    numbers = []
    for g in range(n_pages):
        got = number_refs[0][...]
        for i in range(1, n_pages):
            got = jnp.where(jnp.bitwise_xor(mine, g) == i, number_refs[i][...], got)
        numbers.append(got.astype(F32))
    numbers = jnp.concatenate(numbers, axis=0).astype(BF16)

    local = iota((ranks, requests), 0)
    hits = jnp.zeros((ranks, requests), F32)
    slot = jnp.zeros((ranks, 1), F32)
    for j in range(PPR):
        one = jnp.where(local == table_ref[j : j + 1, :] - device * pages_dev, 1.0, 0.0)
        hits = hits + one
        slot = slot + j * jnp.sum(one, axis=1, keepdims=True)
    hits = jnp.where(local < pages_dev, hits, 0.0)
    facts = dot(hits.astype(BF16), numbers)
    length, keeps = facts[:, :1], facts[:, 1 : 1 + KP]
    choices, renewed = facts[:, 1 + KP : 1 + KP + PPR], facts[:, 1 + KP + PPR : 1 + KP + PPR + NREC]
    place = iota((ranks, PPR), 1).astype(F32)
    choice = jnp.sum(jnp.where(place == slot, choices, 0.0), axis=1, keepdims=True)
    found = jnp.sum(hits, axis=1, keepdims=True) > 0.5
    kept_hit = jnp.where(keeps == slot, 1.0, 0.0)
    kept = (jnp.sum(kept_hit, axis=1, keepdims=True) > 0.5) & found
    kept_place = PAGE * jnp.sum(kept_hit * iota((ranks, KP), 1).astype(F32), axis=1, keepdims=True)
    dropped = jnp.logical_not(kept) & found & (slot * PAGE < length)

    owner = jnp.concatenate(
        [jnp.sum(hits[:, g * group : (g + 1) * group], axis=1, keepdims=True) for g in range(n_pages)], axis=1
    )
    below = jnp.where(iota((ranks, ranks), 0) > iota((ranks, ranks), 1), 1.0, 0.0).astype(BF16)
    before = dot(below, owner.astype(BF16))
    group_of = iota((ranks, n_pages), 1).astype(F32)
    rank = jnp.where(before < 1.5, 2 * group_of + before, 2 * n_pages + group_of)
    rank = jnp.sum(owner * rank, axis=1, keepdims=True)
    rank = jnp.where(found, rank, -1.0)
    rank_hit = jnp.where(rank == iota((ranks, ranks), 1).astype(F32), 1.0, 0.0).astype(BF16)

    weights = jnp.zeros((ranks, PAGE), F32)
    for f in range(NF):
        weights = jnp.where(choice == f, fold_ref[f : f + 1, :], weights)
    live = slot * PAGE + iota((ranks, PAGE), 1).astype(F32) < length
    weights = jnp.where(live & dropped, weights, 0.0)
    weights = jnp.concatenate([weights] * pages_dev, axis=1)
    tokens = pages_dev * PAGE
    own = jnp.right_shift(iota((ranks, tokens), 1), 4) == iota((ranks, tokens), 0)
    weights = jnp.where(own, weights, 0.0)
    total = jnp.zeros((ranks, tokens), F32)
    for part in parts_of(weights, 3):
        total = total + dot_tn(rank_hit, part)
    weight_ref[...] = total

    lanes = valid_ref.shape[1]
    lane_rank = jnp.bitwise_and(iota((ranks, lanes), 1), ranks - 1).astype(F32)
    for_rank = jnp.where(lane_rank == rank, 1.0, 0.0)
    kept_for = jnp.where(kept, for_rank, 0.0)
    dropped_for = jnp.where(dropped, for_rank, 0.0)
    renewed = jnp.concatenate([renewed] * (renew_ref.shape[1] // NREC), axis=1)
    renewed = jnp.where(kept, renewed - kept_place, -1.0)
    inside = iota((PAGE, renew_ref.shape[1]), 0).astype(F32)
    for p in range(pages_dev):
        some = slice(p * PAGE, (p + 1) * PAGE)
        valid_ref[some, :] = jnp.broadcast_to(kept_for[p : p + 1, :], (PAGE, lanes))
        renew_ref[some, :] = jnp.where(inside == renewed[p : p + 1, :], 1.0, 0.0).astype(BF16)
    valid_ref[tokens:, :] = dot_tn(rank_hit, dropped_for.astype(BF16))
    renew_ref[tokens:, :] = jnp.zeros((ranks, renew_ref.shape[1]), BF16)


def pack_kernel(held_ref, new_ref, gain_ref, out_ref):
    group, chunk = new_ref.shape
    held = held_ref[...].astype(F32)
    held = held - jnp.sum(held, axis=1, keepdims=True) / D
    spread = jnp.sum(held * held, axis=1, keepdims=True) / D
    held = held * lax.rsqrt(spread + EPSILON) * gain_ref[...]
    rows = [held[:, c * chunk : (c + 1) * chunk] for c in range(D // chunk)] + [new_ref[...].astype(F32)]
    rows = jnp.concatenate(rows, axis=0).astype(BF16)
    for i in range(out_ref.shape[0]):
        out_ref[i] = rows


def project_kernel(dims, *refs):
    group, n_blk, held_rows, heads = dims
    pack_refs, refs = refs[:2], refs[2:]
    gain_ref, weight_hbm, cos_ref, low_ref, high_ref, sel_ref, *refs = refs
    send_ref, own_ref, leaf_ref, weight_buf, rows_ref, acc_ref, sems = refs
    chunk = D // n_blk
    width = 3 * heads * HD
    head_lanes = heads * HD
    extra = 2 * heads * NREC
    period = cos_ref.shape[1]
    period_heads = period // (3 * HD)
    core = jnp.bitwise_and(lax.axis_index("blk"), 1)

    def weight_copy(part, step):
        return pltpu.make_async_copy(
            weight_hbm.at[pl.ds(step * chunk, chunk), pl.ds(part * period, period)],
            weight_buf.at[part, step],
            sems.at[part, step],
        )

    flight = 6
    for step in range(flight):
        weight_copy(0, step).start()

    pieces, places = [], []
    for other in range(2):
        for z in range(n_blk // 2):
            b = 2 * z + jnp.bitwise_xor(core, other)
            values = pack_refs[other][z].astype(F32)
            pieces.append(values[n_blk * held_rows :])
            places.append(b)
            first = pl.multiple_of(group + b * held_rows, 8)
            for c in range(n_blk):
                rows_ref[c, pl.ds(first, held_rows), :] = values[c * held_rows : (c + 1) * held_rows]
    mean = sum(jnp.sum(piece, axis=1, keepdims=True) for piece in pieces) / D
    pieces = [piece - mean for piece in pieces]
    spread = sum(jnp.sum(piece * piece, axis=1, keepdims=True) for piece in pieces) / D
    spread = lax.rsqrt(spread + EPSILON)
    leaves = []
    for i, (b, piece) in enumerate(zip(places, pieces)):
        z = i % (n_blk // 2)
        some = slice(2 * z * chunk, 2 * (z + 1) * chunk)
        gain = gain_ref[:, some]
        gain = jnp.where(b == 2 * z, gain[:, :chunk], gain[:, chunk:])
        piece = piece * spread
        rows_ref[b, 0:group, :] = piece * gain[0:1]
        leaves.append(piece * gain[1:2])
    leaf_ref[...] = jnp.concatenate(leaves, axis=0).astype(BF16)

    rows = acc_ref.shape[0]
    wide = heads * NREC
    score = jnp.zeros((rows, wide), F32)
    head_at = jnp.right_shift(iota((rows, wide), 1), 3)
    queries, values = [], []
    for j in range(width // period):
        acc_ref[...] = jnp.zeros_like(acc_ref)

        def one_chunk(step, carry, j=j):
            @pl.when(step + flight < n_blk)
            def _():
                weight_copy(j, step + flight).start()

            if j + 1 < width // period:

                @pl.when(step + flight >= n_blk)
                def _():
                    weight_copy(j + 1, step + flight - n_blk).start()

            weight_copy(j, step).wait()
            acc_ref[...] += dot(rows_ref[step].astype(BF16), weight_buf[j, step])
            return carry

        lax.fori_loop(0, n_blk, one_chunk, 0)
        block = acc_ref[...]
        up = jnp.concatenate([block[:, ROT // 2 :], block[:, : ROT // 2]], axis=1)
        down = jnp.concatenate([block[:, -ROT // 2 :], block[:, : -ROT // 2]], axis=1)
        turned = block * cos_ref[...] + up * low_ref[...] + down * high_ref[...]
        turned = turned.astype(BF16).astype(F32)
        for h in range(period_heads):
            first = h * 3 * HD
            query = turned[:group, first : first + HD]
            key = turned[:, first + HD : first + 2 * HD]
            queries.append(query)
            values.append(turned[:group, first + 2 * HD : first + 3 * HD])
            own_product = key[:group] * query
            held_product = key[group:].reshape(group, -1, HD) * query[:, None, :]
            product = jnp.concatenate([own_product, held_product.reshape(rows - group, HD)], axis=0)
            score = jnp.where(
                head_at == j * period_heads + h, jnp.sum(product, axis=1, keepdims=True), score
            )
    score = score * SCALE
    sel = sel_ref[...]
    asked = dot(sel, jnp.concatenate(queries, axis=1).astype(BF16))
    own_ref[:, :head_lanes] = jnp.concatenate(values, axis=1).astype(BF16)

    held_score = score[group:]
    held_count = held_score.shape[0]
    row_id = jnp.bitwise_and(iota((held_count, wide), 0), NREC - 1)
    lane_id = jnp.bitwise_and(iota((held_count, wide), 1), NREC - 1)
    held_score = jnp.where(row_id == lane_id, held_score, 0.0)
    per_request = held_count // group
    spread_ids = jnp.right_shift(iota((group, held_count), 1), per_request.bit_length() - 1)
    spread_rows = jnp.where(spread_ids == iota((group, held_count), 0), 1.0, 0.0).astype(BF16)
    sel_rows = dot(sel, spread_rows).astype(BF16)
    both = jnp.concatenate(parts_of(held_score, 2), axis=1)
    given = dot(sel_rows, both)
    both = jnp.concatenate([asked, given], axis=1).astype(BF16)
    lanes = both.shape[1]
    n_dev = send_ref.shape[0]
    tails = wire_tail(both[2 * n_dev :], lanes)
    for d in range(n_dev):
        send_ref[d, :, :lanes] = both[2 * d : 2 * d + 2]
        send_ref[d, :, lanes:] = tails[2 * d : 2 * d + 2]

    own_score = score[:group]
    lane = iota((group, extra), 1)
    own = jnp.zeros((group, extra), F32)
    for i, part in enumerate(parts_of(own_score, 3)):
        part = part.astype(F32)
        for h in range(heads):
            own = jnp.where(lane == i * heads + h, part[:, h * NREC : h * NREC + 1], own)
    own_ref[:, head_lanes : head_lanes + extra] = own.astype(BF16)


def fold_kernel(weight_ref, page_ref, fold_ref):
    parts = jnp.concatenate(parts_of(weight_ref[...], 3), axis=0)
    rows = weight_ref.shape[0]
    sums = dot(parts, page_ref[...])
    folded = sums[:rows] + sums[rows : 2 * rows] + sums[2 * rows :]
    fold_ref[...] = folded.astype(BF16)


def place_kernel(dims, pick_ref, got_ref, out_ref, rows_ref):
    width, first_lane = dims
    n_dev = got_ref.shape[0]
    for d in range(n_dev):
        rows_ref[2 * d : 2 * d + 2, :] = got_ref[d, :, first_lane:width].astype(F32)
        rows_ref[2 * n_dev + d : 2 * n_dev + d + 1, :] = third_row(got_ref, (d,), width, first_lane, width)
    found = dot(pick_ref[...], rows_ref[...].astype(BF16)).astype(BF16)
    group = out_ref.shape[1]
    for j in range(out_ref.shape[0]):
        out_ref[j] = found[j * group : (j + 1) * group]


def attend_kernel(dims, ask_ref, valid_ref, place_ref, page_ref, fold_ref, *refs):
    send_ref = refs[-1]
    n_pages, slots, dests, heads = dims
    rows = n_pages * slots
    head_lanes = heads * HD
    extra = 2 * heads * NREC
    tokens = page_ref.shape[0]
    width = head_lanes + extra
    asks = []
    for b in range(dests):
        pairs = [ask_ref[g, b, :, :width].astype(F32) for g in range(n_pages)]
        thirds = [third_row(ask_ref, (g, b), width, 0, width) for g in range(n_pages)]
        asks.append(jnp.concatenate([*pairs, *thirds, jnp.zeros((rows - 3 * n_pages, width), F32)], axis=0))
    query = jnp.concatenate([a[:, :head_lanes] for a in asks], axis=1)
    given = jnp.concatenate([a[:, head_lanes : head_lanes + extra] for a in asks], axis=1)
    valid = valid_ref[...] > 0.5
    place = place_ref[...]
    touched = jnp.sum(place[:, :NREC].astype(F32), axis=1, keepdims=True) > 0.5
    lanes = OCTET * rows
    shift = rows.bit_length() - 1
    lane_head = jnp.right_shift(iota((HD, lanes), 1), shift)
    blank = jnp.zeros((HD, lanes), F32)
    lane = iota((lanes, lanes), 1)
    lane_in = jnp.bitwise_and(lane, extra - 1)
    lane_dest = jnp.right_shift(lane, extra.bit_length() - 1) * heads
    given_head = jnp.right_shift(jnp.bitwise_and(lane_in, heads * NREC - 1), 3) + lane_dest
    row_head = jnp.right_shift(iota((lanes, lanes), 0), shift)
    own_lane = jnp.bitwise_and(iota((rows, lanes), 1), rows - 1) == iota((rows, lanes), 0)
    goals = []
    for i in range(3):
        hit = (lane_in >= i * heads) & (lane_in < (i + 1) * heads)
        hit = hit & (row_head == lane_dest + lane_in - i * heads)
        goals.append(jnp.where(hit, 1.0, 0.0).astype(BF16))
    octets = range(STEP_HEADS // OCTET)
    all_scores = []
    for o in octets:
        heads_here = range(o * OCTET, (o + 1) * OCTET)
        asked = jnp.concatenate([query[:, h * HD : (h + 1) * HD] for h in heads_here], axis=0)
        asked = jnp.concatenate([asked, jnp.zeros((lanes, 128 - HD), F32)], axis=1).T[:HD]
        stacked = []
        for h in range(OCTET):
            stacked += [jnp.where(lane_head == h, asked, 0.0), blank]
        stacked = jnp.concatenate(stacked, axis=0).astype(BF16)
        told = jnp.concatenate([given[:, o * lanes : (o + 1) * lanes]] * OCTET, axis=0)
        told = jnp.where(given_head == row_head, told, 0.0).T.astype(BF16)
        some = slice(o * OCTET * 2 * HD, (o + 1) * OCTET * 2 * HD)
        page = jnp.concatenate([page_ref[:, some], fold_ref[:, some]], axis=0)
        all_scores.append(jnp.where(touched, dot(place, told), dot(page, stacked) * SCALE))
    all_weights, extras = [], []
    for scores in all_scores:
        scores = jnp.where(valid, scores, NEVER)
        top = jnp.max(scores, axis=0, keepdims=True)
        weights = jnp.where(valid, jnp.exp(scores - top), 0.0)
        total = jnp.sum(weights, axis=0, keepdims=True)
        safe = jnp.where(total > 0.0, total, 1.0)
        rest = jnp.zeros((256 - weights.shape[0], lanes), F32)
        all_weights.append(jnp.concatenate([weights * (1.0 / safe), rest], axis=0).T.astype(BF16))
        lse = jnp.where(own_lane, jnp.where(total > 0.0, top + jnp.log(safe), NEVER), 0.0)
        spread = jnp.zeros((rows, lanes), F32)
        for part, goal in zip(parts_of(lse, 3), goals):
            spread = spread + dot(part, goal)
        extras.append(spread)
    gathered = []
    for o in octets:
        for i in range(OCTET // QUAD):
            first = (o * OCTET + i * QUAD) * 2 * HD
            some = slice(first, first + QUAD * 2 * HD)
            page = [page_ref[:, some], fold_ref[:, some]]
            page.append(jnp.zeros((256 - tokens - rows, QUAD * 2 * HD), BF16))
            mixed = dot(all_weights[o][i * QUAD * rows : (i + 1) * QUAD * rows], jnp.concatenate(page, axis=0))
            for h in range(QUAD):
                gathered.append(mixed[h * rows : (h + 1) * rows, 2 * HD * h + HD : 2 * HD * (h + 1)])
    gathered = jnp.concatenate(gathered, axis=1)
    extras = jnp.concatenate(extras, axis=1)
    fold_lanes = 2 * head_lanes
    all_lanes = width + fold_lanes
    for b in range(dests):
        whole = jnp.concatenate(
            [
                gathered[:, b * head_lanes : (b + 1) * head_lanes].astype(BF16),
                extras[:, b * extra : (b + 1) * extra].astype(BF16),
                fold_ref[:, b * fold_lanes : (b + 1) * fold_lanes],
            ],
            axis=1,
        )
        tails = wire_tail(whole[2 * n_pages : 3 * n_pages], all_lanes)
        for g in range(n_pages):
            send_ref[g, b, :, :all_lanes] = whole[2 * g : 2 * g + 2]
            send_ref[g, b, :, all_lanes:] = tails[2 * g : 2 * g + 2]


def merge_kernel(
    dims, got_ref, own_ref, sel_ref, back_ref, *refs
):
    group, n_dev, heads, n_pages = dims
    share_refs, dense_hbm, refs = refs[:n_pages], refs[n_pages], refs[n_pages + 1 :]
    head_lanes = heads * HD
    extra = 2 * heads * NREC
    n_blk = n_dev // n_pages
    out_ref, dense_buf, rows_ref, sems = refs
    chunk = D // n_blk
    steps, _, cols = dense_buf.shape

    def dense_copy(step):
        return pltpu.make_async_copy(
            dense_hbm.at[:, pl.ds(step * cols, cols)], dense_buf.at[step], sems.at[step]
        )

    for step in range(steps):
        dense_copy(step).start()
    for d in range(n_dev):
        rows_ref[2 * d : 2 * d + 2, :] = got_ref[d, :, : head_lanes + extra].astype(F32)
        rows_ref[2 * n_dev + d : 2 * n_dev + d + 1, :] = third_row(
            got_ref, (d,), 3 * head_lanes + extra, 0, head_lanes + extra
        )
    rows_ref[3 * n_dev :, :] = own_ref[...].astype(F32)
    count = rows_ref.shape[0]
    parts = rows_ref[:, head_lanes : head_lanes + extra].astype(BF16)
    to, source = iota((extra, 128), 1), iota((extra, 128), 0)
    hit = None
    for i in range(3):
        one = (to < heads) & (source == to + i * heads)
        hit = one if hit is None else hit | one
    lse = dot(parts, jnp.where(hit, 1.0, 0.0).astype(BF16))
    tops = jnp.zeros((count, 128), F32)
    for r in range(group):
        mine = sel_ref[:, r : r + 1] > 0.5
        top = jnp.max(jnp.where(mine, lse, -3e38), axis=0, keepdims=True)
        tops = jnp.where(mine, top, tops)
    weights = jnp.exp(jnp.minimum(lse - tops, 0.0))
    back = back_ref[...]
    totals = jnp.zeros((group, 128), F32)
    for part in parts_of(weights, 3):
        totals = totals + dot(back, part)
    inverse = 1.0 / totals
    lanes, heads_of = iota((128, head_lanes), 1), iota((128, head_lanes), 0)
    over = lanes - heads_of * HD
    spread = jnp.where((over >= 0) & (over < HD), 1.0, 0.0).astype(BF16)
    weighted = split_dot(weights, spread, 2) * rows_ref[:, :head_lanes]
    mixed = jnp.zeros((group, head_lanes), F32)
    for part in parts_of(weighted, 2):
        mixed = mixed + dot(back, part)
    attended = (mixed * split_dot(inverse, spread, 3)).astype(BF16)
    for step in range(steps):
        dense_copy(step).wait()
        some = slice(step * cols, (step + 1) * cols)
        result = dot(attended, dense_buf[step])
        for share_ref in share_refs:
            result = result + share_ref[:, some].astype(F32)
        for i in range(cols // chunk):
            out_ref[step * (cols // chunk) + i] = result[:, i * chunk : (i + 1) * chunk].astype(BF16)


def mlp_kernel(dims, *refs):
    group, n_pages, n_blk = dims
    leaf_refs, refs = refs[:n_pages], refs[n_pages:]
    in_hbm, out_hbm, _, *refs = refs
    part_refs, (in_buf, out_buf, sems_in, sems_out) = refs[:n_pages], refs[n_pages:]
    chunk = D // n_blk
    n_steps, cols = out_buf.shape[0], out_buf.shape[2]
    core = jnp.bitwise_and(lax.axis_index("blk"), 1)

    def in_copy(step):
        return pltpu.make_async_copy(
            in_hbm.at[pl.ds(step * chunk, chunk), :], in_buf.at[step], sems_in.at[step]
        )

    def out_copy(step):
        return pltpu.make_async_copy(
            out_hbm.at[:, pl.ds(step * cols, cols)], out_buf.at[step], sems_out.at[step]
        )

    copies = [in_copy(step) for step in range(n_blk)] + [out_copy(step) for step in range(n_steps)]
    flight = 4
    for copy in copies[:flight]:
        copy.start()

    def arrived(step):
        copies[step].wait()
        if step + flight < len(copies):
            copies[step + flight].start()

    leaves = [ref[...].astype(F32) for ref in leaf_refs]
    half = n_blk // 2
    hidden = jnp.zeros((n_pages * group, in_buf.shape[2]), F32)
    for z in range(half):
        arrived(2 * z)
        arrived(2 * z + 1)
        for i, c in ((z, 2 * z + core), (half + z, 2 * z + 1 - core)):
            rows = [leaf[i * group : (i + 1) * group] for leaf in leaves]
            hidden = hidden + dot(jnp.concatenate(rows, axis=0).astype(BF16), in_buf[c])
    active = (0.5 * hidden * (1.0 + lax.erf(hidden * math.sqrt(0.5)))).astype(BF16)
    for step in range(n_steps):
        arrived(n_blk + step)
        result = dot(active, out_buf[step]).astype(BF16)
        for g in range(n_pages):
            part_refs[g][:, step * cols : (step + 1) * cols] = result[g * group : (g + 1) * group]


VMEM = pl.BlockSpec(memory_space=pltpu.VMEM)
HBM = pl.BlockSpec(memory_space=pltpu.HBM)
ANY = pl.BlockSpec(memory_space=pl.ANY)


def shape_of(shape, kind=BF16):
    return jax.ShapeDtypeStruct(shape, kind)


def params_of(mib):
    return pltpu.CompilerParams(vmem_limit_bytes=mib * MIB)


def cost_of(flops, nbytes):
    return pl.CostEstimate(flops=int(flops), bytes_accessed=int(nbytes), transcendentals=0)


def on_device(
    new_hidden,
    attn_gain,
    mlp_gain,
    qkv_weight,
    dense_weight,
    in_weight,
    out_weight,
    page_store,
    held_states,
    fold_weights,
    page_table,
    lengths,
    keep_slots,
    fold_index,
    recompute_list,
):
    n_pages = lax.axis_size("pages")
    n_blk = lax.axis_size("blk")
    n_dev = n_pages * n_blk
    mine = lax.axis_index("pages")
    device = lax.axis_index(("pages", "blk"))
    group = lengths.shape[0]
    pages_dev = page_store.shape[0]
    slots = -(-(pages_dev // n_pages) // 4) * 4
    ranks = n_pages * slots
    heads = H // n_blk
    head_lanes = heads * HD
    extra = 2 * heads * NREC
    lanes = head_lanes + extra
    chunk = D // n_blk
    held_rows = held_states.shape[0] * NREC
    kept_count = KP * PAGE

    def swapped(array, axis, size, by):
        return lax.ppermute(array, axis, [(i, i ^ by) for i in range(size)])

    def swapped(array, axis, size, by):
        return lax.ppermute(array, axis, [(i, i ^ by) for i in range(size)])

    def fixed(array):
        return pltpu.with_memory_space_constraint(array, pltpu.HBM)

    half = n_blk // 2
    pack = pl.pallas_call(
        pack_kernel,
        in_specs=[VMEM] * 3,
        out_specs=VMEM,
        out_shape=shape_of((half, n_blk * held_rows + group, chunk)),
        compiler_params=params_of(16),
        name="pack",
    )(fixed(held_states.reshape(held_rows, D)), fixed(new_hidden), fixed(attn_gain[None]))
    pack = lax.all_to_all(
        pack,
        "blk",
        0,
        0,
        axis_index_groups=[list(range(core, n_blk, 2)) for core in range(2)],
        tiled=True,
    )

    n_rows = n_dev * 3
    rows = group * (1 + NREC)
    period = 12 * HD if (3 * head_lanes) % (12 * HD) == 0 else 3 * head_lanes
    lane = np.arange(HD)
    frequency = np.where(lane < ROT, ROT_BASE ** (-2.0 * (lane % (ROT // 2)) / ROT), 0.0).astype(np.float32)
    gains, cosine, low, high, sel, sel_all, back, pick, numbers = pl.pallas_call(
        functools.partial(prep_kernel, (n_pages, pages_dev, period // (3 * HD))),
        in_specs=[pl.BlockSpec(memory_space=pltpu.SMEM)] + [VMEM] * 8,
        out_specs=[VMEM] * 9,
        out_shape=[
            shape_of((2, D), F32),
            *[shape_of((rows, period), F32)] * 3,
            shape_of((n_rows, group)),
            shape_of((n_rows + group, group), F32),
            shape_of((group, n_rows + group)),
            shape_of((PPR * group, n_rows)),
            shape_of((group, 1 + KP + PPR + NREC), jnp.int32),
        ],
        compiler_params=params_of(16),
        cost_estimate=cost_of(0, 0),
        name="prep",
    )(
        page_table.T,
        fixed(page_table.T),
        fixed(lengths[None]),
        fixed(keep_slots),
        fixed(fold_index),
        fixed(recompute_list),
        fixed(jnp.asarray(frequency[None])),
        fixed(attn_gain[None]),
        fixed(mlp_gain[None]),
    )

    numbers = [numbers] + [swapped(numbers, "pages", n_pages, i) for i in range(1, n_pages)]

    tokens = pages_dev * PAGE
    pages = page_store.reshape(tokens, 2 * D)
    steps = H // STEP_HEADS
    step_lanes = STEP_HEADS * 2 * HD
    dests = STEP_HEADS // heads
    fold_width = 2 * head_lanes

    pack, cosine = lax.optimization_barrier((pack, cosine))
    packs = [pack, swapped(pack, "blk", n_blk, 1)]

    wire = lanes + wire_split(lanes)
    send, own, leaf = pl.pallas_call(
        functools.partial(project_kernel, (group, n_blk, held_rows, heads)),
        in_specs=[VMEM] * 3 + [HBM] + [VMEM] * 4,
        out_specs=[VMEM] * 3,
        out_shape=[
            shape_of((n_dev, 2, wire)),
            shape_of((group, lanes)),
            shape_of((n_blk * group, chunk)),
        ],
        scratch_shapes=[
            pltpu.VMEM((3 * head_lanes // period, n_blk, chunk, period), BF16),
            pltpu.VMEM((n_blk, rows, chunk), F32),
            pltpu.VMEM((rows, period), F32),
            pltpu.SemaphoreType.DMA((3 * head_lanes // period, n_blk)),
        ],
        compiler_params=params_of(50),
        cost_estimate=cost_of(2 * rows * D * 3 * head_lanes, 6 * D * head_lanes),
        name="project",
    )(
        *packs,
        gains,
        fixed(qkv_weight),
        cosine,
        low,
        high,
        sel,
    )
    send, *numbers = lax.optimization_barrier((send, *numbers))
    asked = lax.all_to_all(send, ("pages", "blk"), 0, 0, tiled=True)
    fold_rows, valid, renew = pl.pallas_call(
        functools.partial(facts_kernel, (n_pages, pages_dev, slots)),
        in_specs=[VMEM] * (n_pages + 2),
        out_specs=[VMEM] * 3,
        out_shape=[
            shape_of((ranks, tokens), F32),
            shape_of((tokens + ranks, OCTET * ranks), F32),
            shape_of((tokens + ranks, 2 * OCTET * NREC)),
        ],
        compiler_params=params_of(16),
        cost_estimate=cost_of(0, 0),
        name="facts",
    )(*numbers, fixed(page_table.T), fixed(fold_weights))

    leaf, fold_rows = lax.optimization_barrier((leaf, fold_rows))
    leaves = [leaf] + [swapped(leaf, "pages", n_pages, i) for i in range(1, n_pages)]

    folded_rows = pl.pallas_call(
        fold_kernel,
        grid=(steps,),
        in_specs=[
            pl.BlockSpec((ranks, tokens), lambda i: (0, 0)),
            pl.BlockSpec((tokens, step_lanes), lambda i: (0, i)),
        ],
        out_specs=pl.BlockSpec((ranks, step_lanes), lambda i: (0, i)),
        out_shape=shape_of((ranks, 2 * D)),
        compiler_params=params_of(16),
        cost_estimate=cost_of(0, 0),
        name="fold",
    )(fold_rows, fixed(pages))

    all_lanes = lanes + fold_width
    all_wire = all_lanes + wire_split(all_lanes)
    partial = pl.pallas_call(
        functools.partial(attend_kernel, (n_pages, slots, dests, heads)),
        grid=(steps,),
        in_specs=[
            pl.BlockSpec((n_pages, dests, 2, wire), lambda i: (0, i, 0, 0)),
            pl.BlockSpec((tokens + ranks, OCTET * ranks), lambda i: (0, 0)),
            pl.BlockSpec((tokens + ranks, 2 * OCTET * NREC), lambda i: (0, 0)),
            pl.BlockSpec((tokens, step_lanes), lambda i: (0, i)),
            pl.BlockSpec((ranks, step_lanes), lambda i: (0, i)),
        ],
        out_specs=pl.BlockSpec((n_pages, dests, 2, all_wire), lambda i: (0, i, 0, 0)),
        out_shape=shape_of((n_pages, n_blk, 2, all_wire)),
        compiler_params=params_of(16),
        cost_estimate=cost_of(2 * 128 * tokens * 2 * D, tokens * 4 * D),
        name="attend",
    )(asked.reshape(n_pages, n_blk, 2, wire), valid, renew, fixed(pages), folded_rows)
    partial, *leaves = lax.optimization_barrier((partial, *leaves))
    got = lax.all_to_all(partial.reshape(n_dev, 2, all_wire), ("pages", "blk"), 0, 0, tiled=True)

    hidden = in_weight.shape[1]
    mlp_parts = pl.pallas_call(
        functools.partial(mlp_kernel, (group, n_pages, n_blk)),
        in_specs=[VMEM] * n_pages + [HBM, HBM, ANY],
        out_specs=[VMEM] * n_pages,
        out_shape=[shape_of((group, D))] * n_pages,
        scratch_shapes=[
            pltpu.VMEM((n_blk, chunk, hidden), BF16),
            pltpu.VMEM((8, hidden, D // 8), BF16),
            pltpu.SemaphoreType.DMA((n_blk,)),
            pltpu.SemaphoreType.DMA((8,)),
        ],
        compiler_params=params_of(24),
        cost_estimate=cost_of(4 * n_pages * group * D * hidden, 4 * D * hidden),
        name="mlp",
    )(*leaves, fixed(in_weight), fixed(out_weight), partial)
    mlp_share = [mlp_parts[0]] + [swapped(mlp_parts[i], "pages", n_pages, i) for i in range(1, n_pages)]

    out_part = pl.pallas_call(
        functools.partial(merge_kernel, (group, n_dev, heads, n_pages)),
        in_specs=[VMEM] * (n_pages + 4) + [HBM],
        out_specs=VMEM,
        out_shape=shape_of((n_blk, group, chunk)),
        scratch_shapes=[
            pltpu.VMEM((8, head_lanes, D // 8), BF16),
            pltpu.VMEM((n_rows + group, lanes), F32),
            pltpu.SemaphoreType.DMA((8,)),
        ],
        compiler_params=params_of(24),
        cost_estimate=cost_of(2 * group * D * head_lanes, 2 * D * head_lanes),
        name="merge",
    )(
        got,
        own,
        sel_all,
        back,
        *mlp_share,
        fixed(dense_weight),
    )
    out_got = lax.all_to_all(out_part, "blk", 0, 0, tiled=True)
    summed = jnp.sum(out_got.astype(F32), axis=0).astype(BF16)

    folded = pl.pallas_call(
        functools.partial(place_kernel, (all_lanes, lanes)),
        in_specs=[VMEM, VMEM],
        out_specs=VMEM,
        out_shape=shape_of((PPR, group, fold_width)),
        scratch_shapes=[pltpu.VMEM((n_rows, fold_width), F32)],
        compiler_params=params_of(16),
        cost_estimate=cost_of(0, 4 * n_rows * fold_width),
        name="place",
    )(pick, got)
    folded = jnp.transpose(folded, (1, 0, 2))
    return (summed, folded)


def solution(mesh):
    in_specs = (
        P("pages", "blk"),
        P(),
        P(),
        P(None, "blk"),
        P("blk", None),
        P(None, ("pages", "blk")),
        P(("pages", "blk"), None),
        P(("pages", "blk"), None, None),
        P(("pages", "blk"), None, None),
        P(),
        P(),
        P("pages"),
        P("pages", None),
        P("pages", None),
        P("pages", None),
    )
    out_specs = (P("pages", "blk"), P("pages", None, "blk"))
    return jax.shard_map(
        on_device, mesh=mesh, in_specs=in_specs, out_specs=out_specs, check_vma=False
    )
```

```python
import functools
import math

import jax
import jax.numpy as jnp
import numpy as np
from jax import lax
from jax.experimental import pallas as pl
from jax.experimental.pallas import tpu as pltpu
from jax.sharding import PartitionSpec as P

D = 6144
H = 64
HD = 96
ROT = 24
PAGE = 16
PPR = 12
KP = 5
NREC = 8
NF = 8
FF = 24576

EPSILON = 1e-05
ROT_BASE = 10000.0
NEVER = -1e30
F32 = jnp.float32
BF16 = jnp.bfloat16
SCALE = 1.0 / math.sqrt(HD)
MIB = 1024 * 1024
STEP_HEADS = 32
ATTEND_HEADS = 64
QUAD = 4
OCTET = 8


def iota(shape, axis):
    return lax.broadcasted_iota(jnp.int32, shape, axis)


def dot(left, right):
    return jnp.dot(left, right, preferred_element_type=F32)


def dot_nt(left, right):
    return lax.dot_general(left, right, (((1,), (1,)), ((), ())), preferred_element_type=F32)


def dot_tn(left, right):
    return lax.dot_general(left, right, (((0,), (0,)), ((), ())), preferred_element_type=F32)


def parts_of(values, count):
    parts = []
    for _ in range(count):
        part = values.astype(BF16)
        parts.append(part)
        values = values - part.astype(F32)
    return parts


def split_dot(values, selector, count):
    total = None
    for part in parts_of(values, count):
        term = dot(part, selector)
        total = term if total is None else total + term
    return total


def wire_split(width):
    return (width // 128 + 1) // 2 * 128 if width % 128 == 0 else (width + 1) // 2


def wire_tail(thirds, width):
    first = wire_split(width)
    count = thirds.shape[0]
    at, of = iota((2 * count, count), 0), iota((2 * count, count), 1)
    upper = jnp.where(at == 2 * of, 1.0, 0.0).astype(BF16)
    lower = jnp.where(at == 2 * of + 1, 1.0, 0.0).astype(BF16)
    rest = thirds[:, first:]
    if width < 2 * first:
        rest = jnp.concatenate([rest, jnp.zeros((count, 2 * first - width), BF16)], axis=1)
    return (dot(upper, thirds[:, :first]) + dot(lower, rest)).astype(BF16)


def third_row(ref, index, width, start, stop):
    first = wire_split(width)
    third = []
    if start < first:
        third.append(ref[(*index, slice(0, 1), slice(width + start, width + min(stop, first)))].astype(F32))
    if stop > first:
        begin = max(start, first) - first
        third.append(ref[(*index, slice(1, 2), slice(width + begin, width + stop - first))].astype(F32))
    return third[0] if len(third) == 1 else jnp.concatenate(third, axis=1)


def prep_kernel(dims, table_smem, table_ref, length_ref, keep_ref, choice_ref, list_ref, frequency_ref, *refs):
    n_pages, pages_dev, period_heads = dims
    attn_gain_ref, mlp_gain_ref, *refs = refs
    gain_ref, cos_ref, low_ref, high_ref, sel_ref, sel_all_ref, back_ref, pick_ref, number_ref = refs
    gain_ref[0:1, :] = attn_gain_ref[...]
    gain_ref[1:2, :] = mlp_gain_ref[...]
    group = keep_ref.shape[0]
    n_rows = sel_ref.shape[0]
    mine = lax.axis_index("pages")

    ids = table_ref[:, :group]
    for g in range(1, n_pages):
        ids = jnp.where(mine == g, table_ref[:, g * group : (g + 1) * group], ids)
    holder = jnp.floor((ids.astype(F32) + 0.5) * (1.0 / pages_dev)).astype(jnp.int32)

    def one_request(r, rank):
        for j in range(PPR):
            other = table_smem[j, mine * group + r]
            earlier = (holder == lax.div(other, jnp.int32(pages_dev))) & (ids > other)
            rank = rank + jnp.where(earlier, 1, 0)
        return rank

    rank = lax.fori_loop(0, group, one_request, jnp.zeros_like(ids))
    row = jnp.where(rank < 2, 2 * holder + rank, n_rows // 3 * 2 + holder)
    at = iota((n_rows, group), 0)
    hit = None
    for j in range(PPR):
        one = at == row[j : j + 1, :]
        hit = one if hit is None else hit | one
    hit = jnp.where(hit, 1.0, 0.0)
    same = jnp.where(iota((group, group), 0) == iota((group, group), 1), 1.0, 0.0)
    sel_ref[...] = hit.astype(BF16)
    sel_all_ref[:n_rows, :] = hit
    sel_all_ref[n_rows:, :] = same
    turned = row.astype(F32).T
    at = iota((group, n_rows), 1).astype(F32)
    back = jnp.zeros((group, n_rows), F32)
    for j in range(PPR):
        one = jnp.where(at == turned[:, j : j + 1], 1.0, 0.0)
        pick_ref[j * group : (j + 1) * group, :] = one.astype(BF16)
        back = back + one
    back_ref[:, :n_rows] = back.astype(BF16)
    back_ref[:, n_rows:] = same.astype(BF16)

    length = jnp.sum(same * length_ref[...].astype(F32), axis=1, keepdims=True)
    renewed = list_ref[...]
    slot = jnp.zeros_like(renewed)
    for k in range(KP):
        slot = jnp.where(jnp.right_shift(renewed, 4) == k, keep_ref[:, k : k + 1], slot)
    place = (slot * PAGE + jnp.bitwise_and(renewed, PAGE - 1)).astype(F32)
    place = jnp.broadcast_to(place[:, None, :], (group, NREC, NREC)).reshape(group * NREC, NREC)
    shape = (group * NREC, NREC)
    place = jnp.where(jnp.bitwise_and(iota(shape, 0), NREC - 1) == iota(shape, 1), place, 0.0)
    place = jnp.concatenate([length, jnp.sum(place, axis=1, keepdims=True)], axis=0)
    angle = place * frequency_ref[...]
    cosine, sine = jnp.cos(angle), jnp.sin(angle)
    lane = iota(angle.shape, 1)
    low = jnp.where(lane < ROT // 2, -sine, 0.0)
    high = jnp.where((lane >= ROT // 2) & (lane < ROT), sine, 0.0)
    one, none = jnp.ones_like(angle), jnp.zeros_like(angle)
    cos_ref[...] = jnp.concatenate([cosine, cosine, one] * period_heads, axis=1)
    low_ref[...] = jnp.concatenate([low, low, none] * period_heads, axis=1)
    high_ref[...] = jnp.concatenate([high, high, none] * period_heads, axis=1)
    numbers = [length.astype(jnp.int32), keep_ref[...], choice_ref[...], renewed]
    number_ref[...] = jnp.concatenate(numbers, axis=1)


def facts_kernel(dims, *refs):
    n_pages, pages_dev, slots = dims
    number_refs, (table_ref, fold_ref, weight_ref, valid_ref, renew_ref) = refs[:n_pages], refs[n_pages:]
    group = number_refs[0].shape[0]
    requests = n_pages * group
    ranks = n_pages * slots
    mine = lax.axis_index("pages")
    device = lax.axis_index(("pages", "blk"))
    numbers = []
    for g in range(n_pages):
        got = number_refs[0][...]
        for i in range(1, n_pages):
            got = jnp.where(jnp.bitwise_xor(mine, g) == i, number_refs[i][...], got)
        numbers.append(got.astype(F32))
    numbers = jnp.concatenate(numbers, axis=0).astype(BF16)

    local = iota((ranks, requests), 0)
    hits = jnp.zeros((ranks, requests), F32)
    slot = jnp.zeros((ranks, 1), F32)
    for j in range(PPR):
        one = jnp.where(local == table_ref[j : j + 1, :] - device * pages_dev, 1.0, 0.0)
        hits = hits + one
        slot = slot + j * jnp.sum(one, axis=1, keepdims=True)
    hits = jnp.where(local < pages_dev, hits, 0.0)
    facts = dot(hits.astype(BF16), numbers)
    length, keeps = facts[:, :1], facts[:, 1 : 1 + KP]
    choices, renewed = facts[:, 1 + KP : 1 + KP + PPR], facts[:, 1 + KP + PPR : 1 + KP + PPR + NREC]
    place = iota((ranks, PPR), 1).astype(F32)
    choice = jnp.sum(jnp.where(place == slot, choices, 0.0), axis=1, keepdims=True)
    found = jnp.sum(hits, axis=1, keepdims=True) > 0.5
    kept_hit = jnp.where(keeps == slot, 1.0, 0.0)
    kept = (jnp.sum(kept_hit, axis=1, keepdims=True) > 0.5) & found
    kept_place = PAGE * jnp.sum(kept_hit * iota((ranks, KP), 1).astype(F32), axis=1, keepdims=True)
    dropped = jnp.logical_not(kept) & found & (slot * PAGE < length)

    owner = jnp.concatenate(
        [jnp.sum(hits[:, g * group : (g + 1) * group], axis=1, keepdims=True) for g in range(n_pages)], axis=1
    )
    below = jnp.where(iota((ranks, ranks), 0) > iota((ranks, ranks), 1), 1.0, 0.0).astype(BF16)
    before = dot(below, owner.astype(BF16))
    group_of = iota((ranks, n_pages), 1).astype(F32)
    rank = jnp.where(before < 1.5, 2 * group_of + before, 2 * n_pages + group_of)
    rank = jnp.sum(owner * rank, axis=1, keepdims=True)
    rank = jnp.where(found, rank, -1.0)
    rank_hit = jnp.where(rank == iota((ranks, ranks), 1).astype(F32), 1.0, 0.0).astype(BF16)

    weights = jnp.zeros((ranks, PAGE), F32)
    for f in range(NF):
        weights = jnp.where(choice == f, fold_ref[f : f + 1, :], weights)
    live = slot * PAGE + iota((ranks, PAGE), 1).astype(F32) < length
    weights = jnp.where(live & dropped, weights, 0.0)
    weights = jnp.concatenate([weights] * pages_dev, axis=1)
    tokens = pages_dev * PAGE
    own = jnp.right_shift(iota((ranks, tokens), 1), 4) == iota((ranks, tokens), 0)
    weights = jnp.where(own, weights, 0.0)
    total = jnp.zeros((ranks, tokens), F32)
    for part in parts_of(weights, 3):
        total = total + dot_tn(rank_hit, part)
    weight_ref[...] = total

    lanes = valid_ref.shape[1]
    lane_rank = jnp.bitwise_and(iota((ranks, lanes), 1), ranks - 1).astype(F32)
    for_rank = jnp.where(lane_rank == rank, 1.0, 0.0)
    kept_for = jnp.where(kept, for_rank, 0.0)
    dropped_for = jnp.where(dropped, for_rank, 0.0)
    renewed = jnp.concatenate([renewed] * (renew_ref.shape[1] // NREC), axis=1)
    renewed = jnp.where(kept, renewed - kept_place, -1.0)
    inside = iota((PAGE, renew_ref.shape[1]), 0).astype(F32)
    for p in range(pages_dev):
        some = slice(p * PAGE, (p + 1) * PAGE)
        valid_ref[some, :] = jnp.broadcast_to(kept_for[p : p + 1, :], (PAGE, lanes))
        renew_ref[some, :] = jnp.where(inside == renewed[p : p + 1, :], 1.0, 0.0).astype(BF16)
    valid_ref[tokens:, :] = dot_tn(rank_hit, dropped_for.astype(BF16))
    renew_ref[tokens:, :] = jnp.zeros((ranks, renew_ref.shape[1]), BF16)


def pack_kernel(held_ref, new_ref, gain_ref, out_ref):
    group, chunk = new_ref.shape
    held = held_ref[...].astype(F32)
    held = held - jnp.sum(held, axis=1, keepdims=True) / D
    spread = jnp.sum(held * held, axis=1, keepdims=True) / D
    held = held * lax.rsqrt(spread + EPSILON) * gain_ref[...]
    rows = [held[:, c * chunk : (c + 1) * chunk] for c in range(D // chunk)] + [new_ref[...].astype(F32)]
    rows = jnp.concatenate(rows, axis=0).astype(BF16)
    for i in range(out_ref.shape[0]):
        out_ref[i] = rows


def project_kernel(dims, *refs):
    group, n_blk, held_rows, heads = dims
    pack_refs, refs = refs[:2], refs[2:]
    gain_ref, weight_hbm, cos_ref, low_ref, high_ref, sel_ref, *refs = refs
    send_ref, own_ref, leaf_ref, weight_buf, rows_ref, acc_ref, sems = refs
    chunk = D // n_blk
    width = 3 * heads * HD
    head_lanes = heads * HD
    extra = 2 * heads * NREC
    period = cos_ref.shape[1]
    period_heads = period // (3 * HD)
    core = jnp.bitwise_and(lax.axis_index("blk"), 1)

    def weight_copy(part, step):
        return pltpu.make_async_copy(
            weight_hbm.at[pl.ds(step * chunk, chunk), pl.ds(part * period, period)],
            weight_buf.at[part, step],
            sems.at[part, step],
        )

    flight = 6
    for step in range(flight):
        weight_copy(0, step).start()

    pieces, places = [], []
    for other in range(2):
        for z in range(n_blk // 2):
            b = 2 * z + jnp.bitwise_xor(core, other)
            values = pack_refs[other][z].astype(F32)
            pieces.append(values[n_blk * held_rows :])
            places.append(b)
            first = pl.multiple_of(group + b * held_rows, 8)
            for c in range(n_blk):
                rows_ref[c, pl.ds(first, held_rows), :] = values[c * held_rows : (c + 1) * held_rows]
    mean = sum(jnp.sum(piece, axis=1, keepdims=True) for piece in pieces) / D
    pieces = [piece - mean for piece in pieces]
    spread = sum(jnp.sum(piece * piece, axis=1, keepdims=True) for piece in pieces) / D
    spread = lax.rsqrt(spread + EPSILON)
    leaves = []
    for i, (b, piece) in enumerate(zip(places, pieces)):
        z = i % (n_blk // 2)
        some = slice(2 * z * chunk, 2 * (z + 1) * chunk)
        gain = gain_ref[:, some]
        gain = jnp.where(b == 2 * z, gain[:, :chunk], gain[:, chunk:])
        piece = piece * spread
        rows_ref[b, 0:group, :] = piece * gain[0:1]
        leaves.append(piece * gain[1:2])
    leaf_ref[...] = jnp.concatenate(leaves, axis=0).astype(BF16)

    rows = acc_ref.shape[0]
    wide = heads * NREC
    score = jnp.zeros((rows, wide), F32)
    head_at = jnp.right_shift(iota((rows, wide), 1), 3)
    queries, values = [], []
    for j in range(width // period):
        acc_ref[...] = jnp.zeros_like(acc_ref)

        def one_chunk(step, carry, j=j):
            @pl.when(step + flight < n_blk)
            def _():
                weight_copy(j, step + flight).start()

            if j + 1 < width // period:

                @pl.when(step + flight >= n_blk)
                def _():
                    weight_copy(j + 1, step + flight - n_blk).start()

            weight_copy(j, step).wait()
            acc_ref[...] += dot(rows_ref[step].astype(BF16), weight_buf[j, step])
            return carry

        lax.fori_loop(0, n_blk, one_chunk, 0)
        block = acc_ref[...]
        up = jnp.concatenate([block[:, ROT // 2 :], block[:, : ROT // 2]], axis=1)
        down = jnp.concatenate([block[:, -ROT // 2 :], block[:, : -ROT // 2]], axis=1)
        turned = block * cos_ref[...] + up * low_ref[...] + down * high_ref[...]
        turned = turned.astype(BF16).astype(F32)
        for h in range(period_heads):
            first = h * 3 * HD
            query = turned[:group, first : first + HD]
            key = turned[:, first + HD : first + 2 * HD]
            queries.append(query)
            values.append(turned[:group, first + 2 * HD : first + 3 * HD])
            own_product = key[:group] * query
            held_product = key[group:].reshape(group, -1, HD) * query[:, None, :]
            product = jnp.concatenate([own_product, held_product.reshape(rows - group, HD)], axis=0)
            score = jnp.where(
                head_at == j * period_heads + h, jnp.sum(product, axis=1, keepdims=True), score
            )
    score = score * SCALE
    sel = sel_ref[...]
    asked = dot(sel, jnp.concatenate(queries, axis=1).astype(BF16))
    own_ref[:, :head_lanes] = jnp.concatenate(values, axis=1).astype(BF16)

    held_score = score[group:]
    held_count = held_score.shape[0]
    row_id = jnp.bitwise_and(iota((held_count, wide), 0), NREC - 1)
    lane_id = jnp.bitwise_and(iota((held_count, wide), 1), NREC - 1)
    held_score = jnp.where(row_id == lane_id, held_score, 0.0)
    per_request = held_count // group
    spread_ids = jnp.right_shift(iota((group, held_count), 1), per_request.bit_length() - 1)
    spread_rows = jnp.where(spread_ids == iota((group, held_count), 0), 1.0, 0.0).astype(BF16)
    sel_rows = dot(sel, spread_rows).astype(BF16)
    both = jnp.concatenate(parts_of(held_score, 2), axis=1)
    given = dot(sel_rows, both)
    both = jnp.concatenate([asked, given], axis=1).astype(BF16)
    lanes = both.shape[1]
    n_dev = send_ref.shape[0]
    tails = wire_tail(both[2 * n_dev :], lanes)
    for d in range(n_dev):
        send_ref[d, :, :lanes] = both[2 * d : 2 * d + 2]
        send_ref[d, :, lanes:] = tails[2 * d : 2 * d + 2]

    own_score = score[:group]
    lane = iota((group, extra), 1)
    own = jnp.zeros((group, extra), F32)
    for i, part in enumerate(parts_of(own_score, 3)):
        part = part.astype(F32)
        for h in range(heads):
            own = jnp.where(lane == i * heads + h, part[:, h * NREC : h * NREC + 1], own)
    own_ref[:, head_lanes : head_lanes + extra] = own.astype(BF16)


def fold_kernel(weight_ref, page_ref, fold_ref):
    parts = jnp.concatenate(parts_of(weight_ref[...], 3), axis=0)
    rows = weight_ref.shape[0]
    sums = dot(parts, page_ref[...])
    folded = sums[:rows] + sums[rows : 2 * rows] + sums[2 * rows :]
    fold_ref[...] = folded.astype(BF16)


def place_kernel(dims, pick_ref, got_ref, out_ref, rows_ref):
    width, first_lane = dims
    n_dev = got_ref.shape[0]
    for d in range(n_dev):
        rows_ref[2 * d : 2 * d + 2, :] = got_ref[d, :, first_lane:width].astype(F32)
        rows_ref[2 * n_dev + d : 2 * n_dev + d + 1, :] = third_row(got_ref, (d,), width, first_lane, width)
    found = dot(pick_ref[...], rows_ref[...].astype(BF16)).astype(BF16)
    group = out_ref.shape[1]
    for j in range(out_ref.shape[0]):
        out_ref[j] = found[j * group : (j + 1) * group]


def attend_kernel(dims, ask_ref, valid_ref, place_ref, page_hbm, fold_ref, send_ref, page_buf, sems):
    n_pages, slots, dests, heads = dims
    rows = n_pages * slots
    head_lanes = heads * HD
    extra = 2 * heads * NREC
    tokens = page_hbm.shape[0]
    octets = range(ATTEND_HEADS // OCTET)
    octet_lanes = OCTET * 2 * HD

    def page_copy(o):
        return pltpu.make_async_copy(
            page_hbm.at[:, pl.ds(o * octet_lanes, octet_lanes)], page_buf.at[o], sems.at[o]
        )

    for o in octets:
        page_copy(o).start()
    width = head_lanes + extra
    asks = []
    for b in range(dests):
        pairs = [ask_ref[g, b, :, :width].astype(F32) for g in range(n_pages)]
        thirds = [third_row(ask_ref, (g, b), width, 0, width) for g in range(n_pages)]
        asks.append(jnp.concatenate([*pairs, *thirds, jnp.zeros((rows - 3 * n_pages, width), F32)], axis=0))
    query = jnp.concatenate([a[:, :head_lanes] for a in asks], axis=1)
    given = jnp.concatenate([a[:, head_lanes : head_lanes + extra] for a in asks], axis=1)
    valid = valid_ref[...] > 0.5
    place = place_ref[...]
    touched = jnp.sum(place[:, :NREC].astype(F32), axis=1, keepdims=True) > 0.5
    lanes = OCTET * rows
    shift = rows.bit_length() - 1
    lane_head = jnp.right_shift(iota((HD, lanes), 1), shift)
    blank = jnp.zeros((HD, lanes), F32)
    lane = iota((lanes, lanes), 1)
    lane_in = jnp.bitwise_and(lane, extra - 1)
    lane_dest = jnp.right_shift(lane, extra.bit_length() - 1) * heads
    given_head = jnp.right_shift(jnp.bitwise_and(lane_in, heads * NREC - 1), 3) + lane_dest
    row_head = jnp.right_shift(iota((lanes, lanes), 0), shift)
    own_lane = jnp.bitwise_and(iota((rows, lanes), 1), rows - 1) == iota((rows, lanes), 0)
    goals = []
    for i in range(3):
        hit = (lane_in >= i * heads) & (lane_in < (i + 1) * heads)
        hit = hit & (row_head == lane_dest + lane_in - i * heads)
        goals.append(jnp.where(hit, 1.0, 0.0).astype(BF16))
    all_scores = []
    for o in octets:
        heads_here = range(o * OCTET, (o + 1) * OCTET)
        asked = jnp.concatenate([query[:, h * HD : (h + 1) * HD] for h in heads_here], axis=0)
        asked = jnp.concatenate([asked, jnp.zeros((lanes, 128 - HD), F32)], axis=1).T[:HD]
        stacked = []
        for h in range(OCTET):
            stacked += [jnp.where(lane_head == h, asked, 0.0), blank]
        stacked = jnp.concatenate(stacked, axis=0).astype(BF16)
        told = jnp.concatenate([given[:, o * lanes : (o + 1) * lanes]] * OCTET, axis=0)
        told = jnp.where(given_head == row_head, told, 0.0).T.astype(BF16)
        page_copy(o).wait()
        page = jnp.concatenate([page_buf[o], fold_ref[:, o * octet_lanes : (o + 1) * octet_lanes]], axis=0)
        all_scores.append(jnp.where(touched, dot(place, told), dot(page, stacked) * SCALE))
    all_weights, extras = [], []
    for scores in all_scores:
        scores = jnp.where(valid, scores, NEVER)
        top = jnp.max(scores, axis=0, keepdims=True)
        weights = jnp.where(valid, jnp.exp(scores - top), 0.0)
        total = jnp.sum(weights, axis=0, keepdims=True)
        safe = jnp.where(total > 0.0, total, 1.0)
        rest = jnp.zeros((256 - weights.shape[0], lanes), F32)
        all_weights.append(jnp.concatenate([weights * (1.0 / safe), rest], axis=0).T.astype(BF16))
        lse = jnp.where(own_lane, jnp.where(total > 0.0, top + jnp.log(safe), NEVER), 0.0)
        spread = jnp.zeros((rows, lanes), F32)
        for part, goal in zip(parts_of(lse, 3), goals):
            spread = spread + dot(part, goal)
        extras.append(spread)
    gathered = []
    for o in octets:
        for i in range(OCTET // QUAD):
            quad_lanes = QUAD * 2 * HD
            first = o * octet_lanes + i * quad_lanes
            page = [page_buf[o, :, i * quad_lanes : (i + 1) * quad_lanes], fold_ref[:, first : first + quad_lanes]]
            page.append(jnp.zeros((256 - tokens - rows, QUAD * 2 * HD), BF16))
            mixed = dot(all_weights[o][i * QUAD * rows : (i + 1) * QUAD * rows], jnp.concatenate(page, axis=0))
            for h in range(QUAD):
                gathered.append(mixed[h * rows : (h + 1) * rows, 2 * HD * h + HD : 2 * HD * (h + 1)])
    gathered = jnp.concatenate(gathered, axis=1)
    extras = jnp.concatenate(extras, axis=1)
    fold_lanes = 2 * head_lanes
    all_lanes = width + fold_lanes
    for b in range(dests):
        whole = jnp.concatenate(
            [
                gathered[:, b * head_lanes : (b + 1) * head_lanes].astype(BF16),
                extras[:, b * extra : (b + 1) * extra].astype(BF16),
                fold_ref[:, b * fold_lanes : (b + 1) * fold_lanes],
            ],
            axis=1,
        )
        tails = wire_tail(whole[2 * n_pages : 3 * n_pages], all_lanes)
        for g in range(n_pages):
            send_ref[g, b, :, :all_lanes] = whole[2 * g : 2 * g + 2]
            send_ref[g, b, :, all_lanes:] = tails[2 * g : 2 * g + 2]


def merge_kernel(
    dims, got_ref, own_ref, sel_ref, back_ref, *refs
):
    group, n_dev, heads, n_pages = dims
    share_refs, dense_hbm, refs = refs[:n_pages], refs[n_pages], refs[n_pages + 1 :]
    head_lanes = heads * HD
    extra = 2 * heads * NREC
    n_blk = n_dev // n_pages
    out_ref, dense_buf, rows_ref, sems = refs
    chunk = D // n_blk
    steps, _, cols = dense_buf.shape

    def dense_copy(step):
        return pltpu.make_async_copy(
            dense_hbm.at[:, pl.ds(step * cols, cols)], dense_buf.at[step], sems.at[step]
        )

    for step in range(steps):
        dense_copy(step).start()
    for d in range(n_dev):
        rows_ref[2 * d : 2 * d + 2, :] = got_ref[d, :, : head_lanes + extra].astype(F32)
        rows_ref[2 * n_dev + d : 2 * n_dev + d + 1, :] = third_row(
            got_ref, (d,), 3 * head_lanes + extra, 0, head_lanes + extra
        )
    rows_ref[3 * n_dev :, :] = own_ref[...].astype(F32)
    count = rows_ref.shape[0]
    parts = rows_ref[:, head_lanes : head_lanes + extra].astype(BF16)
    to, source = iota((extra, 128), 1), iota((extra, 128), 0)
    hit = None
    for i in range(3):
        one = (to < heads) & (source == to + i * heads)
        hit = one if hit is None else hit | one
    lse = dot(parts, jnp.where(hit, 1.0, 0.0).astype(BF16))
    tops = jnp.zeros((count, 128), F32)
    for r in range(group):
        mine = sel_ref[:, r : r + 1] > 0.5
        top = jnp.max(jnp.where(mine, lse, -3e38), axis=0, keepdims=True)
        tops = jnp.where(mine, top, tops)
    weights = jnp.exp(jnp.minimum(lse - tops, 0.0))
    back = back_ref[...]
    totals = jnp.zeros((group, 128), F32)
    for part in parts_of(weights, 3):
        totals = totals + dot(back, part)
    lanes, heads_of = iota((128, head_lanes), 1), iota((128, head_lanes), 0)
    over = lanes - heads_of * HD
    spread = jnp.where((over >= 0) & (over < HD), 1.0, 0.0).astype(BF16)
    weighted = split_dot(weights, spread, 2) * rows_ref[:, :head_lanes]
    inverse = split_dot(1.0 / totals, spread, 3)
    mixed = jnp.zeros((group, head_lanes), F32)
    for part in parts_of(weighted, 2):
        mixed = mixed + dot(back, part)
    attended = (mixed * inverse).astype(BF16)
    for step in range(steps):
        dense_copy(step).wait()
        some = slice(step * cols, (step + 1) * cols)
        result = dot(attended, dense_buf[step])
        for share_ref in share_refs:
            result = result + share_ref[:, some].astype(F32)
        for i in range(cols // chunk):
            out_ref[step * (cols // chunk) + i] = result[:, i * chunk : (i + 1) * chunk].astype(BF16)


def mlp_kernel(dims, *refs):
    group, n_pages, n_blk = dims
    leaf_refs, refs = refs[:n_pages], refs[n_pages:]
    in_hbm, out_hbm, _, *refs = refs
    part_refs, (in_buf, out_buf, sems_in, sems_out) = refs[:n_pages], refs[n_pages:]
    chunk = D // n_blk
    n_steps, cols = out_buf.shape[0], out_buf.shape[2]
    core = jnp.bitwise_and(lax.axis_index("blk"), 1)

    def in_copy(step):
        return pltpu.make_async_copy(
            in_hbm.at[pl.ds(step * chunk, chunk), :], in_buf.at[step], sems_in.at[step]
        )

    def out_copy(step):
        return pltpu.make_async_copy(
            out_hbm.at[:, pl.ds(step * cols, cols)], out_buf.at[step], sems_out.at[step]
        )

    copies = [in_copy(step) for step in range(n_blk)] + [out_copy(step) for step in range(n_steps)]
    flight = 4
    for copy in copies[:flight]:
        copy.start()

    def arrived(step):
        copies[step].wait()
        if step + flight < len(copies):
            copies[step + flight].start()

    leaves = [ref[...].astype(F32) for ref in leaf_refs]
    half = n_blk // 2
    hidden = jnp.zeros((n_pages * group, in_buf.shape[2]), F32)
    for z in range(half):
        arrived(2 * z)
        arrived(2 * z + 1)
        for i, c in ((z, 2 * z + core), (half + z, 2 * z + 1 - core)):
            rows = [leaf[i * group : (i + 1) * group] for leaf in leaves]
            hidden = hidden + dot(jnp.concatenate(rows, axis=0).astype(BF16), in_buf[c])
    active = (0.5 * hidden * (1.0 + lax.erf(hidden * math.sqrt(0.5)))).astype(BF16)
    for step in range(n_steps):
        arrived(n_blk + step)
        result = dot(active, out_buf[step]).astype(BF16)
        for g in range(n_pages):
            part_refs[g][:, step * cols : (step + 1) * cols] = result[g * group : (g + 1) * group]


VMEM = pl.BlockSpec(memory_space=pltpu.VMEM)
HBM = pl.BlockSpec(memory_space=pltpu.HBM)
ANY = pl.BlockSpec(memory_space=pl.ANY)


def shape_of(shape, kind=BF16):
    return jax.ShapeDtypeStruct(shape, kind)


def params_of(mib):
    return pltpu.CompilerParams(vmem_limit_bytes=mib * MIB)


def cost_of(flops, nbytes):
    return pl.CostEstimate(flops=int(flops), bytes_accessed=int(nbytes), transcendentals=0)


def on_device(
    new_hidden,
    attn_gain,
    mlp_gain,
    qkv_weight,
    dense_weight,
    in_weight,
    out_weight,
    page_store,
    held_states,
    fold_weights,
    page_table,
    lengths,
    keep_slots,
    fold_index,
    recompute_list,
):
    n_pages = lax.axis_size("pages")
    n_blk = lax.axis_size("blk")
    n_dev = n_pages * n_blk
    mine = lax.axis_index("pages")
    device = lax.axis_index(("pages", "blk"))
    group = lengths.shape[0]
    pages_dev = page_store.shape[0]
    slots = -(-(pages_dev // n_pages) // 4) * 4
    ranks = n_pages * slots
    heads = H // n_blk
    head_lanes = heads * HD
    extra = 2 * heads * NREC
    lanes = head_lanes + extra
    chunk = D // n_blk
    held_rows = held_states.shape[0] * NREC
    kept_count = KP * PAGE

    def swapped(array, axis, size, by):
        return lax.ppermute(array, axis, [(i, i ^ by) for i in range(size)])

    def swapped(array, axis, size, by):
        return lax.ppermute(array, axis, [(i, i ^ by) for i in range(size)])

    def fixed(array):
        return pltpu.with_memory_space_constraint(array, pltpu.HBM)

    half = n_blk // 2
    pack = pl.pallas_call(
        pack_kernel,
        in_specs=[VMEM] * 3,
        out_specs=VMEM,
        out_shape=shape_of((half, n_blk * held_rows + group, chunk)),
        compiler_params=params_of(16),
        name="pack",
    )(fixed(held_states.reshape(held_rows, D)), fixed(new_hidden), fixed(attn_gain[None]))
    pack = lax.all_to_all(
        pack,
        "blk",
        0,
        0,
        axis_index_groups=[list(range(core, n_blk, 2)) for core in range(2)],
        tiled=True,
    )

    n_rows = n_dev * 3
    rows = group * (1 + NREC)
    period = 12 * HD if (3 * head_lanes) % (12 * HD) == 0 else 3 * head_lanes
    lane = np.arange(HD)
    frequency = np.where(lane < ROT, ROT_BASE ** (-2.0 * (lane % (ROT // 2)) / ROT), 0.0).astype(np.float32)
    gains, cosine, low, high, sel, sel_all, back, pick, numbers = pl.pallas_call(
        functools.partial(prep_kernel, (n_pages, pages_dev, period // (3 * HD))),
        in_specs=[pl.BlockSpec(memory_space=pltpu.SMEM)] + [VMEM] * 8,
        out_specs=[VMEM] * 9,
        out_shape=[
            shape_of((2, D), F32),
            *[shape_of((rows, period), F32)] * 3,
            shape_of((n_rows, group)),
            shape_of((n_rows + group, group), F32),
            shape_of((group, n_rows + group)),
            shape_of((PPR * group, n_rows)),
            shape_of((group, 1 + KP + PPR + NREC), jnp.int32),
        ],
        compiler_params=params_of(16),
        cost_estimate=cost_of(0, 0),
        name="prep",
    )(
        page_table.T,
        fixed(page_table.T),
        fixed(lengths[None]),
        fixed(keep_slots),
        fixed(fold_index),
        fixed(recompute_list),
        fixed(jnp.asarray(frequency[None])),
        fixed(attn_gain[None]),
        fixed(mlp_gain[None]),
    )

    numbers = [numbers] + [swapped(numbers, "pages", n_pages, i) for i in range(1, n_pages)]

    tokens = pages_dev * PAGE
    pages = page_store.reshape(tokens, 2 * D)
    steps = H // STEP_HEADS
    step_lanes = STEP_HEADS * 2 * HD
    fold_width = 2 * head_lanes

    pack, cosine = lax.optimization_barrier((pack, cosine))
    packs = [pack, swapped(pack, "blk", n_blk, 1)]

    wire = lanes + wire_split(lanes)
    send, own, leaf = pl.pallas_call(
        functools.partial(project_kernel, (group, n_blk, held_rows, heads)),
        in_specs=[VMEM] * 3 + [HBM] + [VMEM] * 4,
        out_specs=[VMEM] * 3,
        out_shape=[
            shape_of((n_dev, 2, wire)),
            shape_of((group, lanes)),
            shape_of((n_blk * group, chunk)),
        ],
        scratch_shapes=[
            pltpu.VMEM((3 * head_lanes // period, n_blk, chunk, period), BF16),
            pltpu.VMEM((n_blk, rows, chunk), F32),
            pltpu.VMEM((rows, period), F32),
            pltpu.SemaphoreType.DMA((3 * head_lanes // period, n_blk)),
        ],
        compiler_params=params_of(50),
        cost_estimate=cost_of(2 * rows * D * 3 * head_lanes, 6 * D * head_lanes),
        name="project",
    )(
        *packs,
        gains,
        fixed(qkv_weight),
        cosine,
        low,
        high,
        sel,
    )
    send, *numbers = lax.optimization_barrier((send, *numbers))
    asked = lax.all_to_all(send, ("pages", "blk"), 0, 0, tiled=True)
    fold_rows, valid, renew = pl.pallas_call(
        functools.partial(facts_kernel, (n_pages, pages_dev, slots)),
        in_specs=[VMEM] * (n_pages + 2),
        out_specs=[VMEM] * 3,
        out_shape=[
            shape_of((ranks, tokens), F32),
            shape_of((tokens + ranks, OCTET * ranks), F32),
            shape_of((tokens + ranks, 2 * OCTET * NREC)),
        ],
        compiler_params=params_of(16),
        cost_estimate=cost_of(0, 0),
        name="facts",
    )(*numbers, fixed(page_table.T), fixed(fold_weights))

    leaf, fold_rows = lax.optimization_barrier((leaf, fold_rows))
    leaves = [leaf] + [swapped(leaf, "pages", n_pages, i) for i in range(1, n_pages)]

    folded_rows = pl.pallas_call(
        fold_kernel,
        grid=(steps,),
        in_specs=[
            pl.BlockSpec((ranks, tokens), lambda i: (0, 0)),
            pl.BlockSpec((tokens, step_lanes), lambda i: (0, i)),
        ],
        out_specs=pl.BlockSpec((ranks, step_lanes), lambda i: (0, i)),
        out_shape=shape_of((ranks, 2 * D)),
        compiler_params=params_of(16),
        cost_estimate=cost_of(0, 0),
        name="fold",
    )(fold_rows, fixed(pages))

    all_lanes = lanes + fold_width
    all_wire = all_lanes + wire_split(all_lanes)
    partial = pl.pallas_call(
        functools.partial(attend_kernel, (n_pages, slots, n_blk, heads)),
        in_specs=[VMEM, VMEM, VMEM, HBM, VMEM],
        out_specs=VMEM,
        out_shape=shape_of((n_pages, n_blk, 2, all_wire)),
        scratch_shapes=[
            pltpu.VMEM((H // OCTET, tokens, OCTET * 2 * HD), BF16),
            pltpu.SemaphoreType.DMA((H // OCTET,)),
        ],
        compiler_params=params_of(32),
        cost_estimate=cost_of(2 * 128 * tokens * 2 * D, tokens * 4 * D),
        name="attend",
    )(asked.reshape(n_pages, n_blk, 2, wire), valid, renew, fixed(pages), folded_rows)
    partial, *leaves = lax.optimization_barrier((partial, *leaves))
    got = lax.all_to_all(partial.reshape(n_dev, 2, all_wire), ("pages", "blk"), 0, 0, tiled=True)

    hidden = in_weight.shape[1]
    mlp_parts = pl.pallas_call(
        functools.partial(mlp_kernel, (group, n_pages, n_blk)),
        in_specs=[VMEM] * n_pages + [HBM, HBM, ANY],
        out_specs=[VMEM] * n_pages,
        out_shape=[shape_of((group, D))] * n_pages,
        scratch_shapes=[
            pltpu.VMEM((n_blk, chunk, hidden), BF16),
            pltpu.VMEM((8, hidden, D // 8), BF16),
            pltpu.SemaphoreType.DMA((n_blk,)),
            pltpu.SemaphoreType.DMA((8,)),
        ],
        compiler_params=params_of(24),
        cost_estimate=cost_of(4 * n_pages * group * D * hidden, 4 * D * hidden),
        name="mlp",
    )(*leaves, fixed(in_weight), fixed(out_weight), partial)
    mlp_share = [mlp_parts[0]] + [swapped(mlp_parts[i], "pages", n_pages, i) for i in range(1, n_pages)]

    out_part = pl.pallas_call(
        functools.partial(merge_kernel, (group, n_dev, heads, n_pages)),
        in_specs=[VMEM] * (n_pages + 4) + [HBM],
        out_specs=VMEM,
        out_shape=shape_of((n_blk, group, chunk)),
        scratch_shapes=[
            pltpu.VMEM((8, head_lanes, D // 8), BF16),
            pltpu.VMEM((n_rows + group, lanes), F32),
            pltpu.SemaphoreType.DMA((8,)),
        ],
        compiler_params=params_of(24),
        cost_estimate=cost_of(2 * group * D * head_lanes, 2 * D * head_lanes),
        name="merge",
    )(
        got,
        own,
        sel_all,
        back,
        *mlp_share,
        fixed(dense_weight),
    )
    out_got = lax.all_to_all(out_part, "blk", 0, 0, tiled=True)
    summed = jnp.sum(out_got.astype(F32), axis=0).astype(BF16)

    folded = pl.pallas_call(
        functools.partial(place_kernel, (all_lanes, lanes)),
        in_specs=[VMEM, VMEM],
        out_specs=VMEM,
        out_shape=shape_of((PPR, group, fold_width)),
        scratch_shapes=[pltpu.VMEM((n_rows, fold_width), F32)],
        compiler_params=params_of(16),
        cost_estimate=cost_of(0, 4 * n_rows * fold_width),
        name="place",
    )(pick, got)
    folded = jnp.transpose(folded, (1, 0, 2))
    return (summed, folded)


def solution(mesh):
    in_specs = (
        P("pages", "blk"),
        P(),
        P(),
        P(None, "blk"),
        P("blk", None),
        P(None, ("pages", "blk")),
        P(("pages", "blk"), None),
        P(("pages", "blk"), None, None),
        P(("pages", "blk"), None, None),
        P(),
        P(),
        P("pages"),
        P("pages", None),
        P("pages", None),
        P("pages", None),
    )
    out_specs = (P("pages", "blk"), P("pages", None, "blk"))
    return jax.shard_map(
        on_device, mesh=mesh, in_specs=in_specs, out_specs=out_specs, check_vma=False
    )
```

```python
import functools
import math

import jax
import jax.numpy as jnp
import numpy as np
from jax import lax
from jax.experimental import pallas as pl
from jax.experimental.pallas import tpu as pltpu
from jax.sharding import PartitionSpec as P

D = 6144
H = 64
HD = 96
ROT = 24
PAGE = 16
PPR = 12
KP = 5
NREC = 8
NF = 8
FF = 24576

EPSILON = 1e-05
ROT_BASE = 10000.0
NEVER = -1e30
F32 = jnp.float32
BF16 = jnp.bfloat16
SCALE = 1.0 / math.sqrt(HD)
MIB = 1024 * 1024
STEP_HEADS = 32
QUAD = 4
OCTET = 8


def iota(shape, axis):
    return lax.broadcasted_iota(jnp.int32, shape, axis)


def dot(left, right):
    return jnp.dot(left, right, preferred_element_type=F32)


def dot_nt(left, right):
    return lax.dot_general(left, right, (((1,), (1,)), ((), ())), preferred_element_type=F32)


def dot_tn(left, right):
    return lax.dot_general(left, right, (((0,), (0,)), ((), ())), preferred_element_type=F32)


def parts_of(values, count):
    parts = []
    for _ in range(count):
        part = values.astype(BF16)
        parts.append(part)
        values = values - part.astype(F32)
    return parts


def split_dot(values, selector, count):
    total = None
    for part in parts_of(values, count):
        term = dot(part, selector)
        total = term if total is None else total + term
    return total


def wire_split(width):
    return (width // 128 + 1) // 2 * 128 if width % 128 == 0 else (width + 1) // 2


def wire_tail(thirds, width):
    first = wire_split(width)
    count = thirds.shape[0]
    at, of = iota((2 * count, count), 0), iota((2 * count, count), 1)
    upper = jnp.where(at == 2 * of, 1.0, 0.0).astype(BF16)
    lower = jnp.where(at == 2 * of + 1, 1.0, 0.0).astype(BF16)
    rest = thirds[:, first:]
    if width < 2 * first:
        rest = jnp.concatenate([rest, jnp.zeros((count, 2 * first - width), BF16)], axis=1)
    return (dot(upper, thirds[:, :first]) + dot(lower, rest)).astype(BF16)


def third_row(ref, index, width, start, stop):
    first = wire_split(width)
    third = []
    if start < first:
        third.append(ref[(*index, slice(0, 1), slice(width + start, width + min(stop, first)))].astype(F32))
    if stop > first:
        begin = max(start, first) - first
        third.append(ref[(*index, slice(1, 2), slice(width + begin, width + stop - first))].astype(F32))
    return third[0] if len(third) == 1 else jnp.concatenate(third, axis=1)


def prep_kernel(dims, table_smem, table_ref, length_ref, keep_ref, choice_ref, list_ref, frequency_ref, *refs):
    n_pages, pages_dev, period_heads = dims
    attn_gain_ref, mlp_gain_ref, *refs = refs
    gain_ref, cos_ref, low_ref, high_ref, sel_ref, sel_all_ref, back_ref, pick_ref, number_ref = refs
    gain_ref[0:1, :] = attn_gain_ref[...]
    gain_ref[1:2, :] = mlp_gain_ref[...]
    group = keep_ref.shape[0]
    n_rows = sel_ref.shape[0]
    mine = lax.axis_index("pages")

    ids = table_ref[:, :group]
    for g in range(1, n_pages):
        ids = jnp.where(mine == g, table_ref[:, g * group : (g + 1) * group], ids)
    holder = jnp.floor((ids.astype(F32) + 0.5) * (1.0 / pages_dev)).astype(jnp.int32)

    def one_request(r, rank):
        for j in range(PPR):
            other = table_smem[j, mine * group + r]
            earlier = (holder == lax.div(other, jnp.int32(pages_dev))) & (ids > other)
            rank = rank + jnp.where(earlier, 1, 0)
        return rank

    rank = lax.fori_loop(0, group, one_request, jnp.zeros_like(ids))
    row = jnp.where(rank < 2, 2 * holder + rank, n_rows // 3 * 2 + holder)
    at = iota((n_rows, group), 0)
    hit = None
    for j in range(PPR):
        one = at == row[j : j + 1, :]
        hit = one if hit is None else hit | one
    hit = jnp.where(hit, 1.0, 0.0)
    same = jnp.where(iota((group, group), 0) == iota((group, group), 1), 1.0, 0.0)
    sel_ref[...] = hit.astype(BF16)
    sel_all_ref[:n_rows, :] = hit
    sel_all_ref[n_rows:, :] = same
    turned = row.astype(F32).T
    at = iota((group, n_rows), 1).astype(F32)
    back = jnp.zeros((group, n_rows), F32)
    for j in range(PPR):
        one = jnp.where(at == turned[:, j : j + 1], 1.0, 0.0)
        pick_ref[j * group : (j + 1) * group, :] = one.astype(BF16)
        back = back + one
    back_ref[:, :n_rows] = back.astype(BF16)
    back_ref[:, n_rows:] = same.astype(BF16)

    length = jnp.sum(same * length_ref[...].astype(F32), axis=1, keepdims=True)
    renewed = list_ref[...]
    slot = jnp.zeros_like(renewed)
    for k in range(KP):
        slot = jnp.where(jnp.right_shift(renewed, 4) == k, keep_ref[:, k : k + 1], slot)
    place = (slot * PAGE + jnp.bitwise_and(renewed, PAGE - 1)).astype(F32)
    place = jnp.broadcast_to(place[:, None, :], (group, NREC, NREC)).reshape(group * NREC, NREC)
    shape = (group * NREC, NREC)
    place = jnp.where(jnp.bitwise_and(iota(shape, 0), NREC - 1) == iota(shape, 1), place, 0.0)
    place = jnp.concatenate([length, jnp.sum(place, axis=1, keepdims=True)], axis=0)
    angle = place * frequency_ref[...]
    cosine, sine = jnp.cos(angle), jnp.sin(angle)
    lane = iota(angle.shape, 1)
    low = jnp.where(lane < ROT // 2, -sine, 0.0)
    high = jnp.where((lane >= ROT // 2) & (lane < ROT), sine, 0.0)
    one, none = jnp.ones_like(angle), jnp.zeros_like(angle)
    cos_ref[...] = jnp.concatenate([cosine, cosine, one] * period_heads, axis=1)
    low_ref[...] = jnp.concatenate([low, low, none] * period_heads, axis=1)
    high_ref[...] = jnp.concatenate([high, high, none] * period_heads, axis=1)
    numbers = [length.astype(jnp.int32), keep_ref[...], choice_ref[...], renewed]
    number_ref[...] = jnp.concatenate(numbers, axis=1)


def facts_kernel(dims, *refs):
    n_pages, pages_dev, slots = dims
    number_refs, (table_ref, fold_ref, weight_ref, valid_ref, renew_ref) = refs[:n_pages], refs[n_pages:]
    group = number_refs[0].shape[0]
    requests = n_pages * group
    ranks = n_pages * slots
    mine = lax.axis_index("pages")
    device = lax.axis_index(("pages", "blk"))
    numbers = []
    for g in range(n_pages):
        got = number_refs[0][...]
        for i in range(1, n_pages):
            got = jnp.where(jnp.bitwise_xor(mine, g) == i, number_refs[i][...], got)
        numbers.append(got.astype(F32))
    numbers = jnp.concatenate(numbers, axis=0).astype(BF16)

    local = iota((ranks, requests), 0)
    hits = jnp.zeros((ranks, requests), F32)
    slot = jnp.zeros((ranks, 1), F32)
    for j in range(PPR):
        one = jnp.where(local == table_ref[j : j + 1, :] - device * pages_dev, 1.0, 0.0)
        hits = hits + one
        slot = slot + j * jnp.sum(one, axis=1, keepdims=True)
    hits = jnp.where(local < pages_dev, hits, 0.0)
    facts = dot(hits.astype(BF16), numbers)
    length, keeps = facts[:, :1], facts[:, 1 : 1 + KP]
    choices, renewed = facts[:, 1 + KP : 1 + KP + PPR], facts[:, 1 + KP + PPR : 1 + KP + PPR + NREC]
    place = iota((ranks, PPR), 1).astype(F32)
    choice = jnp.sum(jnp.where(place == slot, choices, 0.0), axis=1, keepdims=True)
    found = jnp.sum(hits, axis=1, keepdims=True) > 0.5
    kept_hit = jnp.where(keeps == slot, 1.0, 0.0)
    kept = (jnp.sum(kept_hit, axis=1, keepdims=True) > 0.5) & found
    kept_place = PAGE * jnp.sum(kept_hit * iota((ranks, KP), 1).astype(F32), axis=1, keepdims=True)
    dropped = jnp.logical_not(kept) & found & (slot * PAGE < length)

    owner = jnp.concatenate(
        [jnp.sum(hits[:, g * group : (g + 1) * group], axis=1, keepdims=True) for g in range(n_pages)], axis=1
    )
    below = jnp.where(iota((ranks, ranks), 0) > iota((ranks, ranks), 1), 1.0, 0.0).astype(BF16)
    before = dot(below, owner.astype(BF16))
    group_of = iota((ranks, n_pages), 1).astype(F32)
    rank = jnp.where(before < 1.5, 2 * group_of + before, 2 * n_pages + group_of)
    rank = jnp.sum(owner * rank, axis=1, keepdims=True)
    rank = jnp.where(found, rank, -1.0)
    rank_hit = jnp.where(rank == iota((ranks, ranks), 1).astype(F32), 1.0, 0.0).astype(BF16)

    weights = jnp.zeros((ranks, PAGE), F32)
    for f in range(NF):
        weights = jnp.where(choice == f, fold_ref[f : f + 1, :], weights)
    live = slot * PAGE + iota((ranks, PAGE), 1).astype(F32) < length
    weights = jnp.where(live & dropped, weights, 0.0)
    weights = jnp.concatenate([weights] * pages_dev, axis=1)
    tokens = pages_dev * PAGE
    own = jnp.right_shift(iota((ranks, tokens), 1), 4) == iota((ranks, tokens), 0)
    weights = jnp.where(own, weights, 0.0)
    total = jnp.zeros((ranks, tokens), F32)
    for part in parts_of(weights, 3):
        total = total + dot_tn(rank_hit, part)
    weight_ref[...] = total

    lanes = valid_ref.shape[1]
    lane_rank = jnp.bitwise_and(iota((ranks, lanes), 1), ranks - 1).astype(F32)
    for_rank = jnp.where(lane_rank == rank, 1.0, 0.0)
    kept_for = jnp.where(kept, for_rank, 0.0)
    dropped_for = jnp.where(dropped, for_rank, 0.0)
    renewed = jnp.concatenate([renewed] * (renew_ref.shape[1] // NREC), axis=1)
    renewed = jnp.where(kept, renewed - kept_place, -1.0)
    inside = iota((PAGE, renew_ref.shape[1]), 0).astype(F32)
    for p in range(pages_dev):
        some = slice(p * PAGE, (p + 1) * PAGE)
        valid_ref[some, :] = jnp.broadcast_to(kept_for[p : p + 1, :], (PAGE, lanes))
        renew_ref[some, :] = jnp.where(inside == renewed[p : p + 1, :], 1.0, 0.0).astype(BF16)
    valid_ref[tokens:, :] = dot_tn(rank_hit, dropped_for.astype(BF16))
    renew_ref[tokens:, :] = jnp.zeros((ranks, renew_ref.shape[1]), BF16)


def pack_kernel(held_ref, new_ref, gain_ref, out_ref):
    group, chunk = new_ref.shape
    held = held_ref[...].astype(F32)
    held = held - jnp.sum(held, axis=1, keepdims=True) / D
    spread = jnp.sum(held * held, axis=1, keepdims=True) / D
    held = held * lax.rsqrt(spread + EPSILON) * gain_ref[...]
    rows = [held[:, c * chunk : (c + 1) * chunk] for c in range(D // chunk)] + [new_ref[...].astype(F32)]
    rows = jnp.concatenate(rows, axis=0).astype(BF16)
    for i in range(out_ref.shape[0]):
        out_ref[i] = rows


def project_kernel(dims, *refs):
    group, n_blk, held_rows, heads = dims
    pack_refs, refs = refs[:2], refs[2:]
    gain_ref, weight_hbm, cos_ref, low_ref, high_ref, sel_ref, *refs = refs
    send_ref, own_ref, leaf_ref, weight_buf, rows_ref, acc_ref, sems = refs
    chunk = D // n_blk
    width = 3 * heads * HD
    head_lanes = heads * HD
    extra = 2 * heads * NREC
    period = cos_ref.shape[1]
    period_heads = period // (3 * HD)
    core = jnp.bitwise_and(lax.axis_index("blk"), 1)

    def weight_copy(part, step):
        return pltpu.make_async_copy(
            weight_hbm.at[pl.ds(step * chunk, chunk), pl.ds(part * period, period)],
            weight_buf.at[part, step],
            sems.at[part, step],
        )

    flight = 6
    for step in range(flight):
        weight_copy(0, step).start()

    pieces, places = [], []
    for other in range(2):
        for z in range(n_blk // 2):
            b = 2 * z + jnp.bitwise_xor(core, other)
            values = pack_refs[other][z].astype(F32)
            pieces.append(values[n_blk * held_rows :])
            places.append(b)
            first = pl.multiple_of(group + b * held_rows, 8)
            for c in range(n_blk):
                rows_ref[c, pl.ds(first, held_rows), :] = values[c * held_rows : (c + 1) * held_rows]
    mean = sum(jnp.sum(piece, axis=1, keepdims=True) for piece in pieces) / D
    pieces = [piece - mean for piece in pieces]
    spread = sum(jnp.sum(piece * piece, axis=1, keepdims=True) for piece in pieces) / D
    spread = lax.rsqrt(spread + EPSILON)
    leaves = []
    for i, (b, piece) in enumerate(zip(places, pieces)):
        z = i % (n_blk // 2)
        some = slice(2 * z * chunk, 2 * (z + 1) * chunk)
        gain = gain_ref[:, some]
        gain = jnp.where(b == 2 * z, gain[:, :chunk], gain[:, chunk:])
        piece = piece * spread
        rows_ref[b, 0:group, :] = piece * gain[0:1]
        leaves.append(piece * gain[1:2])
    leaf_ref[...] = jnp.concatenate(leaves, axis=0).astype(BF16)

    rows = acc_ref.shape[0]
    wide = heads * NREC
    score = jnp.zeros((rows, wide), F32)
    head_at = jnp.right_shift(iota((rows, wide), 1), 3)
    queries, values = [], []
    for j in range(width // period):
        acc_ref[...] = jnp.zeros_like(acc_ref)

        def one_chunk(step, carry, j=j):
            @pl.when(step + flight < n_blk)
            def _():
                weight_copy(j, step + flight).start()

            if j + 1 < width // period:

                @pl.when(step + flight >= n_blk)
                def _():
                    weight_copy(j + 1, step + flight - n_blk).start()

            weight_copy(j, step).wait()
            acc_ref[...] += dot(rows_ref[step].astype(BF16), weight_buf[j, step])
            return carry

        lax.fori_loop(0, n_blk, one_chunk, 0)
        block = acc_ref[...]
        up = jnp.concatenate([block[:, ROT // 2 :], block[:, : ROT // 2]], axis=1)
        down = jnp.concatenate([block[:, -ROT // 2 :], block[:, : -ROT // 2]], axis=1)
        turned = block * cos_ref[...] + up * low_ref[...] + down * high_ref[...]
        turned = turned.astype(BF16).astype(F32)
        firsts = [h * 3 * HD for h in range(period_heads)]
        asked = [turned[:group, first : first + HD] for first in firsts]
        keys = [turned[:, first + HD : first + 2 * HD] for first in firsts]
        queries += asked
        values += [turned[:group, first + 2 * HD : first + 3 * HD] for first in firsts]
        products = []
        for query, key in zip(asked, keys):
            held_product = key[group:].reshape(group, -1, HD) * query[:, None, :]
            held_product = held_product.reshape(rows - group, HD)
            products.append(jnp.concatenate([key[:group] * query, held_product], axis=0))
        sums = [jnp.sum(product, axis=1, keepdims=True) for product in products]
        for h in range(period_heads):
            score = jnp.where(head_at == j * period_heads + h, sums[h], score)
    score = score * SCALE
    sel = sel_ref[...]
    asked = dot(sel, jnp.concatenate(queries, axis=1).astype(BF16))
    own_ref[:, :head_lanes] = jnp.concatenate(values, axis=1).astype(BF16)

    held_score = score[group:]
    held_count = held_score.shape[0]
    row_id = jnp.bitwise_and(iota((held_count, wide), 0), NREC - 1)
    lane_id = jnp.bitwise_and(iota((held_count, wide), 1), NREC - 1)
    held_score = jnp.where(row_id == lane_id, held_score, 0.0)
    per_request = held_count // group
    spread_ids = jnp.right_shift(iota((group, held_count), 1), per_request.bit_length() - 1)
    spread_rows = jnp.where(spread_ids == iota((group, held_count), 0), 1.0, 0.0).astype(BF16)
    sel_rows = dot(sel, spread_rows).astype(BF16)
    both = jnp.concatenate(parts_of(held_score, 2), axis=1)
    given = dot(sel_rows, both)
    both = jnp.concatenate([asked, given], axis=1).astype(BF16)
    lanes = both.shape[1]
    n_dev = send_ref.shape[0]
    tails = wire_tail(both[2 * n_dev :], lanes)
    for d in range(n_dev):
        send_ref[d, :, :lanes] = both[2 * d : 2 * d + 2]
        send_ref[d, :, lanes:] = tails[2 * d : 2 * d + 2]

    own_score = score[:group]
    lane = iota((group, extra), 1)
    own = jnp.zeros((group, extra), F32)
    for i, part in enumerate(parts_of(own_score, 3)):
        part = part.astype(F32)
        for h in range(heads):
            own = jnp.where(lane == i * heads + h, part[:, h * NREC : h * NREC + 1], own)
    own_ref[:, head_lanes : head_lanes + extra] = own.astype(BF16)


def fold_kernel(weight_ref, page_ref, fold_ref):
    parts = jnp.concatenate(parts_of(weight_ref[...], 3), axis=0)
    rows = weight_ref.shape[0]
    sums = dot(parts, page_ref[...])
    folded = sums[:rows] + sums[rows : 2 * rows] + sums[2 * rows :]
    fold_ref[...] = folded.astype(BF16)


def place_kernel(dims, pick_ref, got_ref, out_ref, rows_ref):
    width, first_lane = dims
    n_dev = got_ref.shape[0]
    for d in range(n_dev):
        rows_ref[2 * d : 2 * d + 2, :] = got_ref[d, :, first_lane:width].astype(F32)
        rows_ref[2 * n_dev + d : 2 * n_dev + d + 1, :] = third_row(got_ref, (d,), width, first_lane, width)
    found = dot(pick_ref[...], rows_ref[...].astype(BF16)).astype(BF16)
    group = out_ref.shape[1]
    for j in range(out_ref.shape[0]):
        out_ref[j] = found[j * group : (j + 1) * group]


def attend_kernel(dims, ask_ref, valid_ref, place_ref, page_ref, fold_ref, *refs):
    send_ref = refs[-1]
    n_pages, slots, dests, heads = dims
    rows = n_pages * slots
    head_lanes = heads * HD
    extra = 2 * heads * NREC
    tokens = page_ref.shape[0]
    width = head_lanes + extra
    asks = []
    for b in range(dests):
        pairs = [ask_ref[g, b, :, :width].astype(F32) for g in range(n_pages)]
        thirds = [third_row(ask_ref, (g, b), width, 0, width) for g in range(n_pages)]
        asks.append(jnp.concatenate([*pairs, *thirds, jnp.zeros((rows - 3 * n_pages, width), F32)], axis=0))
    query = jnp.concatenate([a[:, :head_lanes] for a in asks], axis=1)
    given = jnp.concatenate([a[:, head_lanes : head_lanes + extra] for a in asks], axis=1)
    valid = valid_ref[...] > 0.5
    place = place_ref[...]
    touched = jnp.sum(place[:, :NREC].astype(F32), axis=1, keepdims=True) > 0.5
    lanes = OCTET * rows
    shift = rows.bit_length() - 1
    lane_head = jnp.right_shift(iota((HD, lanes), 1), shift)
    blank = jnp.zeros((HD, lanes), F32)
    lane = iota((lanes, lanes), 1)
    lane_in = jnp.bitwise_and(lane, extra - 1)
    lane_dest = jnp.right_shift(lane, extra.bit_length() - 1) * heads
    given_head = jnp.right_shift(jnp.bitwise_and(lane_in, heads * NREC - 1), 3) + lane_dest
    row_head = jnp.right_shift(iota((lanes, lanes), 0), shift)
    own_lane = jnp.bitwise_and(iota((rows, lanes), 1), rows - 1) == iota((rows, lanes), 0)
    goals = []
    for i in range(3):
        hit = (lane_in >= i * heads) & (lane_in < (i + 1) * heads)
        hit = hit & (row_head == lane_dest + lane_in - i * heads)
        goals.append(jnp.where(hit, 1.0, 0.0).astype(BF16))
    octets = range(STEP_HEADS // OCTET)
    all_scores = []
    for o in octets:
        heads_here = range(o * OCTET, (o + 1) * OCTET)
        asked = jnp.concatenate([query[:, h * HD : (h + 1) * HD] for h in heads_here], axis=0)
        asked = jnp.concatenate([asked, jnp.zeros((lanes, 128 - HD), F32)], axis=1).T[:HD]
        stacked = []
        for h in range(OCTET):
            stacked += [jnp.where(lane_head == h, asked, 0.0), blank]
        stacked = jnp.concatenate(stacked, axis=0).astype(BF16)
        told = jnp.concatenate([given[:, o * lanes : (o + 1) * lanes]] * OCTET, axis=0)
        told = jnp.where(given_head == row_head, told, 0.0).T.astype(BF16)
        some = slice(o * OCTET * 2 * HD, (o + 1) * OCTET * 2 * HD)
        page = jnp.concatenate([page_ref[:, some], fold_ref[:, some]], axis=0)
        all_scores.append(jnp.where(touched, dot(place, told), dot(page, stacked) * SCALE))
    all_weights, extras = [], []
    for scores in all_scores:
        scores = jnp.where(valid, scores, NEVER)
        top = jnp.max(scores, axis=0, keepdims=True)
        weights = jnp.where(valid, jnp.exp(scores - top), 0.0)
        total = jnp.sum(weights, axis=0, keepdims=True)
        safe = jnp.where(total > 0.0, total, 1.0)
        rest = jnp.zeros((256 - weights.shape[0], lanes), F32)
        all_weights.append(jnp.concatenate([weights * (1.0 / safe), rest], axis=0).T.astype(BF16))
        lse = jnp.where(own_lane, jnp.where(total > 0.0, top + jnp.log(safe), NEVER), 0.0)
        spread = jnp.zeros((rows, lanes), F32)
        for part, goal in zip(parts_of(lse, 3), goals):
            spread = spread + dot(part, goal)
        extras.append(spread)
    gathered = []
    for o in octets:
        for i in range(OCTET // QUAD):
            first = (o * OCTET + i * QUAD) * 2 * HD
            some = slice(first, first + QUAD * 2 * HD)
            page = [page_ref[:, some], fold_ref[:, some]]
            page.append(jnp.zeros((256 - tokens - rows, QUAD * 2 * HD), BF16))
            mixed = dot(all_weights[o][i * QUAD * rows : (i + 1) * QUAD * rows], jnp.concatenate(page, axis=0))
            for h in range(QUAD):
                gathered.append(mixed[h * rows : (h + 1) * rows, 2 * HD * h + HD : 2 * HD * (h + 1)])
    gathered = jnp.concatenate(gathered, axis=1)
    extras = jnp.concatenate(extras, axis=1)
    fold_lanes = 2 * head_lanes
    all_lanes = width + fold_lanes
    for b in range(dests):
        whole = jnp.concatenate(
            [
                gathered[:, b * head_lanes : (b + 1) * head_lanes].astype(BF16),
                extras[:, b * extra : (b + 1) * extra].astype(BF16),
                fold_ref[:, b * fold_lanes : (b + 1) * fold_lanes],
            ],
            axis=1,
        )
        tails = wire_tail(whole[2 * n_pages : 3 * n_pages], all_lanes)
        for g in range(n_pages):
            send_ref[g, b, :, :all_lanes] = whole[2 * g : 2 * g + 2]
            send_ref[g, b, :, all_lanes:] = tails[2 * g : 2 * g + 2]


def merge_kernel(
    dims, got_ref, own_ref, sel_ref, back_ref, *refs
):
    group, n_dev, heads, n_pages = dims
    share_refs, dense_hbm, refs = refs[:n_pages], refs[n_pages], refs[n_pages + 1 :]
    head_lanes = heads * HD
    extra = 2 * heads * NREC
    n_blk = n_dev // n_pages
    out_ref, dense_buf, rows_ref, sems = refs
    chunk = D // n_blk
    steps, _, cols = dense_buf.shape

    def dense_copy(step):
        return pltpu.make_async_copy(
            dense_hbm.at[:, pl.ds(step * cols, cols)], dense_buf.at[step], sems.at[step]
        )

    flight = min(5, steps)
    for step in range(flight):
        dense_copy(step).start()
    for d in range(n_dev):
        rows_ref[2 * d : 2 * d + 2, :] = got_ref[d, :, : head_lanes + extra].astype(F32)
        rows_ref[2 * n_dev + d : 2 * n_dev + d + 1, :] = third_row(
            got_ref, (d,), 3 * head_lanes + extra, 0, head_lanes + extra
        )
    rows_ref[3 * n_dev :, :] = own_ref[...].astype(F32)
    count = rows_ref.shape[0]
    parts = rows_ref[:, head_lanes : head_lanes + extra].astype(BF16)
    to, source = iota((extra, 128), 1), iota((extra, 128), 0)
    hit = None
    for i in range(3):
        one = (to < heads) & (source == to + i * heads)
        hit = one if hit is None else hit | one
    lse = dot(parts, jnp.where(hit, 1.0, 0.0).astype(BF16))
    tops = jnp.zeros((count, 128), F32)
    for r in range(group):
        mine = sel_ref[:, r : r + 1] > 0.5
        top = jnp.max(jnp.where(mine, lse, -3e38), axis=0, keepdims=True)
        tops = jnp.where(mine, top, tops)
    weights = jnp.exp(jnp.minimum(lse - tops, 0.0))
    back = back_ref[...]
    totals = jnp.zeros((group, 128), F32)
    for part in parts_of(weights, 3):
        totals = totals + dot(back, part)
    lanes, heads_of = iota((128, head_lanes), 1), iota((128, head_lanes), 0)
    over = lanes - heads_of * HD
    spread = jnp.where((over >= 0) & (over < HD), 1.0, 0.0).astype(BF16)
    weighted = split_dot(weights, spread, 2) * rows_ref[:, :head_lanes]
    inverse = split_dot(1.0 / totals, spread, 3)
    mixed = jnp.zeros((group, head_lanes), F32)
    for part in parts_of(weighted, 2):
        mixed = mixed + dot(back, part)
    attended = (mixed * inverse).astype(BF16)
    for step in range(steps):
        dense_copy(step).wait()
        if step + flight < steps:
            dense_copy(step + flight).start()
        some = slice(step * cols, (step + 1) * cols)
        result = dot(attended, dense_buf[step])
        for share_ref in share_refs:
            result = result + share_ref[:, some].astype(F32)
        for i in range(cols // chunk):
            out_ref[step * (cols // chunk) + i] = result[:, i * chunk : (i + 1) * chunk].astype(BF16)


def mlp_kernel(dims, *refs):
    group, n_pages, n_blk = dims
    leaf_refs, refs = refs[:n_pages], refs[n_pages:]
    in_hbm, out_hbm, _, *refs = refs
    part_refs, (in_buf, out_buf, sems_in, sems_out) = refs[:n_pages], refs[n_pages:]
    chunk = D // n_blk
    n_steps, cols = out_buf.shape[0], out_buf.shape[2]
    core = jnp.bitwise_and(lax.axis_index("blk"), 1)

    def in_copy(step):
        return pltpu.make_async_copy(
            in_hbm.at[pl.ds(step * chunk, chunk), :], in_buf.at[step], sems_in.at[step]
        )

    def out_copy(step):
        return pltpu.make_async_copy(
            out_hbm.at[:, pl.ds(step * cols, cols)], out_buf.at[step], sems_out.at[step]
        )

    copies = [in_copy(step) for step in range(n_blk)] + [out_copy(step) for step in range(n_steps)]
    flight = 6
    for copy in copies[:flight]:
        copy.start()

    def arrived(step):
        copies[step].wait()
        if step + flight < len(copies):
            copies[step + flight].start()

    leaves = [ref[...].astype(F32) for ref in leaf_refs]
    half = n_blk // 2
    hidden = jnp.zeros((n_pages * group, in_buf.shape[2]), F32)
    for z in range(half):
        arrived(2 * z)
        arrived(2 * z + 1)
        for i, c in ((z, 2 * z + core), (half + z, 2 * z + 1 - core)):
            rows = [leaf[i * group : (i + 1) * group] for leaf in leaves]
            hidden = hidden + dot(jnp.concatenate(rows, axis=0).astype(BF16), in_buf[c])
    active = (0.5 * hidden * (1.0 + lax.erf(hidden * math.sqrt(0.5)))).astype(BF16)
    for step in range(n_steps):
        arrived(n_blk + step)
        result = dot(active, out_buf[step]).astype(BF16)
        for g in range(n_pages):
            part_refs[g][:, step * cols : (step + 1) * cols] = result[g * group : (g + 1) * group]


VMEM = pl.BlockSpec(memory_space=pltpu.VMEM)
HBM = pl.BlockSpec(memory_space=pltpu.HBM)
ANY = pl.BlockSpec(memory_space=pl.ANY)


def shape_of(shape, kind=BF16):
    return jax.ShapeDtypeStruct(shape, kind)


def params_of(mib):
    return pltpu.CompilerParams(vmem_limit_bytes=mib * MIB)


def cost_of(flops, nbytes):
    return pl.CostEstimate(flops=int(flops), bytes_accessed=int(nbytes), transcendentals=0)


def on_device(
    new_hidden,
    attn_gain,
    mlp_gain,
    qkv_weight,
    dense_weight,
    in_weight,
    out_weight,
    page_store,
    held_states,
    fold_weights,
    page_table,
    lengths,
    keep_slots,
    fold_index,
    recompute_list,
):
    n_pages = lax.axis_size("pages")
    n_blk = lax.axis_size("blk")
    n_dev = n_pages * n_blk
    mine = lax.axis_index("pages")
    device = lax.axis_index(("pages", "blk"))
    group = lengths.shape[0]
    pages_dev = page_store.shape[0]
    slots = -(-(pages_dev // n_pages) // 4) * 4
    ranks = n_pages * slots
    heads = H // n_blk
    head_lanes = heads * HD
    extra = 2 * heads * NREC
    lanes = head_lanes + extra
    chunk = D // n_blk
    held_rows = held_states.shape[0] * NREC
    kept_count = KP * PAGE

    def swapped(array, axis, size, by):
        return lax.ppermute(array, axis, [(i, i ^ by) for i in range(size)])

    def swapped(array, axis, size, by):
        return lax.ppermute(array, axis, [(i, i ^ by) for i in range(size)])

    def fixed(array):
        return pltpu.with_memory_space_constraint(array, pltpu.HBM)

    half = n_blk // 2
    pack = pl.pallas_call(
        pack_kernel,
        in_specs=[VMEM] * 3,
        out_specs=VMEM,
        out_shape=shape_of((half, n_blk * held_rows + group, chunk)),
        compiler_params=params_of(16),
        name="pack",
    )(fixed(held_states.reshape(held_rows, D)), fixed(new_hidden), fixed(attn_gain[None]))
    pack = lax.all_to_all(
        pack,
        "blk",
        0,
        0,
        axis_index_groups=[list(range(core, n_blk, 2)) for core in range(2)],
        tiled=True,
    )

    n_rows = n_dev * 3
    rows = group * (1 + NREC)
    period = 12 * HD if (3 * head_lanes) % (12 * HD) == 0 else 3 * head_lanes
    lane = np.arange(HD)
    frequency = np.where(lane < ROT, ROT_BASE ** (-2.0 * (lane % (ROT // 2)) / ROT), 0.0).astype(np.float32)
    gains, cosine, low, high, sel, sel_all, back, pick, numbers = pl.pallas_call(
        functools.partial(prep_kernel, (n_pages, pages_dev, period // (3 * HD))),
        in_specs=[pl.BlockSpec(memory_space=pltpu.SMEM)] + [VMEM] * 8,
        out_specs=[VMEM] * 9,
        out_shape=[
            shape_of((2, D), F32),
            *[shape_of((rows, period), F32)] * 3,
            shape_of((n_rows, group)),
            shape_of((n_rows + group, group), F32),
            shape_of((group, n_rows + group)),
            shape_of((PPR * group, n_rows)),
            shape_of((group, 1 + KP + PPR + NREC), jnp.int32),
        ],
        compiler_params=params_of(16),
        cost_estimate=cost_of(0, 0),
        name="prep",
    )(
        page_table.T,
        fixed(page_table.T),
        fixed(lengths[None]),
        fixed(keep_slots),
        fixed(fold_index),
        fixed(recompute_list),
        fixed(jnp.asarray(frequency[None])),
        fixed(attn_gain[None]),
        fixed(mlp_gain[None]),
    )

    numbers = [numbers] + [swapped(numbers, "pages", n_pages, i) for i in range(1, n_pages)]

    tokens = pages_dev * PAGE
    pages = page_store.reshape(tokens, 2 * D)
    steps = H // STEP_HEADS
    step_lanes = STEP_HEADS * 2 * HD
    dests = STEP_HEADS // heads
    fold_width = 2 * head_lanes

    pack, cosine, *numbers = lax.optimization_barrier((pack, cosine, *numbers))
    packs = [pack, swapped(pack, "blk", n_blk, 1)]

    wire = lanes + wire_split(lanes)
    send, own, leaf = pl.pallas_call(
        functools.partial(project_kernel, (group, n_blk, held_rows, heads)),
        in_specs=[VMEM] * 3 + [HBM] + [VMEM] * 4,
        out_specs=[VMEM] * 3,
        out_shape=[
            shape_of((n_dev, 2, wire)),
            shape_of((group, lanes)),
            shape_of((n_blk * group, chunk)),
        ],
        scratch_shapes=[
            pltpu.VMEM((3 * head_lanes // period, n_blk, chunk, period), BF16),
            pltpu.VMEM((n_blk, rows, chunk), F32),
            pltpu.VMEM((rows, period), F32),
            pltpu.SemaphoreType.DMA((3 * head_lanes // period, n_blk)),
        ],
        compiler_params=params_of(50),
        cost_estimate=cost_of(2 * rows * D * 3 * head_lanes, 6 * D * head_lanes),
        name="project",
    )(
        *packs,
        gains,
        fixed(qkv_weight),
        cosine,
        low,
        high,
        sel,
    )
    send, *numbers = lax.optimization_barrier((send, *numbers))
    asked = lax.all_to_all(send, ("pages", "blk"), 0, 0, tiled=True)
    fold_rows, valid, renew = pl.pallas_call(
        functools.partial(facts_kernel, (n_pages, pages_dev, slots)),
        in_specs=[VMEM] * (n_pages + 2),
        out_specs=[VMEM] * 3,
        out_shape=[
            shape_of((ranks, tokens), F32),
            shape_of((tokens + ranks, OCTET * ranks), F32),
            shape_of((tokens + ranks, 2 * OCTET * NREC)),
        ],
        compiler_params=params_of(16),
        cost_estimate=cost_of(0, 0),
        name="facts",
    )(*numbers, fixed(page_table.T), fixed(fold_weights))

    leaf, fold_rows = lax.optimization_barrier((leaf, fold_rows))
    leaves = [leaf] + [swapped(leaf, "pages", n_pages, i) for i in range(1, n_pages)]

    folded_rows = pl.pallas_call(
        fold_kernel,
        grid=(steps,),
        in_specs=[
            pl.BlockSpec((ranks, tokens), lambda i: (0, 0)),
            pl.BlockSpec((tokens, step_lanes), lambda i: (0, i)),
        ],
        out_specs=pl.BlockSpec((ranks, step_lanes), lambda i: (0, i)),
        out_shape=shape_of((ranks, 2 * D)),
        compiler_params=params_of(16),
        cost_estimate=cost_of(0, 0),
        name="fold",
    )(fold_rows, fixed(pages))

    all_lanes = lanes + fold_width
    all_wire = all_lanes + wire_split(all_lanes)
    partial = pl.pallas_call(
        functools.partial(attend_kernel, (n_pages, slots, dests, heads)),
        grid=(steps,),
        in_specs=[
            pl.BlockSpec((n_pages, dests, 2, wire), lambda i: (0, i, 0, 0)),
            pl.BlockSpec((tokens + ranks, OCTET * ranks), lambda i: (0, 0)),
            pl.BlockSpec((tokens + ranks, 2 * OCTET * NREC), lambda i: (0, 0)),
            pl.BlockSpec((tokens, step_lanes), lambda i: (0, i)),
            pl.BlockSpec((ranks, step_lanes), lambda i: (0, i)),
        ],
        out_specs=pl.BlockSpec((n_pages, dests, 2, all_wire), lambda i: (0, i, 0, 0)),
        out_shape=shape_of((n_pages, n_blk, 2, all_wire)),
        compiler_params=params_of(16),
        cost_estimate=cost_of(2 * 128 * tokens * 2 * D, tokens * 4 * D),
        name="attend",
    )(asked.reshape(n_pages, n_blk, 2, wire), valid, renew, fixed(pages), folded_rows)
    partial, *leaves = lax.optimization_barrier((partial, *leaves))
    got = lax.all_to_all(partial.reshape(n_dev, 2, all_wire), ("pages", "blk"), 0, 0, tiled=True)

    hidden = in_weight.shape[1]
    mlp_parts = pl.pallas_call(
        functools.partial(mlp_kernel, (group, n_pages, n_blk)),
        in_specs=[VMEM] * n_pages + [HBM, HBM, ANY],
        out_specs=[VMEM] * n_pages,
        out_shape=[shape_of((group, D))] * n_pages,
        scratch_shapes=[
            pltpu.VMEM((n_blk, chunk, hidden), BF16),
            pltpu.VMEM((8, hidden, D // 8), BF16),
            pltpu.SemaphoreType.DMA((n_blk,)),
            pltpu.SemaphoreType.DMA((8,)),
        ],
        compiler_params=params_of(24),
        cost_estimate=cost_of(4 * n_pages * group * D * hidden, 4 * D * hidden),
        name="mlp",
    )(*leaves, fixed(in_weight), fixed(out_weight), partial)
    mlp_share = [mlp_parts[0]] + [swapped(mlp_parts[i], "pages", n_pages, i) for i in range(1, n_pages)]

    out_part = pl.pallas_call(
        functools.partial(merge_kernel, (group, n_dev, heads, n_pages)),
        in_specs=[VMEM] * (n_pages + 4) + [HBM],
        out_specs=VMEM,
        out_shape=shape_of((n_blk, group, chunk)),
        scratch_shapes=[
            pltpu.VMEM((8, head_lanes, D // 8), BF16),
            pltpu.VMEM((n_rows + group, lanes), F32),
            pltpu.SemaphoreType.DMA((8,)),
        ],
        compiler_params=params_of(24),
        cost_estimate=cost_of(2 * group * D * head_lanes, 2 * D * head_lanes),
        name="merge",
    )(
        got,
        own,
        sel_all,
        back,
        *mlp_share,
        fixed(dense_weight),
    )
    out_got = lax.all_to_all(out_part, "blk", 0, 0, tiled=True)
    summed = jnp.sum(out_got.astype(F32), axis=0).astype(BF16)

    folded = pl.pallas_call(
        functools.partial(place_kernel, (all_lanes, lanes)),
        in_specs=[VMEM, VMEM],
        out_specs=VMEM,
        out_shape=shape_of((PPR, group, fold_width)),
        scratch_shapes=[pltpu.VMEM((n_rows, fold_width), F32)],
        compiler_params=params_of(16),
        cost_estimate=cost_of(0, 4 * n_rows * fold_width),
        name="place",
    )(pick, got)
    folded = jnp.transpose(folded, (1, 0, 2))
    return (summed, folded)


def solution(mesh):
    in_specs = (
        P("pages", "blk"),
        P(),
        P(),
        P(None, "blk"),
        P("blk", None),
        P(None, ("pages", "blk")),
        P(("pages", "blk"), None),
        P(("pages", "blk"), None, None),
        P(("pages", "blk"), None, None),
        P(),
        P(),
        P("pages"),
        P("pages", None),
        P("pages", None),
        P("pages", None),
    )
    out_specs = (P("pages", "blk"), P("pages", None, "blk"))
    return jax.shard_map(
        on_device, mesh=mesh, in_specs=in_specs, out_specs=out_specs, check_vma=False
    )
```
